32 devices in a mesh: outer: 4 (over z), inner: 8 (over y, x, core).
Axes of the slice: x: 2, y: 2, z: 4, core: 2. Of those that a mesh axis runs over, the one named last changes fastest.
Arguments:
- queries: bfloat16 [32768, 1024], P(('outer', 'inner')), may hold values from -6 to 6
- keys: bfloat16 [32768, 1024], P(('outer', 'inner')), may hold values from -0.5 to 0.5
- values: bfloat16 [32768, 1024], P(('outer', 'inner')), may hold values from -6 to 6
- level_weights: float32 [16, 8, 32768], P(None, None, ('outer', 'inner')), as said below
- out_weight: bfloat16 [1024, 1024], replicated, may hold values from -0.046875 to 0.046875
Outputs:
- mixed: bfloat16 [32768, 1024], P(('outer', 'inner'))
The draws below stay inside these ranges and needn't reach their ends.
Inputs may be any that keep to these rules, and one draw needn't show every extreme that they name: `level_weights`: every entry is positive.
All inputs are finite; a program needn't handle non-finite values.
Results may differ from the reference program's by a relative error of at most 0.0057.
Values sent between devices are 32-bit elements; how exact they have to be, the bound alone decides.
No kernel may reach another device: no remote copies, remote signals or barrier semaphores. Data moves between devices by JAX's collectives and lax.ppermute only.
A program may use at most 128 MiB of HBM per device.

```python
import jax
import jax.numpy as jnp
from jax import lax

HEADS = 8
HEAD = 128
D = 1024
TOK_DEV = 1024
TOKENS = 32768
LOCAL_BITS = 10
INNER_BITS = 3
OUTER_BITS = 2
LEVELS = 16
N_OUTER = 4
N_INNER = 8


def draw_level_weights(key, part):
    level_index = jnp.arange(LEVELS).astype(jnp.float32)
    level_scale = 2.0 ** (-jnp.maximum(level_index - 1.0, 0.0) / 2.0)
    shape = (LEVELS, HEADS, TOKENS)
    factor = jnp.exp(jax.random.uniform(key, shape, jnp.float32, jnp.log(0.5), jnp.log(2.0)))
    return (factor * level_scale[:, None, None]).astype(jnp.float32)


def shard_levels(stream_key, extent, split, least, largest):
    def one(dim, shards_of):
        draws = jax.random.uniform(jax.random.fold_in(jax.random.fold_in(stream_key, 6), dim), (shards_of,), jnp.float32, least / len(split), largest / len(split))
        return jnp.repeat(jnp.exp(draws), extent[dim] // shards_of).reshape((-1,) + (1,) * (len(extent) - dim - 1))

    loudness = one(*split[0])
    for cut in split[1:]:
        loudness = loudness * one(*cut)
    return loudness


def gaussian(stream_key, shape, spread, bound, cuts=(), kind=jnp.bfloat16):
    entries = jax.random.normal(stream_key, shape, jnp.float32) * spread
    if len(cuts) > 0:
        entries = shard_levels(stream_key, shape, cuts, -0.22, 0.18) * entries
    return jnp.clip(entries, min=-bound, max=bound).astype(kind)


def setup_inputs(seed: int = 0) -> dict:
    seeds = jax.random.split(jax.random.key(seed), 6)
    return {
        "queries": gaussian(seeds[0], (TOKENS, D), 1.0, 6.0, ((0, 32),)),
        "keys": gaussian(seeds[1], (TOKENS, D), 0.088, 0.5, ((0, 32),)),
        "values": gaussian(seeds[2], (TOKENS, D), 1.0, 6.0, ((0, 32),)),
        "level_weights": draw_level_weights(jax.random.fold_in(seeds[5], 71), 0),
        "out_weight": gaussian(seeds[4], (D, D), (16 * D) ** -0.5, 0.046875),
    }


def level_onehot(row_count, local_bits):
    target = lax.iota(jnp.int32, row_count)[:, None]
    source = lax.iota(jnp.int32, row_count)[None, :]
    differ = jnp.bitwise_xor(target, source)
    level = jnp.zeros((row_count, row_count), jnp.int32)
    for shift in range(local_bits):
        level = level + (jnp.right_shift(differ, shift) > 0).astype(jnp.int32)
    picks = lax.iota(jnp.int32, local_bits + 1)[:, None, None]
    return jnp.logical_and(level[None] == picks, (source <= target)[None]).astype(jnp.float32)


def reference(queries, keys, values, level_weights, out_weight):
    block_count = N_OUTER * N_INNER
    dev_bits = INNER_BITS + OUTER_BITS
    query_blocks = queries.reshape(block_count, TOK_DEV, HEADS, HEAD)
    key_blocks = keys.reshape(block_count, TOK_DEV, HEADS, HEAD)
    value_blocks = values.reshape(block_count, TOK_DEV, HEADS, HEAD)
    lam_blocks = jnp.transpose(level_weights.reshape(LEVELS, HEADS, block_count, TOK_DEV), (2, 0, 1, 3))

    def state_of(pair):
        return jnp.einsum("the,thf->hef", pair[0].astype(jnp.float32), pair[1].astype(jnp.float32),
                          precision=lax.Precision.HIGHEST)

    states = lax.map(state_of, (key_blocks, value_blocks))
    groups = [states]
    running = states
    for level_bit in range(dev_bits - 1):
        running = running[0::2] + running[1::2]
        groups.append(running)
    onehot = level_onehot(TOK_DEV, LOCAL_BITS)

    def one_block(block_index):
        query_here = query_blocks[block_index].astype(jnp.float32)
        key_here = key_blocks[block_index].astype(jnp.float32)
        value_here = value_blocks[block_index].astype(jnp.float32)
        lam_here = lam_blocks[block_index]
        mixing = jnp.einsum("lts,lht->hts", onehot, lam_here[:LOCAL_BITS + 1], precision=lax.Precision.HIGHEST)
        scores = jnp.einsum("the,she->hts", query_here, key_here, precision=lax.Precision.HIGHEST)
        weighted = (scores * mixing).astype(jnp.bfloat16).astype(jnp.float32)
        local_part = jnp.einsum("hts,she->the", weighted, value_here, precision=lax.Precision.HIGHEST)
        buckets = []
        for level_bit in range(dev_bits):
            position = jnp.right_shift(block_index, level_bit)
            upper_half = jnp.bitwise_and(position, 1) == 1
            lower_state = lax.dynamic_index_in_dim(groups[level_bit], jnp.bitwise_xor(position, 1), 0, keepdims=False)
            buckets.append(jnp.where(upper_half, lower_state, jnp.zeros_like(lower_state)))
        stacked = jnp.stack(buckets).astype(jnp.bfloat16).astype(jnp.float32)
        products = jnp.einsum("the,lhef->lthf", query_here, stacked, precision=lax.Precision.HIGHEST)
        remote_lam = jnp.transpose(lam_here[LOCAL_BITS + 1:], (0, 2, 1))[:, :, :, None]
        remote_part = jnp.sum(products * remote_lam, axis=0)
        attended = (local_part + remote_part).astype(jnp.bfloat16).reshape(TOK_DEV, HEADS * HEAD)
        return jnp.dot(attended, out_weight, preferred_element_type=jnp.float32).astype(jnp.bfloat16)

    outputs = lax.map(one_block, jnp.arange(block_count, dtype=jnp.int32))
    return outputs.reshape(TOKENS, HEADS * HEAD)
```

```python
import functools

import jax
import jax.numpy as jnp
from jax import lax
from jax.experimental import pallas as pl
from jax.experimental.pallas import tpu as pltpu
from jax.sharding import PartitionSpec as P

HEADS = 8
HEAD = 128
LOCAL_BITS = 10
CHUNK = 128
F32 = jnp.float32
BF16 = jnp.bfloat16
MIB = 1 << 20


def bits_of(count):
    return count.bit_length() - 1


def swap(block, axis, stride):
    count = lax.axis_size(axis)
    return lax.ppermute(block, axis, [(place, place ^ stride) for place in range(count)])


def raise_to(block, axis, stride):
    count = lax.axis_size(axis)
    route = [(place, place | stride) for place in range(count) if not place & stride]
    return lax.ppermute(block, axis, route)


def cost(flops, moved):
    return pl.CostEstimate(flops=flops, bytes_accessed=moved, transcendentals=0)


def product_tn(left, right):
    return lax.dot_general(left, right, (((0,), (0,)), ((), ())), preferred_element_type=F32)


def product_nt(left, right):
    return lax.dot_general(left, right, (((1,), (1,)), ((), ())), preferred_element_type=F32)


def state_kernel(keys, values, state):
    for low in range(0, keys.shape[1], HEAD):
        part = slice(low, low + HEAD)
        state[part, :] = product_tn(keys[:, part], values[:, part])


def block_state(keys, values):
    tokens, width = keys.shape
    step = 2 * HEAD
    column = pl.BlockSpec((tokens, step), lambda pair: (0, pair))
    return pl.pallas_call(
        state_kernel,
        grid=(width // step,),
        in_specs=[column, column],
        out_specs=pl.BlockSpec((step, HEAD), lambda pair: (pair, 0)),
        out_shape=jax.ShapeDtypeStruct((width, HEAD), F32),
        cost_estimate=cost(2 * tokens * width * HEAD, 5 * MIB),
    )(keys, values)


def local_kernel(queries, keys, values, weights, local):
    head = pl.program_id(0)
    tokens = queries.shape[0]
    rows = weights[:, pl.ds(head, 1), :].reshape(weights.shape[0], tokens)
    columns = rows.T
    source = lax.broadcasted_iota(jnp.int32, (CHUNK, CHUNK), 0)
    target = lax.broadcasted_iota(jnp.int32, (CHUNK, CHUNK), 1)
    differ = jnp.bitwise_xor(source, target)
    level = jnp.zeros((CHUNK, CHUNK), jnp.int32)
    fine = bits_of(CHUNK)
    for shift in range(fine):
        level = level + (jnp.right_shift(differ, shift) > 0).astype(jnp.int32)
    level = jnp.where(source <= target, level, -1)
    picks = [level == pick for pick in range(fine + 1)]
    nodes = [None] * (bits_of(tokens) - fine)
    for chunk in range(tokens // CHUNK):
        span = slice(chunk * CHUNK, (chunk + 1) * CHUNK)
        query, key, value = queries[span, :], keys[span, :], values[span, :]
        mixing = jnp.zeros((CHUNK, CHUNK), F32)
        for pick in range(fine + 1):
            mixing = jnp.where(picks[pick], rows[pick : pick + 1, span], mixing)
        weighted = (product_nt(key, query) * mixing).astype(BF16)
        total = product_tn(weighted, value)
        used = [bit for bit in range(len(nodes)) if chunk >> bit & 1]
        if used:
            wide = query.astype(F32)
            scaled = [
                (wide * columns[span, fine + 1 + bit : fine + 2 + bit]).astype(BF16) for bit in used
            ]
            states = [nodes[bit].astype(BF16) for bit in used]
            total = total + jnp.dot(
                jnp.concatenate(scaled, axis=1),
                jnp.concatenate(states, axis=0),
                preferred_element_type=F32,
            )
        local[span, :] = total
        if chunk + 1 < tokens // CHUNK:
            carry = product_tn(key, value)
            bit = 0
            while chunk >> bit & 1:
                carry = nodes[bit] + carry
                bit += 1
            nodes[bit] = carry


def local_part(queries, keys, values, level_weights):
    tokens, width = queries.shape
    column = pl.BlockSpec((tokens, HEAD), lambda head: (0, head))
    whole = pl.BlockSpec(level_weights.shape, lambda head: (0, 0, 0))
    return pl.pallas_call(
        local_kernel,
        grid=(width // HEAD,),
        in_specs=[column, column, column, whole],
        out_specs=column,
        out_shape=jax.ShapeDtypeStruct((tokens, width), F32),
        cost_estimate=cost(8 * tokens * width * HEAD, 20 * MIB),
        compiler_params=pltpu.CompilerParams(vmem_limit_bytes=24 * MIB),
    )(queries, keys, values, level_weights)


def near_kernel(inner_bits, place, queries, weights, local, first_mine, first_other, mine, other, near, scaled):
    head = pl.program_id(0)
    tokens = queries.shape[0]
    half_heads = pl.num_programs(0) // 2
    core = jnp.bitwise_and(place[0], 1)
    here = jnp.right_shift(head, bits_of(HEADS) - 1) == core
    first = LOCAL_BITS + 1
    columns = weights[:, pl.ds(head, 1), :].reshape(weights.shape[0], tokens).T
    states = []
    for bit in range(inner_bits):
        got = jnp.bitwise_and(jnp.right_shift(place[0], bit), 1) == 1
        if bit == 0:
            state = jnp.where(here, first_mine[...], first_other[...])
        else:
            state = jnp.where(here, mine[bit - 1], other[bit - 1])
        states.append(jnp.where(got, state, 0.0).astype(BF16))
    products = jnp.dot(queries[...], jnp.concatenate(states, axis=1), preferred_element_type=F32)
    total = local[...]
    for bit in range(inner_bits):
        column = columns[:, first + bit : first + bit + 1]
        total = total + column * products[:, bit * HEAD : (bit + 1) * HEAD]
    near[...] = total
    wide = queries[...].astype(F32)
    for bit in range(scaled.shape[0]):
        level = first + inner_bits + bit
        scaled[bit] = (wide * columns[:, level : level + 1]).astype(BF16)


def near_part(place, inner_bits, outer_bits, queries, level_weights, local, first_mine, first_other, mine, other):
    tokens, width = queries.shape
    half_heads = width // HEAD // 2
    column = pl.BlockSpec((tokens, HEAD), lambda head: (0, head))
    whole = pl.BlockSpec(level_weights.shape, lambda head: (0, 0, 0))
    single = pl.BlockSpec((HEAD, HEAD), lambda head: (lax.rem(head, half_heads), 0))
    several = pl.BlockSpec((inner_bits - 1, HEAD, HEAD), lambda head: (0, lax.rem(head, half_heads), 0))
    return pl.pallas_call(
        functools.partial(near_kernel, inner_bits),
        grid=(width // HEAD,),
        in_specs=[
            pl.BlockSpec(memory_space=pltpu.SMEM), column, whole, column, single, single, several, several,
        ],
        out_specs=[column, pl.BlockSpec((outer_bits, tokens, HEAD), lambda head: (0, 0, head))],
        out_shape=[
            jax.ShapeDtypeStruct((tokens, width), F32),
            jax.ShapeDtypeStruct((outer_bits, tokens, width), BF16),
        ],
        cost_estimate=cost(2 * inner_bits * tokens * width * HEAD, 16 * MIB),
        compiler_params=pltpu.CompilerParams(vmem_limit_bytes=24 * MIB),
    )(place, queries, level_weights, local, first_mine, first_other, mine, other)


def far_kernel(place, scaled, near, mine, other, out_weight, mixed, states, attended):
    chips, outer_bits, piece = mine.shape[0], mine.shape[1], mine.shape[2]

    @pl.when(pl.program_id(0) == 0)
    def _():
        core = jnp.bitwise_and(place[0], 1)
        chip = jnp.right_shift(place[0], 1)
        for half in range(2):
            for owner in range(chips):
                slot = jnp.bitwise_xor(chip, owner)
                low = (half * chips + owner) * piece
                for bit in range(outer_bits):
                    got = jnp.bitwise_and(jnp.right_shift(place[1], bit), 1) == 1
                    state = jnp.where(core == half, mine[slot, bit], other[slot, bit])
                    states[bit, low : low + piece, :] = jnp.where(got, state, 0.0).astype(BF16)

    for low in range(0, near.shape[1], HEAD):
        part = slice(low, low + HEAD)
        query = jnp.concatenate([scaled[bit, :, part] for bit in range(outer_bits)], axis=1)
        state = jnp.concatenate([states[bit, part, :] for bit in range(outer_bits)], axis=0)
        total = near[:, part] + jnp.dot(query, state, preferred_element_type=F32)
        attended[:, part] = total.astype(BF16)
    mixed[...] = jnp.dot(attended[...], out_weight[...], preferred_element_type=F32).astype(BF16)


def far_part(place, scaled, near, mine, other, out_weight):
    tokens, width = near.shape
    outer_bits = scaled.shape[0]
    rows = min(256, tokens)
    band = pl.BlockSpec((rows, width), lambda step: (step, 0))
    fixed4 = pl.BlockSpec(mine.shape, lambda step: (0, 0, 0, 0))
    return pl.pallas_call(
        far_kernel,
        grid=(tokens // rows,),
        in_specs=[
            pl.BlockSpec(memory_space=pltpu.SMEM),
            pl.BlockSpec((outer_bits, rows, width), lambda step: (0, step, 0)),
            band,
            fixed4,
            fixed4,
            pl.BlockSpec(out_weight.shape, lambda step: (0, 0)),
        ],
        out_specs=band,
        out_shape=jax.ShapeDtypeStruct((tokens, width), BF16),
        scratch_shapes=[pltpu.VMEM((outer_bits, width, HEAD), BF16), pltpu.VMEM((rows, width), BF16)],
        cost_estimate=cost(2 * tokens * width * (width + outer_bits * HEAD), 14 * MIB),
        compiler_params=pltpu.CompilerParams(vmem_limit_bytes=24 * MIB),
    )(place, scaled, near, mine, other, out_weight)


def body(queries, keys, values, level_weights, out_weight):
    inner, outer = lax.axis_size("inner"), lax.axis_size("outer")
    inner_bits, outer_bits = bits_of(inner), bits_of(outer)
    inner_place, outer_place = lax.axis_index("inner"), lax.axis_index("outer")
    place = jnp.stack([inner_place, outer_place]).astype(jnp.int32)
    core, chip = jnp.bitwise_and(inner_place, 1), jnp.right_shift(inner_place, 1)
    chips = inner // 2

    state = block_state(keys, values)
    half = state.shape[0] // 2
    piece = half // chips
    keep = lax.dynamic_slice_in_dim(state, core * half, half, 0)
    give = lax.dynamic_slice_in_dim(state, (1 - core) * half, half, 0)
    first_mine = swap(give, "inner", 1)
    first_other = raise_to(keep, "inner", 1)
    running = keep + first_mine
    buckets = []
    for bit in range(1, inner_bits):
        arrived = swap(running, "inner", 1 << bit)
        buckets.append(arrived)
        running = running + arrived
    mine = jnp.stack(buckets)
    other = swap(mine, "inner", 1)

    running = lax.dynamic_slice_in_dim(running, chip * piece, piece, 0)
    far = []
    for bit in range(outer_bits):
        arrived = swap(running, "outer", 1 << bit)
        far.append(arrived)
        running = running + arrived
    far = jnp.stack(far)
    far_mine = jnp.stack([far] + [swap(far, "inner", 2 * step) for step in range(1, chips)])
    far_other = swap(far_mine, "inner", 1)

    local = local_part(queries, keys, values, level_weights)
    near, scaled = near_part(
        place, inner_bits, outer_bits, queries, level_weights, local, first_mine, first_other, mine, other
    )
    return far_part(place, scaled, near, far_mine, far_other, out_weight)


def solution(mesh):
    spread = P(("outer", "inner"), None)
    in_specs = (spread, spread, spread, P(None, None, ("outer", "inner")), P())
    return jax.shard_map(body, mesh=mesh, in_specs=in_specs, out_specs=spread, check_vma=False)
```

```python
import functools

import jax
import jax.numpy as jnp
from jax import lax
from jax.experimental import pallas as pl
from jax.experimental.pallas import tpu as pltpu
from jax.sharding import PartitionSpec as P

HEADS = 8
HEAD = 128
LOCAL_BITS = 10
TILE = 128
CHUNK = 256
F32 = jnp.float32
BF16 = jnp.bfloat16
MIB = 1 << 20


def bits_of(count):
    return count.bit_length() - 1


def swap(block, axis, stride):
    count = lax.axis_size(axis)
    return lax.ppermute(block, axis, [(place, place ^ stride) for place in range(count)])


def raise_to(block, axis, stride):
    count = lax.axis_size(axis)
    route = [(place, place | stride) for place in range(count) if not place & stride]
    return lax.ppermute(block, axis, route)


def cost(flops, moved):
    return pl.CostEstimate(flops=flops, bytes_accessed=moved, transcendentals=0)


def params(limit):
    return pltpu.CompilerParams(vmem_limit_bytes=limit * MIB)


def product(left, right):
    return jnp.dot(left, right, preferred_element_type=F32)


def product_nt(left, right):
    return lax.dot_general(left, right, (((1,), (1,)), ((), ())), preferred_element_type=F32)


def identity(size):
    row = lax.broadcasted_iota(jnp.int32, (size, size), 0)
    column = lax.broadcasted_iota(jnp.int32, (size, size), 1)
    return (row == column).astype(F32).astype(BF16)


def turned(block):
    return product_nt(identity(block.shape[1]), block).astype(BF16)


def state_kernel(half, keys, values, state):
    flipped = turned(values[...])
    for low in range(0, keys.shape[1], HEAD):
        part = slice(low, low + HEAD)
        state[part, :] = product(flipped[part, :], keys[:, part])


def block_state(half, keys, values):
    tokens, width = keys.shape
    step = 2 * HEAD
    steps = width // 2 // step
    column = pl.BlockSpec((tokens, step), lambda pair, half: (0, half[0] * steps + pair))
    return pl.pallas_call(
        state_kernel,
        grid_spec=pltpu.PrefetchScalarGridSpec(
            num_scalar_prefetch=1,
            grid=(steps,),
            in_specs=[column, column],
            out_specs=pl.BlockSpec((step, HEAD), lambda pair, half: (pair, 0)),
        ),
        out_shape=jax.ShapeDtypeStruct((width // 2, HEAD), F32),
        cost_estimate=cost(tokens * width * HEAD, 3 * MIB),
        compiler_params=params(58),
    )(half, keys, values)


def tile_mixing(rows):
    target = lax.broadcasted_iota(jnp.int32, (8, TILE), 1)
    source = lax.broadcasted_iota(jnp.int32, (8, TILE), 0)
    rows = [jnp.broadcast_to(row, (8, TILE)) for row in rows]
    within = jnp.bitwise_and(target, 7)
    differ = jnp.bitwise_xor(within, source)
    base = rows[3]
    for level in (2, 1, 0):
        base = jnp.where(differ < 1 << level, rows[level], base)
    parts = [jnp.where(source <= within, base, 0.0)]
    for bit in range(3, bits_of(TILE)):
        upper = jnp.bitwise_and(jnp.right_shift(target, bit), 1) == 1
        parts = [jnp.where(upper, rows[bit + 1], part) for part in parts] + [
            jnp.where(upper, part, 0.0) for part in parts
        ]
    return jnp.concatenate(parts, axis=0)


def local_kernel(first_head, queries, keys, values, weights, local, rows):
    head = pl.program_id(0) + first_head
    tokens = queries.shape[0]
    flipped = turned(values[...])
    rows[...] = weights[:, pl.ds(head, 1), :].reshape(rows.shape)

    def row(level, low, size):
        return rows[level : level + 1, low : low + size]

    nodes = [None] * bits_of(tokens // CHUNK)
    top = bits_of(CHUNK)
    for chunk in range(tokens // CHUNK):
        low = chunk * CHUNK
        span = slice(low, low + CHUNK)
        query, key = queries[span, :], keys[span, :]
        scores = product_nt(key, query)
        lower, upper = (
            tile_mixing([row(level, start, TILE) for level in range(top)]) for start in (low, low + TILE)
        )
        across = row(top, low + TILE, TILE)
        weighted = jnp.concatenate(
            [
                jnp.concatenate([scores[:TILE, :TILE] * lower, scores[:TILE, TILE:] * across], axis=1),
                jnp.concatenate([jnp.zeros_like(lower), scores[TILE:, TILE:] * upper], axis=1),
            ],
            axis=0,
        ).astype(BF16)
        total = product(flipped[:, span], weighted)
        for bit in range(len(nodes)):
            if chunk >> bit & 1:
                total = total + row(top + 1 + bit, low, CHUNK) * product_nt(nodes[bit].astype(BF16), query)
        local[:, span] = total
        if chunk + 1 < tokens // CHUNK:
            carry = product(flipped[:, span], key)
            bit = 0
            while chunk >> bit & 1:
                carry = nodes[bit] + carry
                bit += 1
            nodes[bit] = carry


def local_part(half, queries, keys, values, level_weights):
    tokens, width = queries.shape
    heads = width // HEAD // 2
    column = pl.BlockSpec((tokens, HEAD), lambda head: (0, half * heads + head))
    return pl.pallas_call(
        functools.partial(local_kernel, half * heads),
        grid=(heads,),
        in_specs=[column, column, column, pl.BlockSpec(level_weights.shape, lambda head: (0, 0, 0))],
        out_specs=pl.BlockSpec((HEAD, tokens), lambda head: (head, 0)),
        out_shape=jax.ShapeDtypeStruct((width // 2, tokens), F32),
        scratch_shapes=[pltpu.VMEM((level_weights.shape[0], tokens), F32)],
        cost_estimate=cost(3 * tokens * width * HEAD, 6 * MIB),
        compiler_params=params(40),
    )(queries, keys, values, level_weights)


def has_bit(place, bit):
    return jnp.bitwise_and(jnp.right_shift(place, bit), 1) == 1


def fill(states, base, half, place, digit_place, first_digit, mine, other):
    chips, count, piece = mine.shape[:3]
    core = jnp.bitwise_and(place, 1)
    chip = jnp.right_shift(place, 1)
    for owner in range(chips):
        slot = jnp.bitwise_xor(chip, owner)
        low = base + owner * piece
        for bit in range(count):
            state = jnp.where(core == half, mine[slot, bit], other[slot, bit])
            state = jnp.where(has_bit(digit_place, first_digit + bit), state, 0.0)
            states[first_digit + bit, low : low + piece, :] = state.astype(BF16)


def near_kernel(half, heads, place, queries, weights, local, first_mine, first_other, mine, other, near, states, rows):
    step = pl.program_id(0)
    bits = states.shape[0]

    @pl.when(step == 0)
    def _():
        inner_place = place[0]
        first = jnp.where(jnp.bitwise_and(inner_place, 1) == half, first_mine[...], first_other[...])
        states[0] = jnp.where(has_bit(inner_place, 0), first, 0.0).astype(BF16)
        fill(states, 0, half, inner_place, inner_place, 1, mine, other)

    low = pl.multiple_of(step * HEAD, HEAD)
    rows[...] = weights[:, pl.ds(step + half * heads, 1), :].reshape(rows.shape)
    total = local[...]
    for bit in range(bits):
        level = LOCAL_BITS + 1 + bit
        row = rows[level : level + 1, :]
        total = total + row * product_nt(states[bit, pl.ds(low, HEAD), :], queries[...])
    near[...] = total


def near_part(half, bits, place, queries, level_weights, local, first_mine, first_other, mine, other):
    tokens, width = queries.shape
    heads = width // HEAD // 2
    column = pl.BlockSpec((tokens, HEAD), lambda head: (0, half * heads + head))
    band = pl.BlockSpec((HEAD, tokens), lambda head: (head, 0))
    fixed = [pl.BlockSpec(part.shape, lambda head, rank=part.ndim: (0,) * rank)
             for part in (first_mine, first_other, mine, other)]
    return pl.pallas_call(
        functools.partial(near_kernel, half, heads),
        grid=(heads,),
        in_specs=[
            pl.BlockSpec(memory_space=pltpu.SMEM),
            column,
            pl.BlockSpec(level_weights.shape, lambda head: (0, 0, 0)),
            band,
            *fixed,
        ],
        out_specs=band,
        out_shape=jax.ShapeDtypeStruct((width // 2, tokens), F32),
        scratch_shapes=[
            pltpu.VMEM((bits, width // 2, HEAD), BF16),
            pltpu.VMEM((level_weights.shape[0], tokens), F32),
        ],
        cost_estimate=cost(bits * tokens * width * HEAD, 8 * MIB),
        compiler_params=params(40),
    )(place, queries, level_weights, local, first_mine, first_other, mine, other)


def far_kernel(bits, first_level, place, queries, weights, lower, upper, *rest):
    arrived, (out_weight, mixed, states, flipped, attended) = rest[: 2 * bits], rest[2 * bits :]
    rows, width = attended.shape

    @pl.when(pl.program_id(0) == 0)
    def _():
        for half in range(2):
            for bit in range(bits):
                fill(states, half * (width // 2), half, place[0], place[1], bit, arrived[2 * bit], arrived[2 * bit + 1])

    for half, near in enumerate((lower, upper)):
        for low in range(0, width // 2, HEAD):
            part = slice(half * (width // 2) + low, half * (width // 2) + low + HEAD)
            head = part.start // HEAD
            total = near[low : low + HEAD, :]
            for bit in range(bits):
                row = weights[first_level + bit, head : head + 1, :]
                total = total + row * product_nt(states[bit, part, :], queries[:, part])
            flipped[part, :] = total.astype(BF16)
    unit = identity(rows)
    for low in range(0, width, CHUNK):
        attended[:, low : low + CHUNK] = product_nt(unit, flipped[low : low + CHUNK, :]).astype(BF16)
    mixed[...] = product(attended[...], out_weight[...]).astype(BF16)


def far_part(first_level, place, queries, level_weights, lower, upper, arrived, out_weight):
    tokens, width = queries.shape
    bits = len(arrived) // 2
    rows = min(CHUNK, tokens)
    band = pl.BlockSpec((rows, width), lambda step: (step, 0))
    near = pl.BlockSpec((width // 2, rows), lambda step: (0, step))
    fixed = pl.BlockSpec(arrived[0].shape, lambda step: (0, 0, 0, 0))
    return pl.pallas_call(
        functools.partial(far_kernel, bits, first_level),
        grid=(tokens // rows,),
        in_specs=[
            pl.BlockSpec(memory_space=pltpu.SMEM),
            band,
            pl.BlockSpec(level_weights.shape[:2] + (rows,), lambda step: (0, 0, step)),
            near,
            near,
            *[fixed] * (2 * bits),
            pl.BlockSpec(out_weight.shape, lambda step: (0, 0)),
        ],
        out_specs=band,
        out_shape=jax.ShapeDtypeStruct((tokens, width), BF16),
        scratch_shapes=[
            pltpu.VMEM((bits, width, HEAD), BF16),
            pltpu.VMEM((width, rows), BF16),
            pltpu.VMEM((rows, width), BF16),
        ],
        cost_estimate=cost(2 * tokens * width * (width + bits * HEAD), 12 * MIB),
        compiler_params=params(24),
    )(place, queries, level_weights, lower, upper, *arrived, out_weight)


def spread(block, chips):
    return [swap(block, "inner", 2 * step) for step in range(1, chips)]


def body(queries, keys, values, level_weights, out_weight):
    inner, outer = lax.axis_size("inner"), lax.axis_size("outer")
    inner_bits, outer_bits = bits_of(inner), bits_of(outer)
    inner_place, outer_place = lax.axis_index("inner"), lax.axis_index("outer")
    place = jnp.stack([inner_place, outer_place]).astype(jnp.int32)
    core, chip = jnp.bitwise_and(inner_place, 1), jnp.right_shift(inner_place, 1)
    chips = inner // 2
    half = keys.shape[1] // 2
    piece = half // chips
    tie = lax.optimization_barrier

    give = block_state((1 - core).reshape(1).astype(jnp.int32), keys, values)
    first_mine = swap(give, "inner", 1)
    keep = block_state(core.reshape(1).astype(jnp.int32), keys, values)

    def piece_of(owner):
        low = owner * piece
        return lax.dynamic_slice_in_dim(keep, low, piece, 0) + lax.dynamic_slice_in_dim(first_mine, low, piece, 0)

    parts = [piece_of(jnp.bitwise_xor(chip, step)) for step in range(chips)]
    inputs = (queries, keys, values, level_weights)
    parts, inputs, keep = tie((parts, inputs, keep))
    first_other = raise_to(keep, "inner", 1)
    sums = [parts[0]] + [swap(parts[step], "inner", 2 * step) for step in range(1, chips)]
    local = [local_part(0, *inputs)]
    sums, first_other, local[0] = tie((sums, first_other, local[0]))
    tree = [sums]
    while len(tree[-1]) > 1:
        tree.append([tree[-1][at] + tree[-1][at + 1] for at in range(0, len(tree[-1]), 2)])

    sent = [
        jnp.stack([tree[bit][(step >> bit) ^ 1] for bit in range(inner_bits - 1)]) for step in range(chips)
    ]
    running = tree[-1][0]
    running, sent, inputs = tie((running, sent, inputs))
    arrived = swap(running, "outer", 1)
    got = [sent[0]] + [swap(sent[step], "inner", 2 * step) for step in range(1, chips)]
    local.append(local_part(1, *inputs))
    arrived, got, local[1] = tie((arrived, got, local[1]))

    def near(part, near_mine, near_other):
        return near_part(
            part, inner_bits, place, queries, level_weights, local[part], first_mine, first_other, near_mine, near_other
        )

    far = [arrived]
    nears = []
    pieces = []
    for bit in range(1, outer_bits):
        running = running + arrived
        arrived = swap(running, "outer", 1 << bit)
        pieces.append([far[-1]] + spread(far[-1], chips))
        if bit == 1:
            near_mine = jnp.stack(got)
            near_other = swap(near_mine, "inner", 1)
            nears.append(near(0, near_mine, near_other))
            arrived, pieces, nears = tie((arrived, pieces, nears))
        far.append(arrived)
    if outer_bits == 1:
        near_mine = jnp.stack(got)
        near_other = swap(near_mine, "inner", 1)
    (far[-1], near_mine, pieces) = tie((far[-1], near_mine, pieces))
    last = spread(far[-1], chips)
    arrivals = []

    def collect(blocks):
        mine = jnp.stack(blocks)[:, None]
        return [mine, swap(mine, "inner", 1)]

    for blocks in pieces:
        arrivals += collect(blocks)
    for part in range(len(nears), 2):
        nears.append(near(part, near_mine, near_other))
    last, nears = tie((last, nears))
    arrivals += collect([far[-1]] + last)
    first_level = LOCAL_BITS + 1 + inner_bits
    return far_part(first_level, place, queries, level_weights, *nears, arrivals, out_weight)


def solution(mesh):
    spec = P(("outer", "inner"), None)
    in_specs = (spec, spec, spec, P(None, None, ("outer", "inner")), P())
    return jax.shard_map(body, mesh=mesh, in_specs=in_specs, out_specs=spec, check_vma=False)
```

```python
import functools

import jax
import jax.numpy as jnp
from jax import lax
from jax.experimental import pallas as pl
from jax.experimental.pallas import tpu as pltpu
from jax.sharding import PartitionSpec as P

HEADS = 8
HEAD = 128
LOCAL_BITS = 10
TILE = 128
CHUNK = 256
F32 = jnp.float32
BF16 = jnp.bfloat16
MIB = 1 << 20


def bits_of(count):
    return count.bit_length() - 1


def swap(block, axis, stride):
    count = lax.axis_size(axis)
    return lax.ppermute(block, axis, [(place, place ^ stride) for place in range(count)])


def raise_to(block, axis, stride):
    count = lax.axis_size(axis)
    route = [(place, place | stride) for place in range(count) if not place & stride]
    return lax.ppermute(block, axis, route)


def cost(flops, moved):
    return pl.CostEstimate(flops=flops, bytes_accessed=moved, transcendentals=0)


def params(limit):
    return pltpu.CompilerParams(vmem_limit_bytes=limit * MIB)


def product(left, right):
    return jnp.dot(left, right, preferred_element_type=F32)


def product_nt(left, right):
    return lax.dot_general(left, right, (((1,), (1,)), ((), ())), preferred_element_type=F32)


def identity(size):
    row = lax.broadcasted_iota(jnp.int32, (size, size), 0)
    column = lax.broadcasted_iota(jnp.int32, (size, size), 1)
    return (row == column).astype(F32).astype(BF16)


def turned(block):
    return product_nt(identity(block.shape[1]), block).astype(BF16)


def state_kernel(half, keys, values, state):
    both = product(turned(values[...]), keys[...])
    for low in range(0, keys.shape[1], HEAD):
        part = slice(low, low + HEAD)
        state[part, :] = both[part, part]


def block_state(half, keys, values):
    tokens, width = keys.shape
    step = 2 * HEAD
    steps = width // 2 // step
    column = pl.BlockSpec((tokens, step), lambda pair, half: (0, half[0] * steps + pair))
    return pl.pallas_call(
        state_kernel,
        grid_spec=pltpu.PrefetchScalarGridSpec(
            num_scalar_prefetch=1,
            grid=(steps,),
            in_specs=[column, column],
            out_specs=pl.BlockSpec((step, HEAD), lambda pair, half: (pair, 0)),
        ),
        out_shape=jax.ShapeDtypeStruct((width // 2, HEAD), F32),
        cost_estimate=cost(tokens * width * HEAD, 3 * MIB),
        compiler_params=params(58),
    )(half, keys, values)


def tile_mixing(rows):
    target = lax.broadcasted_iota(jnp.int32, (8, TILE), 1)
    source = lax.broadcasted_iota(jnp.int32, (8, TILE), 0)
    rows = [jnp.broadcast_to(row, (8, TILE)) for row in rows]
    within = jnp.bitwise_and(target, 7)
    differ = jnp.bitwise_xor(within, source)
    base = rows[3]
    for level in (2, 1, 0):
        base = jnp.where(differ < 1 << level, rows[level], base)
    parts = [jnp.where(source <= within, base, 0.0)]
    for bit in range(3, bits_of(TILE)):
        upper = jnp.bitwise_and(jnp.right_shift(target, bit), 1) == 1
        parts = [jnp.where(upper, rows[bit + 1], part) for part in parts] + [
            jnp.where(upper, part, 0.0) for part in parts
        ]
    return jnp.concatenate(parts, axis=0)


def local_kernel(first_head, queries, keys, values, weights, local, rows):
    tokens, width = queries.shape
    chunks = tokens // CHUNK
    levels = rows.shape[1]
    top = bits_of(CHUNK)
    spans = [slice(low, low + CHUNK) for low in range(0, tokens, CHUNK)]
    parts = [slice(low, low + HEAD) for low in range(0, width, HEAD)]
    first = first_head + pl.program_id(0) * len(parts)
    for at in range(len(parts)):
        rows[at] = weights[:, pl.ds(first + at, 1), :].reshape(levels, tokens)
    flipped = turned(values[...])

    def row(at, level, low, size):
        return rows[at, level : level + 1, low : low + size]

    nodes = []
    for part in parts:
        line = [product(flipped[part, span], keys[span, part]) for span in spans[:-1]]
        known = [line]
        while len(known[-1]) > 1:
            below = known[-1]
            known.append([below[at] + below[at + 1] for at in range(0, len(below) - 1, 2)])
        nodes.append([[state.astype(BF16) for state in level] for level in known])
    scores = {}
    for at, part in enumerate(parts):
        for chunk, span in enumerate(spans):
            used = [bit for bit in range(bits_of(chunks)) if chunk >> bit & 1]
            left = [keys[span, part]] + [nodes[at][bit][(chunk >> bit) - 1] for bit in used]
            left = jnp.concatenate(left, axis=0) if used else left[0]
            scores[at, chunk] = product_nt(left, queries[span, part])
    for at, part in enumerate(parts):
        for chunk, span in enumerate(spans):
            low = chunk * CHUNK
            score = scores[at, chunk]
            lower, upper = (
                tile_mixing([row(at, level, start, TILE) for level in range(top)]) for start in (low, low + TILE)
            )
            across = row(at, top, low + TILE, TILE)
            weighted = jnp.concatenate(
                [
                    jnp.concatenate([score[:TILE, :TILE] * lower, score[:TILE, TILE:] * across], axis=1),
                    jnp.concatenate([jnp.zeros_like(lower), score[TILE:CHUNK, TILE:] * upper], axis=1),
                ],
                axis=0,
            ).astype(BF16)
            total = product(flipped[part, span], weighted)
            below = CHUNK
            for bit in range(bits_of(chunks)):
                if chunk >> bit & 1:
                    total = total + row(at, top + 1 + bit, low, CHUNK) * score[below : below + HEAD, :]
                    below += HEAD
            local[part, span] = total


def local_part(half, queries, keys, values, level_weights):
    tokens, width = queries.shape
    step = 2 * HEAD
    steps = width // step // 2
    column = pl.BlockSpec((tokens, step), lambda pair: (0, half * steps + pair))
    return pl.pallas_call(
        functools.partial(local_kernel, half * steps * 2),
        grid=(steps,),
        in_specs=[column, column, column, pl.BlockSpec(level_weights.shape, lambda pair: (0, 0, 0))],
        out_specs=pl.BlockSpec((step, tokens), lambda pair: (pair, 0)),
        out_shape=jax.ShapeDtypeStruct((width // 2, tokens), F32),
        scratch_shapes=[pltpu.VMEM((2, level_weights.shape[0], tokens), F32)],
        cost_estimate=cost(3 * tokens * width * HEAD, 6 * MIB),
        compiler_params=params(40),
    )(queries, keys, values, level_weights)


def has_bit(place, bit):
    return jnp.bitwise_and(jnp.right_shift(place, bit), 1) == 1


def fill(states, base, half, place, digit_place, first_digit, mine, other, first=None):
    core = jnp.bitwise_and(place, 1)
    side = jnp.bitwise_and(jnp.right_shift(place, 1), 1)
    count, quarters, size = mine.shape[:3]
    for quarter in range(quarters):
        slot = jnp.bitwise_xor(side, quarter)
        for bit in range(count):
            if first is not None and bit == 0:
                here, there = first[quarter * size : (quarter + 1) * size, :], other[0, quarter]
            else:
                here, there = mine[bit, slot], other[bit, slot]
            state = jnp.where(core == half, here, there)
            state = jnp.where(has_bit(digit_place, first_digit + bit), state, 0.0).astype(BF16)
            for at in range(0, size, HEAD):
                head = (base + quarter * size + at) // HEAD
                low = (first_digit + bit) * HEAD
                states[head, low : low + HEAD, :] = state[at : at + HEAD]


def near_kernel(half, heads, place, queries, weights, local, first, mine, other, near, states, rows):
    step = pl.program_id(0)
    bits = states.shape[1] // HEAD

    @pl.when(step == 0)
    def _():
        fill(states, 0, half, place[0], place[0], 0, mine, other, first)

    for at in range(rows.shape[0]):
        part = slice(at * HEAD, (at + 1) * HEAD)
        head = step * rows.shape[0] + at
        rows[at] = weights[:, pl.ds(half * heads + head, 1), :].reshape(rows.shape[1:])
        products = product_nt(states[head], queries[:, part])
        total = local[part, :]
        for bit in range(bits):
            level = LOCAL_BITS + 1 + bit
            total = total + rows[at, level : level + 1, :] * products[bit * HEAD : (bit + 1) * HEAD]
        near[part, :] = total


def near_part(half, bits, place, queries, level_weights, local, first, mine, other):
    tokens, width = queries.shape
    heads = width // HEAD // 2
    step = 2 * HEAD
    steps = width // step // 2
    column = pl.BlockSpec((tokens, step), lambda pair: (0, half * steps + pair))
    band = pl.BlockSpec((step, tokens), lambda pair: (pair, 0))
    fixed = [pl.BlockSpec(part.shape, lambda pair, rank=part.ndim: (0,) * rank)
             for part in (first, mine, other)]
    return pl.pallas_call(
        functools.partial(near_kernel, half, heads),
        grid=(steps,),
        in_specs=[
            pl.BlockSpec(memory_space=pltpu.SMEM),
            column,
            pl.BlockSpec(level_weights.shape, lambda pair: (0, 0, 0)),
            band,
            *fixed,
        ],
        out_specs=band,
        out_shape=jax.ShapeDtypeStruct((width // 2, tokens), F32),
        scratch_shapes=[
            pltpu.VMEM((heads, bits * HEAD, HEAD), BF16),
            pltpu.VMEM((2, level_weights.shape[0], tokens), F32),
        ],
        cost_estimate=cost(bits * tokens * width * HEAD, 8 * MIB),
        compiler_params=params(40),
    )(place, queries, level_weights, local, first, mine, other)


def far_kernel(first_level, place, queries, weights, lower, upper, *rest):
    arrived, (out_weight, mixed, states, flipped, attended) = rest[:-5], rest[-5:]
    rows, width = attended.shape
    bits = states.shape[1] // HEAD

    @pl.when(pl.program_id(0) == 0)
    def _():
        for half in range(2):
            digit = 0
            for mine, other in zip(arrived[::2], arrived[1::2]):
                fill(states, half * (width // 2), half, place[0], place[1], digit, mine, other)
                digit += mine.shape[0]

    for half, near in enumerate((lower, upper)):
        for low in range(0, width // 2, HEAD):
            part = slice(half * (width // 2) + low, half * (width // 2) + low + HEAD)
            head = part.start // HEAD
            products = product_nt(states[head], queries[:, part])
            total = near[low : low + HEAD, :]
            for bit in range(bits):
                row = weights[first_level + bit, head : head + 1, :]
                total = total + row * products[bit * HEAD : (bit + 1) * HEAD]
            flipped[part, :] = total.astype(BF16)
    unit = identity(CHUNK)
    for top in range(0, rows, CHUNK):
        for low in range(0, width, CHUNK):
            block = flipped[low : low + CHUNK, top : top + CHUNK]
            attended[top : top + CHUNK, low : low + CHUNK] = product_nt(unit, block).astype(BF16)
    mixed[...] = product(attended[...], out_weight[...]).astype(BF16)


def far_part(first_level, place, queries, level_weights, lower, upper, arrived, out_weight):
    tokens, width = queries.shape
    bits = sum(part.shape[0] for part in arrived[::2])
    rows = min(2 * CHUNK, tokens)
    band = pl.BlockSpec((rows, width), lambda step: (step, 0))
    near = pl.BlockSpec((width // 2, rows), lambda step: (0, step))
    fixed = [pl.BlockSpec(part.shape, lambda step: (0, 0, 0, 0)) for part in arrived]
    return pl.pallas_call(
        functools.partial(far_kernel, first_level),
        grid=(tokens // rows,),
        in_specs=[
            pl.BlockSpec(memory_space=pltpu.SMEM),
            band,
            pl.BlockSpec(level_weights.shape[:2] + (rows,), lambda step: (0, 0, step)),
            near,
            near,
            *fixed,
            pl.BlockSpec(out_weight.shape, lambda step: (0, 0)),
        ],
        out_specs=band,
        out_shape=jax.ShapeDtypeStruct((tokens, width), BF16),
        scratch_shapes=[
            pltpu.VMEM((width // HEAD, bits * HEAD, HEAD), BF16),
            pltpu.VMEM((width, rows), BF16),
            pltpu.VMEM((rows, width), BF16),
        ],
        cost_estimate=cost(2 * tokens * width * (width + bits * HEAD), 12 * MIB),
        compiler_params=params(28),
    )(place, queries, level_weights, lower, upper, *arrived, out_weight)


def body(queries, keys, values, level_weights, out_weight):
    inner, outer = lax.axis_size("inner"), lax.axis_size("outer")
    inner_bits, outer_bits = bits_of(inner), bits_of(outer)
    inner_place, outer_place = lax.axis_index("inner"), lax.axis_index("outer")
    place = jnp.stack([inner_place, outer_place]).astype(jnp.int32)
    core = jnp.bitwise_and(inner_place, 1)
    side = jnp.bitwise_and(jnp.right_shift(inner_place, 1), 1)
    half = keys.shape[1] // 2
    quarter = half // 2
    tie = lax.optimization_barrier

    give = block_state((1 - core).reshape(1).astype(jnp.int32), keys, values)
    first = swap(give, "inner", 1)
    keep = block_state(core.reshape(1).astype(jnp.int32), keys, values)

    def quarter_of(at):
        return lax.dynamic_slice_in_dim(keep, at * quarter, quarter, 0) + lax.dynamic_slice_in_dim(
            first, at * quarter, quarter, 0
        )

    own, passed = quarter_of(side), quarter_of(1 - side)
    running = own
    buckets = []
    for bit in range(1, inner_bits):
        buckets.append(swap(passed if bit == 1 else running, "inner", 1 << bit))
        running = running + buckets[-1]

    inputs = (queries, keys, values, level_weights)
    sent = jnp.stack([own] + buckets[1:])
    running, sent, inputs = tie((running, sent, inputs))
    arrived = swap(running, "outer", 1)
    local = [local_part(0, *inputs)]
    arrived, sent, local[0] = tie((arrived, sent, local[0]))
    others = swap(sent, "inner", 2)

    far = [arrived]
    beside = []
    for bit in range(1, outer_bits):
        running = running + arrived
        running, inputs = tie((running, inputs))
        arrived = swap(running, "outer", 1 << bit)
        if bit == 1:
            local.append(local_part(1, *inputs))
            arrived, far, others, local[1] = tie((arrived, far, others, local[1]))
        beside.append(swap(far[-1], "inner", 2))
        far.append(arrived)
    if len(local) < 2:
        local.append(local_part(1, *inputs))
    mine = jnp.stack(
        [keep.reshape(2, quarter, HEAD)] + [jnp.stack([bucket, others[at]]) for at, bucket in enumerate(buckets)]
    )
    other = swap(mine, "inner", 1)
    far[-1], local = tie((far[-1], local))
    last = swap(far[-1], "inner", 2)
    nears = [
        near_part(part, inner_bits, place, queries, level_weights, local[part], first, mine, other) for part in range(2)
    ]
    last, beside, nears = tie((last, beside, nears))
    far_mine = jnp.stack([jnp.stack(pair) for pair in zip(far, beside + [last])])
    arrivals = [far_mine, swap(far_mine, "inner", 1)]
    first_level = LOCAL_BITS + 1 + inner_bits
    return far_part(first_level, place, queries, level_weights, *nears, arrivals, out_weight)


def solution(mesh):
    spec = P(("outer", "inner"), None)
    in_specs = (spec, spec, spec, P(None, None, ("outer", "inner")), P())
    return jax.shard_map(body, mesh=mesh, in_specs=in_specs, out_specs=spec, check_vma=False)
```

```python
import functools

import jax
import jax.numpy as jnp
from jax import lax
from jax.experimental import pallas as pl
from jax.experimental.pallas import tpu as pltpu
from jax.sharding import PartitionSpec as P

HEADS = 8
HEAD = 128
LOCAL_BITS = 10
TILE = 128
CHUNK = 256
F32 = jnp.float32
BF16 = jnp.bfloat16
MIB = 1 << 20


def bits_of(count):
    return count.bit_length() - 1


def swap(block, axis, stride):
    count = lax.axis_size(axis)
    return lax.ppermute(block, axis, [(place, place ^ stride) for place in range(count)])


def raise_to(block, axis, stride):
    count = lax.axis_size(axis)
    route = [(place, place | stride) for place in range(count) if not place & stride]
    return lax.ppermute(block, axis, route)


def cost(flops, moved):
    return pl.CostEstimate(flops=flops, bytes_accessed=moved, transcendentals=0)


def params(limit):
    return pltpu.CompilerParams(vmem_limit_bytes=limit * MIB)


def product(left, right):
    return jnp.dot(left, right, preferred_element_type=F32)


def product_nt(left, right):
    return lax.dot_general(left, right, (((1,), (1,)), ((), ())), preferred_element_type=F32)


def identity(size):
    row = lax.broadcasted_iota(jnp.int32, (size, size), 0)
    column = lax.broadcasted_iota(jnp.int32, (size, size), 1)
    return (row == column).astype(F32).astype(BF16)


def turned(block):
    return product_nt(identity(block.shape[1]), block).astype(BF16)


def state_kernel(place, keys, values, state):
    both = product(turned(values[...]), keys[...])
    for low in range(0, keys.shape[1], HEAD):
        part = slice(low, low + HEAD)
        state[part, :] = both[part, part]


def block_state(place, share, keys, values):
    tokens, width = keys.shape
    step = 2 * HEAD
    steps = width // share // step
    column = pl.BlockSpec((tokens, step), lambda pair, place: (0, place[0] * steps + pair))
    return pl.pallas_call(
        state_kernel,
        grid_spec=pltpu.PrefetchScalarGridSpec(
            num_scalar_prefetch=1,
            grid=(steps,),
            in_specs=[column, column],
            out_specs=pl.BlockSpec((step, HEAD), lambda pair, place: (pair, 0)),
        ),
        out_shape=pltpu.VMEM((width // share, HEAD), F32),
        cost_estimate=cost(2 * tokens * width * HEAD // share, 5 * MIB // share),
        compiler_params=params(16),
    )(place.reshape(1).astype(jnp.int32), keys, values)


def tile_mixing(rows):
    target = lax.broadcasted_iota(jnp.int32, (8, TILE), 1)
    source = lax.broadcasted_iota(jnp.int32, (8, TILE), 0)
    rows = [jnp.broadcast_to(row, (8, TILE)) for row in rows]
    within = jnp.bitwise_and(target, 7)
    differ = jnp.bitwise_xor(within, source)
    base = rows[3]
    for level in (2, 1, 0):
        base = jnp.where(differ < 1 << level, rows[level], base)
    parts = [jnp.where(source <= within, base, 0.0)]
    for bit in range(3, bits_of(TILE)):
        upper = jnp.bitwise_and(jnp.right_shift(target, bit), 1) == 1
        parts = [jnp.where(upper, rows[bit + 1], part) for part in parts] + [
            jnp.where(upper, part, 0.0) for part in parts
        ]
    return jnp.concatenate(parts, axis=0)


def local_kernel(first_head, queries, keys, values, weights, local, rows):
    tokens, width = queries.shape
    chunks = tokens // CHUNK
    levels = rows.shape[1]
    top = bits_of(CHUNK)
    spans = [slice(low, low + CHUNK) for low in range(0, tokens, CHUNK)]
    parts = [slice(low, low + HEAD) for low in range(0, width, HEAD)]
    first = first_head + pl.program_id(0) * len(parts)
    for at in range(len(parts)):
        rows[at] = weights[:, pl.ds(first + at, 1), :].reshape(levels, tokens)
    flipped = turned(values[...])

    def row(at, level, low, size):
        return rows[at, level : level + 1, low : low + size]

    nodes = []
    for part in parts:
        line = [product(flipped[part, span], keys[span, part]) for span in spans[:-1]]
        known = [line]
        while len(known[-1]) > 1:
            below = known[-1]
            known.append([below[at] + below[at + 1] for at in range(0, len(below) - 1, 2)])
        nodes.append([[state.astype(BF16) for state in level] for level in known])
    scores = {}
    for at, part in enumerate(parts):
        for chunk, span in enumerate(spans):
            used = [bit for bit in range(bits_of(chunks)) if chunk >> bit & 1]
            left = [keys[span, part]] + [nodes[at][bit][(chunk >> bit) - 1] for bit in used]
            left = jnp.concatenate(left, axis=0) if used else left[0]
            scores[at, chunk] = product_nt(left, queries[span, part])
    for at, part in enumerate(parts):
        for chunk, span in enumerate(spans):
            low = chunk * CHUNK
            score = scores[at, chunk]
            lower, upper = (
                tile_mixing([row(at, level, start, TILE) for level in range(top)]) for start in (low, low + TILE)
            )
            across = row(at, top, low + TILE, TILE)
            weighted = jnp.concatenate(
                [
                    jnp.concatenate([score[:TILE, :TILE] * lower, score[:TILE, TILE:] * across], axis=1),
                    jnp.concatenate([jnp.zeros_like(lower), score[TILE:CHUNK, TILE:] * upper], axis=1),
                ],
                axis=0,
            ).astype(BF16)
            total = product(flipped[part, span], weighted)
            below = CHUNK
            for bit in range(bits_of(chunks)):
                if chunk >> bit & 1:
                    total = total + row(at, top + 1 + bit, low, CHUNK) * score[below : below + HEAD, :]
                    below += HEAD
            local[part, span] = total


def local_part(half, queries, keys, values, level_weights):
    tokens, width = queries.shape
    step = 2 * HEAD
    steps = width // step // 2
    column = pl.BlockSpec((tokens, step), lambda pair: (0, half * steps + pair))
    return pl.pallas_call(
        functools.partial(local_kernel, half * steps * 2),
        grid=(steps,),
        in_specs=[column, column, column, pl.BlockSpec(level_weights.shape, lambda pair: (0, 0, 0))],
        out_specs=pl.BlockSpec((step, tokens), lambda pair: (pair, 0)),
        out_shape=jax.ShapeDtypeStruct((width // 2, tokens), F32),
        scratch_shapes=[pltpu.VMEM((2, level_weights.shape[0], tokens), F32)],
        cost_estimate=cost(tokens * width, MIB // 4),
        compiler_params=params(16),
    )(queries, keys, values, level_weights)


def has_bit(place, bit):
    return jnp.bitwise_and(jnp.right_shift(place, bit), 1) == 1


def fill(states, base, half, place, digit_place, first_digit, mine, other, first=None):
    core = jnp.bitwise_and(place, 1)
    side = jnp.bitwise_and(jnp.right_shift(place, 1), 1)
    count, quarters, size = mine.shape[:3]
    for quarter in range(quarters):
        slot = jnp.bitwise_xor(side, quarter)
        for bit in range(count):
            if first is not None and bit == 0:
                here, there = first[quarter * size : (quarter + 1) * size, :], other[0, slot]
            else:
                here, there = mine[bit, slot], other[bit, slot]
            state = jnp.where(core == half, here, there)
            state = jnp.where(has_bit(digit_place, first_digit + bit), state, 0.0).astype(BF16)
            for at in range(0, size, HEAD):
                head = (base + quarter * size + at) // HEAD
                low = (first_digit + bit) * HEAD
                states[head, low : low + HEAD, :] = state[at : at + HEAD]


def near_kernel(half, heads, place, queries, weights, local, first, mine, other, near, states, rows):
    step = pl.program_id(0)
    bits = states.shape[1] // HEAD

    @pl.when(step == 0)
    def _():
        fill(states, 0, half, place[0], place[0], 0, mine, other, first)

    for at in range(rows.shape[0]):
        part = slice(at * HEAD, (at + 1) * HEAD)
        head = step * rows.shape[0] + at
        rows[at] = weights[:, pl.ds(half * heads + head, 1), :].reshape(rows.shape[1:])
        products = product_nt(states[head], queries[:, part])
        total = local[part, :]
        for bit in range(bits):
            level = LOCAL_BITS + 1 + bit
            total = total + rows[at, level : level + 1, :] * products[bit * HEAD : (bit + 1) * HEAD]
        near[part, :] = total


def near_part(half, bits, place, queries, level_weights, local, first, mine, other):
    tokens, width = queries.shape
    heads = width // HEAD // 2
    step = 2 * HEAD
    steps = width // step // 2
    column = pl.BlockSpec((tokens, step), lambda pair: (0, half * steps + pair))
    band = pl.BlockSpec((step, tokens), lambda pair: (pair, 0))
    fixed = [pl.BlockSpec(part.shape, lambda pair, rank=part.ndim: (0,) * rank)
             for part in (first, mine, other)]
    return pl.pallas_call(
        functools.partial(near_kernel, half, heads),
        grid=(steps,),
        in_specs=[
            pl.BlockSpec(memory_space=pltpu.SMEM),
            column,
            pl.BlockSpec(level_weights.shape, lambda pair: (0, 0, 0)),
            band,
            *fixed,
        ],
        out_specs=band,
        out_shape=jax.ShapeDtypeStruct((width // 2, tokens), F32),
        scratch_shapes=[
            pltpu.VMEM((heads, bits * HEAD, HEAD), BF16),
            pltpu.VMEM((2, level_weights.shape[0], tokens), F32),
        ],
        cost_estimate=cost(tokens * width, MIB // 4),
        compiler_params=params(16),
    )(place, queries, level_weights, local, first, mine, other)


def far_kernel(first_level, place, queries, weights, lower, upper, *rest):
    arrived, (out_weight, mixed, states, flipped, attended) = rest[:-5], rest[-5:]
    rows, width = attended.shape
    bits = states.shape[1] // HEAD

    @pl.when(pl.program_id(0) == 0)
    def _():
        for half in range(2):
            digit = 0
            for mine, other in zip(arrived[::2], arrived[1::2]):
                fill(states, half * (width // 2), half, place[0], place[1], digit, mine, other)
                digit += mine.shape[0]

    for half, near in enumerate((lower, upper)):
        for low in range(0, width // 2, HEAD):
            part = slice(half * (width // 2) + low, half * (width // 2) + low + HEAD)
            head = part.start // HEAD
            products = product_nt(states[head], queries[:, part])
            total = near[low : low + HEAD, :]
            for bit in range(bits):
                row = weights[first_level + bit, head : head + 1, :]
                total = total + row * products[bit * HEAD : (bit + 1) * HEAD]
            flipped[part, :] = total.astype(BF16)
    unit = identity(CHUNK)
    for top in range(0, rows, CHUNK):
        for low in range(0, width, CHUNK):
            block = flipped[low : low + CHUNK, top : top + CHUNK]
            attended[top : top + CHUNK, low : low + CHUNK] = product_nt(unit, block).astype(BF16)
    mixed[...] = product(attended[...], out_weight[...]).astype(BF16)


def far_part(first_level, place, queries, level_weights, lower, upper, arrived, out_weight):
    tokens, width = queries.shape
    bits = sum(part.shape[0] for part in arrived[::2])
    rows = min(2 * CHUNK, tokens)
    band = pl.BlockSpec((rows, width), lambda step: (step, 0))
    near = pl.BlockSpec((width // 2, rows), lambda step: (0, step))
    fixed = [pl.BlockSpec(part.shape, lambda step: (0, 0, 0, 0)) for part in arrived]
    return pl.pallas_call(
        functools.partial(far_kernel, first_level),
        grid=(tokens // rows,),
        in_specs=[
            pl.BlockSpec(memory_space=pltpu.SMEM),
            band,
            pl.BlockSpec(level_weights.shape[:2] + (rows,), lambda step: (0, 0, step)),
            near,
            near,
            *fixed,
            pl.BlockSpec(out_weight.shape, lambda step: (0, 0)),
        ],
        out_specs=band,
        out_shape=jax.ShapeDtypeStruct((tokens, width), BF16),
        scratch_shapes=[
            pltpu.VMEM((width // HEAD, bits * HEAD, HEAD), BF16),
            pltpu.VMEM((width, rows), BF16),
            pltpu.VMEM((rows, width), BF16),
        ],
        cost_estimate=cost(2 * tokens * width * (width + bits * HEAD), 12 * MIB),
        compiler_params=params(28),
    )(place, queries, level_weights, lower, upper, *arrived, out_weight)


def body(queries, keys, values, level_weights, out_weight):
    inner, outer = lax.axis_size("inner"), lax.axis_size("outer")
    inner_bits, outer_bits = bits_of(inner), bits_of(outer)
    inner_place, outer_place = lax.axis_index("inner"), lax.axis_index("outer")
    place = jnp.stack([inner_place, outer_place]).astype(jnp.int32)
    core = jnp.bitwise_and(inner_place, 1)
    side = jnp.bitwise_and(jnp.right_shift(inner_place, 1), 1)
    half = keys.shape[1] // 2
    quarter = half // 2
    tie = lax.optimization_barrier

    inputs = tuple(pltpu.with_memory_space_constraint(part, pltpu.HBM) for part in (keys, values))
    give = block_state(1 - core, 2, *inputs)
    give, inputs = tie((give, inputs))
    first = swap(give, "inner", 1)

    def quarter_of(at, state):
        return state + lax.dynamic_slice_in_dim(first, at * quarter, quarter, 0)

    keep_theirs = block_state(2 * core + 1 - side, 4, *inputs)
    passed = quarter_of(1 - side, keep_theirs)
    passed, inputs = tie((passed, inputs))
    buckets = [swap(passed, "inner", 2)]
    keep_ours = block_state(2 * core + side, 4, *inputs)
    inputs = (queries, keys, values, level_weights)
    own = quarter_of(side, keep_ours)
    others = [swap(own, "inner", 2)]
    running = own + buckets[0]
    running, inputs = tie((running, inputs))
    local = [local_part(0, *inputs)]
    for bit in range(2, inner_bits):
        arrived = swap(running, "inner", 1 << bit)
        if bit == 2:
            arrived, local[0] = tie((arrived, local[0]))
        buckets.append(arrived)
        running = running + arrived
    sent = swap(jnp.stack(buckets[1:]), "inner", 2)

    far = [swap(running, "outer", 1)]
    beside = []
    for bit in range(1, outer_bits):
        running = running + far[-1]
        running, inputs = tie((running, inputs))
        far.append(swap(running, "outer", 1 << bit))
        beside.append(swap(far[-2], "inner", 2))
        if bit == 1:
            local.append(local_part(1, *inputs))
            far[-1], beside, sent, others, local[1] = tie((far[-1], beside, sent, others, local[1]))
    if len(local) < 2:
        local.append(local_part(1, *inputs))
    others += [sent[at] for at in range(inner_bits - 2)]
    mine = jnp.stack([jnp.stack([keep_ours, keep_theirs])] + [jnp.stack(pair) for pair in zip(buckets, others)])
    other = swap(mine, "inner", 1)
    far[-1], local = tie((far[-1], local))
    last = swap(far[-1], "inner", 2)
    nears = [
        near_part(part, inner_bits, place, queries, level_weights, local[part], first, mine, other) for part in range(2)
    ]
    last, beside, nears = tie((last, beside, nears))
    far_mine = jnp.stack([jnp.stack(pair) for pair in zip(far, beside + [last])])
    arrivals = [far_mine, swap(far_mine, "inner", 1)]
    first_level = LOCAL_BITS + 1 + inner_bits
    return far_part(first_level, place, queries, level_weights, *nears, arrivals, out_weight)


def solution(mesh):
    spec = P(("outer", "inner"), None)
    in_specs = (spec, spec, spec, P(None, None, ("outer", "inner")), P())
    return jax.shard_map(body, mesh=mesh, in_specs=in_specs, out_specs=spec, check_vma=False)
```

```python
import functools

import jax
import jax.numpy as jnp
from jax import lax
from jax.experimental import pallas as pl
from jax.experimental.pallas import tpu as pltpu
from jax.sharding import PartitionSpec as P

HEADS = 8
HEAD = 128
LOCAL_BITS = 10
TILE = 128
CHUNK = 256
F32 = jnp.float32
BF16 = jnp.bfloat16
MIB = 1 << 20


def bits_of(count):
    return count.bit_length() - 1


def swap(block, axis, stride):
    count = lax.axis_size(axis)
    return lax.ppermute(block, axis, [(place, place ^ stride) for place in range(count)])


def raise_to(block, axis, stride):
    count = lax.axis_size(axis)
    route = [(place, place | stride) for place in range(count) if not place & stride]
    return lax.ppermute(block, axis, route)


def cost(flops, moved):
    return pl.CostEstimate(flops=flops, bytes_accessed=moved, transcendentals=0)


def params(limit):
    return pltpu.CompilerParams(vmem_limit_bytes=limit * MIB)


def outside(*parts):
    return tuple(pltpu.with_memory_space_constraint(part, pltpu.HBM) for part in parts)


def product(left, right):
    return jnp.dot(left, right, preferred_element_type=F32)


def product_nt(left, right):
    return lax.dot_general(left, right, (((1,), (1,)), ((), ())), preferred_element_type=F32)


def identity(size):
    row = lax.broadcasted_iota(jnp.int32, (size, size), 0)
    column = lax.broadcasted_iota(jnp.int32, (size, size), 1)
    return (row == column).astype(F32).astype(BF16)


def turned(block):
    return product_nt(identity(block.shape[1]), block).astype(BF16)


def state_kernel(place, keys, values, state):
    both = product(turned(values[...]), keys[...])
    for low in range(0, keys.shape[1], HEAD):
        part = slice(low, low + HEAD)
        state[part, :] = both[part, part]


def block_state(place, share, keys, values):
    tokens, width = keys.shape
    step = 2 * HEAD
    steps = width // share // step
    column = pl.BlockSpec((tokens, step), lambda pair, place: (0, place[0] * steps + pair))
    return pl.pallas_call(
        state_kernel,
        grid_spec=pltpu.PrefetchScalarGridSpec(
            num_scalar_prefetch=1,
            grid=(steps,),
            in_specs=[column, column],
            out_specs=pl.BlockSpec((step, HEAD), lambda pair, place: (pair, 0)),
        ),
        out_shape=pltpu.VMEM((width // share, HEAD), F32),
        cost_estimate=cost(2 * tokens * width * HEAD // share, 5 * MIB // share),
        compiler_params=params(16),
    )(place.reshape(1).astype(jnp.int32), keys, values)


def tile_mixing(rows):
    target = lax.broadcasted_iota(jnp.int32, (8, TILE), 1)
    source = lax.broadcasted_iota(jnp.int32, (8, TILE), 0)
    rows = [jnp.broadcast_to(row, (8, TILE)) for row in rows]
    within = jnp.bitwise_and(target, 7)
    differ = jnp.bitwise_xor(within, source)
    base = rows[3]
    for level in (2, 1, 0):
        base = jnp.where(differ < 1 << level, rows[level], base)
    parts = [jnp.where(source <= within, base, 0.0)]
    for bit in range(3, bits_of(TILE)):
        upper = jnp.bitwise_and(jnp.right_shift(target, bit), 1) == 1
        parts = [jnp.where(upper, rows[bit + 1], part) for part in parts] + [
            jnp.where(upper, part, 0.0) for part in parts
        ]
    return jnp.concatenate(parts, axis=0)


def local_kernel(half, queries, keys, values, weights, local, rows):
    tokens, width = queries.shape
    chunks = tokens // CHUNK
    levels = rows.shape[1]
    top = bits_of(CHUNK)
    spans = [slice(low, low + CHUNK) for low in range(0, tokens, CHUNK)]
    parts = [slice(low, low + HEAD) for low in range(0, width, HEAD)]
    first = (half[0] * pl.num_programs(0) + pl.program_id(0)) * len(parts)
    for at in range(len(parts)):
        rows[at] = weights[:, pl.ds(first + at, 1), :].reshape(levels, tokens)
    flipped = turned(values[...])

    def row(at, level, low, size):
        return rows[at, level : level + 1, low : low + size]

    nodes = []
    for part in parts:
        line = [product(flipped[part, span], keys[span, part]) for span in spans[:-1]]
        known = [line]
        while len(known[-1]) > 1:
            below = known[-1]
            known.append([below[at] + below[at + 1] for at in range(0, len(below) - 1, 2)])
        nodes.append([[state.astype(BF16) for state in level] for level in known])
    scores = {}
    for at, part in enumerate(parts):
        for chunk, span in enumerate(spans):
            used = [bit for bit in range(bits_of(chunks)) if chunk >> bit & 1]
            left = [keys[span, part]] + [nodes[at][bit][(chunk >> bit) - 1] for bit in used]
            left = jnp.concatenate(left, axis=0) if used else left[0]
            scores[at, chunk] = product_nt(left, queries[span, part])
    for at, part in enumerate(parts):
        for chunk, span in enumerate(spans):
            low = chunk * CHUNK
            score = scores[at, chunk]
            lower, upper = (
                tile_mixing([row(at, level, start, TILE) for level in range(top)]) for start in (low, low + TILE)
            )
            across = row(at, top, low + TILE, TILE)
            weighted = jnp.concatenate(
                [
                    jnp.concatenate([score[:TILE, :TILE] * lower, score[:TILE, TILE:] * across], axis=1),
                    jnp.concatenate([jnp.zeros_like(lower), score[TILE:CHUNK, TILE:] * upper], axis=1),
                ],
                axis=0,
            ).astype(BF16)
            total = product(flipped[part, span], weighted)
            below = CHUNK
            for bit in range(bits_of(chunks)):
                if chunk >> bit & 1:
                    total = total + row(at, top + 1 + bit, low, CHUNK) * score[below : below + HEAD, :]
                    below += HEAD
            local[part, span] = total


def local_part(half, queries, keys, values, level_weights):
    tokens, width = queries.shape
    step = 2 * HEAD
    steps = width // step // 2
    column = pl.BlockSpec((tokens, step), lambda pair, half: (0, half[0] * steps + pair))
    return pl.pallas_call(
        local_kernel,
        grid_spec=pltpu.PrefetchScalarGridSpec(
            num_scalar_prefetch=1,
            grid=(steps,),
            in_specs=[column, column, column, pl.BlockSpec(level_weights.shape, lambda pair, half: (0, 0, 0))],
            out_specs=pl.BlockSpec((step, tokens), lambda pair, half: (pair, 0)),
            scratch_shapes=[pltpu.VMEM((2, level_weights.shape[0], tokens), F32)],
        ),
        out_shape=pltpu.HBM((width // 2, tokens), F32),
        cost_estimate=cost(tokens * width, MIB // 4),
        compiler_params=params(16),
    )(half.reshape(1), queries, keys, values, level_weights)


def has_bit(place, bit):
    return jnp.bitwise_and(jnp.right_shift(place, bit), 1) == 1


def near_kernel(half, place, queries, weights, local, held, *rest):
    *first, near, states, rows = rest
    step = pl.program_id(0)
    bits = states.shape[1] // HEAD
    size = held.shape[1]

    @pl.when(step == 0)
    def _():
        side = jnp.bitwise_and(jnp.right_shift(place[0], 1), 1)
        for quarter in range(2):
            slot = jnp.bitwise_xor(side, quarter)
            for bit in range(bits):
                if first and bit == 0:
                    state = first[0][quarter * size : (quarter + 1) * size, :]
                else:
                    state = held[2 * bit + slot]
                state = jnp.where(has_bit(place[0], bit), state, 0.0).astype(BF16)
                for at in range(0, size, HEAD):
                    states[(quarter * size + at) // HEAD, bit * HEAD : (bit + 1) * HEAD, :] = state[at : at + HEAD]

    for at in range(rows.shape[0]):
        part = slice(at * HEAD, (at + 1) * HEAD)
        head = step * rows.shape[0] + at
        rows[at] = weights[:, pl.ds(half[0] * states.shape[0] + head, 1), :].reshape(rows.shape[1:])
        products = product_nt(states[head], queries[:, part])
        total = local[part, :]
        for bit in range(bits):
            level = LOCAL_BITS + 1 + bit
            total = total + rows[at, level : level + 1, :] * products[bit * HEAD : (bit + 1) * HEAD]
        near[part, :] = total


def near_part(half, place, bits, queries, level_weights, local, held, *first):
    tokens, width = queries.shape
    heads = width // HEAD // 2
    step = 2 * HEAD
    steps = width // step // 2
    return pl.pallas_call(
        near_kernel,
        grid_spec=pltpu.PrefetchScalarGridSpec(
            num_scalar_prefetch=2,
            grid=(steps,),
            in_specs=[
                pl.BlockSpec((tokens, step), lambda pair, half, place: (0, half[0] * steps + pair)),
                pl.BlockSpec(level_weights.shape, lambda pair, half, place: (0, 0, 0)),
                pl.BlockSpec((step, tokens), lambda pair, half, place: (pair, 0)),
                pl.BlockSpec((2 * bits,) + held.shape[1:], lambda pair, half, place: (0, 0, 0)),
                *[pl.BlockSpec(part.shape, lambda pair, half, place: (0, 0)) for part in first],
            ],
            out_specs=pl.BlockSpec((step, tokens), lambda pair, half, place: (pair, 0)),
            scratch_shapes=[
                pltpu.VMEM((heads, bits * HEAD, HEAD), BF16),
                pltpu.VMEM((2, level_weights.shape[0], tokens), F32),
            ],
        ),
        out_shape=pltpu.VMEM((width // 2, tokens), F32),
        cost_estimate=cost(tokens * width, MIB // 4),
        compiler_params=params(16),
    )(half.reshape(1), place, *outside(queries, level_weights, local), held, *first)


def far_kernel(first_level, place, queries, weights, near_mine, near_other, early, early_other, late, late_other,
               out_weight, mixed, states, flipped, attended):
    rows, width = attended.shape
    bits = states.shape[1] // HEAD
    size = late.shape[0]
    skip = early.shape[0] + 1 - 2 * bits
    core = jnp.bitwise_and(place[0], 1)

    @pl.when(pl.program_id(0) == 0)
    def _():
        side = jnp.bitwise_and(jnp.right_shift(place[0], 1), 1)
        for bit in range(bits):
            mine, other = ([part[skip + 2 * bit], part[skip + 2 * bit + 1] if bit + 1 < bits else final[...]]
                           for part, final in ((early, late), (early_other, late_other)))
            for quarter in range(4):
                here, there = (jnp.where(side == quarter % 2, *part) for part in (mine, other))
                state = jnp.where(core == quarter // 2, here, there)
                state = jnp.where(has_bit(place[1], bit), state, 0.0).astype(BF16)
                for at in range(0, size, HEAD):
                    head = (quarter * size + at) // HEAD
                    states[head, bit * HEAD : (bit + 1) * HEAD, :] = state[at : at + HEAD]

    start = pl.multiple_of(pl.program_id(0) * rows, rows)
    band = pl.ds(start, rows)
    for half in range(2):
        for low in range(0, width // 2, HEAD):
            part = slice(half * (width // 2) + low, half * (width // 2) + low + HEAD)
            head = part.start // HEAD
            products = product_nt(states[head], queries[band, part])
            span = slice(low, low + HEAD)
            total = jnp.where(core == half, near_mine[span, band], near_other[span, band])
            for bit in range(bits):
                row = weights[first_level + bit, head : head + 1, band]
                total = total + row * products[bit * HEAD : (bit + 1) * HEAD]
            flipped[part, :] = total.astype(BF16)
    unit = identity(CHUNK)
    for top in range(0, rows, CHUNK):
        for low in range(0, width, CHUNK):
            block = flipped[low : low + CHUNK, top : top + CHUNK]
            attended[top : top + CHUNK, low : low + CHUNK] = product_nt(unit, block).astype(BF16)
    mixed[...] = product(attended[...], out_weight[...]).astype(BF16)


def far_part(first_level, bits, place, *operands):
    queries = operands[0]
    tokens, width = queries.shape
    rows = min(2 * CHUNK, tokens)
    return pl.pallas_call(
        functools.partial(far_kernel, first_level),
        grid=(tokens // rows,),
        in_specs=[pl.BlockSpec(memory_space=pltpu.SMEM)]
        + [pl.BlockSpec(memory_space=pltpu.VMEM)] * len(operands),
        out_specs=pl.BlockSpec((rows, width), lambda step: (step, 0)),
        out_shape=jax.ShapeDtypeStruct((tokens, width), BF16),
        scratch_shapes=[
            pltpu.VMEM((width // HEAD, bits * HEAD, HEAD), BF16),
            pltpu.VMEM((width, rows), BF16),
            pltpu.VMEM((rows, width), BF16),
        ],
        cost_estimate=cost(2 * tokens * width * (width + bits * HEAD), 12 * MIB),
        compiler_params=params(28),
    )(place, *(pltpu.with_memory_space_constraint(part, pltpu.VMEM) for part in operands))


def body(queries, keys, values, level_weights, out_weight):
    inner, outer = lax.axis_size("inner"), lax.axis_size("outer")
    inner_bits, outer_bits = bits_of(inner), bits_of(outer)
    inner_place, outer_place = lax.axis_index("inner"), lax.axis_index("outer")
    place = jnp.stack([inner_place, outer_place]).astype(jnp.int32)
    core = jnp.bitwise_and(inner_place, 1).astype(jnp.int32)
    side = jnp.bitwise_and(jnp.right_shift(inner_place, 1), 1)
    half = keys.shape[1] // 2
    quarter = half // 2
    tie = lax.optimization_barrier

    inputs = outside(keys, values)
    give = block_state(1 - core, 2, *inputs)
    give, inputs = tie((give, inputs))
    first = swap(give, "inner", 1)

    def quarter_of(at, state):
        return state + lax.dynamic_slice_in_dim(first, at * quarter, quarter, 0)

    keep_theirs = block_state(2 * core + 1 - side, 4, *inputs)
    passed = quarter_of(1 - side, keep_theirs)
    passed, inputs = tie((passed, inputs))
    buckets = [swap(passed, "inner", 2)]
    keep_ours = block_state(2 * core + side, 4, *inputs)
    inputs = outside(queries, keys, values, level_weights)
    own = quarter_of(side, keep_ours)
    others = [swap(own, "inner", 2)]
    running = own + buckets[0]
    running, inputs = tie((running, inputs))
    local = [local_part(core, *inputs)]
    for bit in range(2, inner_bits):
        arrived = swap(running, "inner", 1 << bit)
        if bit == 2:
            arrived, others, local[0] = tie((arrived, others, local[0]))
        buckets.append(arrived)
        running = running + arrived
    sent = swap(jnp.stack(buckets[1:]), "inner", 2)

    far = [swap(running, "outer", 1)]
    beside = []
    for bit in range(1, outer_bits):
        running = running + far[-1]
        running, inputs = tie((running, inputs))
        far.append(swap(running, "outer", 1 << bit))
        beside.append(swap(far[-2], "inner", 2))
        if bit == 1:
            local.append(local_part(1 - core, *inputs))
            far[-1], beside, sent, others, local[1] = tie((far[-1], beside, sent, others, local[1]))
    if len(local) < 2:
        local.append(local_part(1 - core, *inputs))
        far[-1], sent, others, local[1] = tie((far[-1], sent, others, local[1]))
    late = swap(far[-1], "inner", 2)
    others += [sent[at] for at in range(inner_bits - 2)]
    pairs = [(keep_ours, keep_theirs), *zip(buckets, others), *zip(far, beside)]
    mine = jnp.stack([part for pair in pairs for part in pair] + far[-1:])
    other = swap(mine, "inner", 1)
    nears = [
        near_part(core, place, inner_bits, queries, level_weights, local[0], mine, first),
        near_part(1 - core, place, inner_bits, queries, level_weights, local[1], other),
    ]
    late, nears = tie((late, nears))
    late_other = swap(late, "inner", 1)
    first_level = LOCAL_BITS + 1 + inner_bits
    return far_part(
        first_level, outer_bits, place, queries, level_weights, *nears, mine, other, late, late_other, out_weight
    )


def solution(mesh):
    spec = P(("outer", "inner"), None)
    in_specs = (spec, spec, spec, P(None, None, ("outer", "inner")), P())
    return jax.shard_map(body, mesh=mesh, in_specs=in_specs, out_specs=spec, check_vma=False)
```

```python
import functools

import jax
import jax.numpy as jnp
from jax import lax
from jax.experimental import pallas as pl
from jax.experimental.pallas import tpu as pltpu
from jax.sharding import PartitionSpec as P

HEADS = 8
HEAD = 128
LOCAL_BITS = 10
TILE = 128
CHUNK = 256
F32 = jnp.float32
BF16 = jnp.bfloat16
MIB = 1 << 20


def bits_of(count):
    return count.bit_length() - 1


def swap(block, axis, stride):
    count = lax.axis_size(axis)
    return lax.ppermute(block, axis, [(place, place ^ stride) for place in range(count)])


def raise_to(block, axis, stride):
    count = lax.axis_size(axis)
    route = [(place, place | stride) for place in range(count) if not place & stride]
    return lax.ppermute(block, axis, route)


def cost(flops, moved):
    return pl.CostEstimate(flops=flops, bytes_accessed=moved, transcendentals=0)


def params(limit):
    return pltpu.CompilerParams(vmem_limit_bytes=limit * MIB)


def outside(*parts):
    return tuple(pltpu.with_memory_space_constraint(part, pltpu.HBM) for part in parts)


def inside(*parts):
    return tuple(pltpu.with_memory_space_constraint(part, pltpu.VMEM) for part in parts)


def product(left, right):
    return jnp.dot(left, right, preferred_element_type=F32)


def product_nt(left, right):
    return lax.dot_general(left, right, (((1,), (1,)), ((), ())), preferred_element_type=F32)


def identity(size):
    row = lax.broadcasted_iota(jnp.int32, (size, size), 0)
    column = lax.broadcasted_iota(jnp.int32, (size, size), 1)
    return (row == column).astype(F32).astype(BF16)


def turned(block):
    return product_nt(identity(block.shape[1]), block).astype(BF16)


def state_kernel(place, keys, values, state):
    both = product(turned(values[...]), keys[...])
    for low in range(0, keys.shape[1], HEAD):
        part = slice(low, low + HEAD)
        state[part, :] = both[part, part]


def block_state(place, share, keys, values):
    tokens, width = keys.shape
    step = 2 * HEAD
    steps = width // share // step
    column = pl.BlockSpec((tokens, step), lambda pair, place: (0, place[0] * steps + pair))
    return pl.pallas_call(
        state_kernel,
        grid_spec=pltpu.PrefetchScalarGridSpec(
            num_scalar_prefetch=1,
            grid=(steps,),
            in_specs=[column, column],
            out_specs=pl.BlockSpec((step, HEAD), lambda pair, place: (pair, 0)),
        ),
        out_shape=pltpu.VMEM((width // share, HEAD), F32),
        cost_estimate=cost(2 * tokens * width * HEAD // share, 5 * MIB // share),
        compiler_params=params(16),
    )(place.reshape(1).astype(jnp.int32), keys, values)


def tile_mixing(rows):
    target = lax.broadcasted_iota(jnp.int32, (8, TILE), 1)
    source = lax.broadcasted_iota(jnp.int32, (8, TILE), 0)
    rows = [jnp.broadcast_to(row, (8, TILE)) for row in rows]
    within = jnp.bitwise_and(target, 7)
    differ = jnp.bitwise_xor(within, source)
    base = rows[3]
    for level in (2, 1, 0):
        base = jnp.where(differ < 1 << level, rows[level], base)
    parts = [jnp.where(source <= within, base, 0.0)]
    for bit in range(3, bits_of(TILE)):
        upper = jnp.bitwise_and(jnp.right_shift(target, bit), 1) == 1
        parts = [jnp.where(upper, rows[bit + 1], part) for part in parts] + [
            jnp.where(upper, part, 0.0) for part in parts
        ]
    return jnp.concatenate(parts, axis=0)


def local_kernel(half, queries, keys, values, weights, local, rows):
    tokens, width = queries.shape
    chunks = tokens // CHUNK
    levels = rows.shape[1]
    top = bits_of(CHUNK)
    spans = [slice(low, low + CHUNK) for low in range(0, tokens, CHUNK)]
    parts = [slice(low, low + HEAD) for low in range(0, width, HEAD)]
    first = (half[0] * pl.num_programs(0) + pl.program_id(0)) * len(parts)
    for at in range(len(parts)):
        rows[at] = weights[:, pl.ds(first + at, 1), :].reshape(levels, tokens)
    flipped = turned(values[...])

    def row(at, level, low, size):
        return rows[at, level : level + 1, low : low + size]

    nodes = []
    for part in parts:
        line = [product(flipped[part, span], keys[span, part]) for span in spans[:-1]]
        known = [line]
        while len(known[-1]) > 1:
            below = known[-1]
            known.append([below[at] + below[at + 1] for at in range(0, len(below) - 1, 2)])
        nodes.append([[state.astype(BF16) for state in level] for level in known])
    scores = {}
    for at, part in enumerate(parts):
        for chunk, span in enumerate(spans):
            used = [bit for bit in range(bits_of(chunks)) if chunk >> bit & 1]
            left = [keys[span, part]] + [nodes[at][bit][(chunk >> bit) - 1] for bit in used]
            left = jnp.concatenate(left, axis=0) if used else left[0]
            scores[at, chunk] = product_nt(left, queries[span, part])
    for at, part in enumerate(parts):
        for chunk, span in enumerate(spans):
            low = chunk * CHUNK
            score = scores[at, chunk]
            lower, upper = (
                tile_mixing([row(at, level, start, TILE) for level in range(top)]) for start in (low, low + TILE)
            )
            across = row(at, top, low + TILE, TILE)
            weighted = jnp.concatenate(
                [
                    jnp.concatenate([score[:TILE, :TILE] * lower, score[:TILE, TILE:] * across], axis=1),
                    jnp.concatenate([jnp.zeros_like(lower), score[TILE:CHUNK, TILE:] * upper], axis=1),
                ],
                axis=0,
            ).astype(BF16)
            total = product(flipped[part, span], weighted)
            below = CHUNK
            for bit in range(bits_of(chunks)):
                if chunk >> bit & 1:
                    total = total + row(at, top + 1 + bit, low, CHUNK) * score[below : below + HEAD, :]
                    below += HEAD
            local[part, span] = total


def local_part(half, queries, keys, values, level_weights):
    tokens, width = queries.shape
    step = 2 * HEAD
    steps = width // step // 2
    column = pl.BlockSpec((tokens, step), lambda pair, half: (0, half[0] * steps + pair))
    return pl.pallas_call(
        local_kernel,
        grid_spec=pltpu.PrefetchScalarGridSpec(
            num_scalar_prefetch=1,
            grid=(steps,),
            in_specs=[column, column, column, pl.BlockSpec(level_weights.shape, lambda pair, half: (0, 0, 0))],
            out_specs=pl.BlockSpec((step, tokens), lambda pair, half: (pair, 0)),
            scratch_shapes=[pltpu.VMEM((2, level_weights.shape[0], tokens), F32)],
        ),
        out_shape=pltpu.VMEM((width // 2, tokens), F32),
        cost_estimate=cost(tokens * width, MIB // 4),
        compiler_params=params(16),
    )(half.reshape(1), queries, keys, values, level_weights)


def has_bit(place, bit):
    return jnp.bitwise_and(jnp.right_shift(place, bit), 1) == 1


def near_kernel(half, place, queries, weights, local, *rest):
    *held, near, states, rows = rest
    step = pl.program_id(0)
    bits = states.shape[1] // HEAD
    size = states.shape[0] * HEAD // 2

    def quarter_state(bit, quarter, slot):
        if len(held) == 1:
            return held[0][2 * bit + slot]
        if bit == 0:
            return held[0][quarter * size : (quarter + 1) * size, :]
        return jnp.where(slot == 0, held[2 * bit - 1][...], held[2 * bit][...])

    @pl.when(step == 0)
    def _():
        side = jnp.bitwise_and(jnp.right_shift(place[0], 1), 1)
        for quarter in range(2):
            slot = jnp.bitwise_xor(side, quarter)
            for bit in range(bits):
                state = jnp.where(has_bit(place[0], bit), quarter_state(bit, quarter, slot), 0.0).astype(BF16)
                for at in range(0, size, HEAD):
                    states[(quarter * size + at) // HEAD, bit * HEAD : (bit + 1) * HEAD, :] = state[at : at + HEAD]

    for at in range(rows.shape[0]):
        part = slice(at * HEAD, (at + 1) * HEAD)
        head = step * rows.shape[0] + at
        rows[at] = weights[:, pl.ds(half[0] * states.shape[0] + head, 1), :].reshape(rows.shape[1:])
        products = product_nt(states[head], queries[:, part])
        total = local[part, :]
        for bit in range(bits):
            level = LOCAL_BITS + 1 + bit
            total = total + rows[at, level : level + 1, :] * products[bit * HEAD : (bit + 1) * HEAD]
        near[part, :] = total


def near_part(half, place, bits, queries, level_weights, local, *held):
    tokens, width = queries.shape
    heads = width // HEAD // 2
    step = 2 * HEAD
    steps = width // step // 2
    return pl.pallas_call(
        near_kernel,
        grid_spec=pltpu.PrefetchScalarGridSpec(
            num_scalar_prefetch=2,
            grid=(steps,),
            in_specs=[
                pl.BlockSpec((tokens, step), lambda pair, half, place: (0, half[0] * steps + pair)),
                pl.BlockSpec(level_weights.shape, lambda pair, half, place: (0, 0, 0)),
                pl.BlockSpec((step, tokens), lambda pair, half, place: (pair, 0)),
                *[
                    pl.BlockSpec(
                        (2 * bits,) + part.shape[1:] if part.ndim == 3 else part.shape,
                        lambda pair, half, place, rank=part.ndim: (0,) * rank,
                    )
                    for part in held
                ],
            ],
            out_specs=pl.BlockSpec((step, tokens), lambda pair, half, place: (pair, 0)),
            scratch_shapes=[
                pltpu.VMEM((heads, bits * HEAD, HEAD), BF16),
                pltpu.VMEM((2, level_weights.shape[0], tokens), F32),
            ],
        ),
        out_shape=pltpu.VMEM((width // 2, tokens), F32),
        cost_estimate=cost(tokens * width, MIB // 4),
        compiler_params=params(16),
    )(half.reshape(1), place, queries, level_weights, local, *held)


def far_kernel(first_level, place, queries, weights, near_mine, near_other, early, early_other, late, late_other,
               out_weight, mixed, states, flipped, attended):
    rows, width = attended.shape
    bits = states.shape[1] // HEAD
    size = late.shape[0]
    skip = early.shape[0] + 1 - 2 * bits
    core = jnp.bitwise_and(place[0], 1)

    @pl.when(pl.program_id(0) == 0)
    def _():
        side = jnp.bitwise_and(jnp.right_shift(place[0], 1), 1)
        for bit in range(bits):
            mine, other = ([part[skip + 2 * bit], part[skip + 2 * bit + 1] if bit + 1 < bits else final[...]]
                           for part, final in ((early, late), (early_other, late_other)))
            for quarter in range(4):
                here, there = (jnp.where(side == quarter % 2, *part) for part in (mine, other))
                state = jnp.where(core == quarter // 2, here, there)
                state = jnp.where(has_bit(place[1], bit), state, 0.0).astype(BF16)
                for at in range(0, size, HEAD):
                    head = (quarter * size + at) // HEAD
                    states[head, bit * HEAD : (bit + 1) * HEAD, :] = state[at : at + HEAD]

    for half in range(2):
        for low in range(0, width // 2, HEAD):
            part = slice(half * (width // 2) + low, half * (width // 2) + low + HEAD)
            head = part.start // HEAD
            products = product_nt(states[head], queries[:, part])
            span = slice(low, low + HEAD)
            total = jnp.where(core == half, near_mine[span, :], near_other[span, :])
            for bit in range(bits):
                row = weights[first_level + bit, head : head + 1, :]
                total = total + row * products[bit * HEAD : (bit + 1) * HEAD]
            flipped[part, :] = total.astype(BF16)
    unit = identity(CHUNK)
    for top in range(0, rows, CHUNK):
        for low in range(0, width, CHUNK):
            block = flipped[low : low + CHUNK, top : top + CHUNK]
            attended[top : top + CHUNK, low : low + CHUNK] = product_nt(unit, block).astype(BF16)
    mixed[...] = product(attended[...], out_weight[...]).astype(BF16)


def far_part(first_level, bits, place, queries, level_weights, near_mine, near_other, *fixed):
    tokens, width = queries.shape
    rows = min(2 * CHUNK, tokens)
    band = pl.BlockSpec((rows, width), lambda step: (step, 0))
    near = pl.BlockSpec((width // 2, rows), lambda step: (0, step))
    return pl.pallas_call(
        functools.partial(far_kernel, first_level),
        grid=(tokens // rows,),
        in_specs=[
            pl.BlockSpec(memory_space=pltpu.SMEM),
            band,
            pl.BlockSpec(level_weights.shape[:2] + (rows,), lambda step: (0, 0, step)),
            near,
            near,
            *[pl.BlockSpec(part.shape, lambda step, rank=part.ndim: (0,) * rank) for part in fixed],
        ],
        out_specs=band,
        out_shape=jax.ShapeDtypeStruct((tokens, width), BF16),
        scratch_shapes=[
            pltpu.VMEM((width // HEAD, bits * HEAD, HEAD), BF16),
            pltpu.VMEM((width, rows), BF16),
            pltpu.VMEM((rows, width), BF16),
        ],
        cost_estimate=cost(2 * tokens * width * (width + bits * HEAD), 12 * MIB),
        compiler_params=params(28),
    )(place, queries, level_weights, near_mine, near_other, *fixed)


def body(queries, keys, values, level_weights, out_weight):
    inner, outer = lax.axis_size("inner"), lax.axis_size("outer")
    inner_bits, outer_bits = bits_of(inner), bits_of(outer)
    inner_place, outer_place = lax.axis_index("inner"), lax.axis_index("outer")
    place = jnp.stack([inner_place, outer_place]).astype(jnp.int32)
    core = jnp.bitwise_and(inner_place, 1).astype(jnp.int32)
    side = jnp.bitwise_and(jnp.right_shift(inner_place, 1), 1)
    half = keys.shape[1] // 2
    quarter = half // 2
    tie = lax.optimization_barrier

    inputs = outside(keys, values)
    give = block_state(1 - core, 2, *inputs)
    give, inputs = tie((give, inputs))
    first = swap(give, "inner", 1)

    def quarter_of(at, state):
        return state + lax.dynamic_slice_in_dim(first, at * quarter, quarter, 0)

    keep_theirs = block_state(2 * core + 1 - side, 4, *inputs)
    passed = quarter_of(1 - side, keep_theirs)
    passed, inputs = tie((passed, inputs))
    buckets = [swap(passed, "inner", 2)]
    keep_ours = block_state(2 * core + side, 4, *inputs)
    inputs = inside(queries, keys, values, level_weights)
    own = quarter_of(side, keep_ours)
    others = [swap(own, "inner", 2)]
    running = own + buckets[0]
    running, inputs = tie((running, inputs))
    local = [local_part(core, *inputs)]
    for bit in range(2, inner_bits):
        arrived = swap(running, "inner", 1 << bit)
        if bit == 2:
            arrived, others, local[0] = tie((arrived, others, local[0]))
        buckets.append(arrived)
        running = running + arrived
    sent = swap(jnp.stack(buckets[1:]), "inner", 2)

    pairs = [(keep_ours, keep_theirs)]

    def own_near(local):
        nonlocal sent, others
        sent, others, local[:] = tie((sent, others, local))
        pairs.extend(zip(buckets, others + [sent[at] for at in range(inner_bits - 2)]))
        held = [part for pair in pairs[1:] for part in pair]
        return near_part(core, place, inner_bits, inputs[0], inputs[3], local[0], first, *held)

    far = [swap(running, "outer", 1)]
    beside = []
    for bit in range(1, outer_bits):
        running = running + far[-1]
        running, inputs = tie((running, inputs))
        far.append(swap(running, "outer", 1 << bit))
        beside.append(swap(far[-2], "inner", 2))
        if bit == 1:
            local.append(local_part(1 - core, *inputs))
            near_mine = own_near(local)
            far[-1], beside, near_mine, local[1], pairs = tie((far[-1], beside, near_mine, local[1], pairs))
    if len(local) < 2:
        local.append(local_part(1 - core, *inputs))
        near_mine = own_near(local)
        far[-1], near_mine, local[1], pairs = tie((far[-1], near_mine, local[1], pairs))
    late = swap(far[-1], "inner", 2)
    pairs += zip(far, beside)
    mine = jnp.stack([part for pair in pairs for part in pair] + far[-1:])
    other = swap(mine, "inner", 1)
    nears = [near_mine, near_part(1 - core, place, inner_bits, inputs[0], inputs[3], local[1], other)]
    late, nears = tie((late, nears))
    late_other = swap(late, "inner", 1)
    first_level = LOCAL_BITS + 1 + inner_bits
    return far_part(
        first_level, outer_bits, place, queries, level_weights, *nears, mine, other, late, late_other, out_weight
    )


def solution(mesh):
    spec = P(("outer", "inner"), None)
    in_specs = (spec, spec, spec, P(None, None, ("outer", "inner")), P())
    return jax.shard_map(body, mesh=mesh, in_specs=in_specs, out_specs=spec, check_vma=False)
```

```python
import functools

import jax
import jax.numpy as jnp
from jax import lax
from jax.experimental import pallas as pl
from jax.experimental.pallas import tpu as pltpu
from jax.sharding import PartitionSpec as P

HEADS = 8
HEAD = 128
LOCAL_BITS = 10
TILE = 128
CHUNK = 256
F32 = jnp.float32
BF16 = jnp.bfloat16
MIB = 1 << 20


def bits_of(count):
    return count.bit_length() - 1


def swap(block, axis, stride):
    count = lax.axis_size(axis)
    return lax.ppermute(block, axis, [(place, place ^ stride) for place in range(count)])


def raise_to(block, axis, stride):
    count = lax.axis_size(axis)
    route = [(place, place | stride) for place in range(count) if not place & stride]
    return lax.ppermute(block, axis, route)


def cost(flops, moved):
    return pl.CostEstimate(flops=flops, bytes_accessed=moved, transcendentals=0)


def params(limit):
    return pltpu.CompilerParams(vmem_limit_bytes=limit * MIB)


def outside(*parts):
    return tuple(pltpu.with_memory_space_constraint(part, pltpu.HBM) for part in parts)


def product(left, right):
    return jnp.dot(left, right, preferred_element_type=F32)


def product_nt(left, right):
    return lax.dot_general(left, right, (((1,), (1,)), ((), ())), preferred_element_type=F32)


def identity(size):
    row = lax.broadcasted_iota(jnp.int32, (size, size), 0)
    column = lax.broadcasted_iota(jnp.int32, (size, size), 1)
    return (row == column).astype(F32).astype(BF16)


def turned(block):
    return product_nt(identity(block.shape[1]), block).astype(BF16)


def state_kernel(place, keys, values, state):
    both = product(turned(values[...]), keys[...])
    for low in range(0, keys.shape[1], HEAD):
        part = slice(low, low + HEAD)
        state[part, :] = both[part, part]


def block_state(place, share, keys, values):
    tokens, width = keys.shape
    step = 2 * HEAD
    steps = width // share // step
    column = pl.BlockSpec((tokens, step), lambda pair, place: (0, place[0] * steps + pair))
    return pl.pallas_call(
        state_kernel,
        grid_spec=pltpu.PrefetchScalarGridSpec(
            num_scalar_prefetch=1,
            grid=(steps,),
            in_specs=[column, column],
            out_specs=pl.BlockSpec((step, HEAD), lambda pair, place: (pair, 0)),
        ),
        out_shape=pltpu.VMEM((width // share, HEAD), F32),
        cost_estimate=cost(2 * tokens * width * HEAD // share, 5 * MIB // share),
        compiler_params=params(16),
    )(place.reshape(1).astype(jnp.int32), keys, values)


def tile_mixing(rows):
    target = lax.broadcasted_iota(jnp.int32, (8, TILE), 1)
    source = lax.broadcasted_iota(jnp.int32, (8, TILE), 0)
    rows = [jnp.broadcast_to(row, (8, TILE)) for row in rows]
    within = jnp.bitwise_and(target, 7)
    differ = jnp.bitwise_xor(within, source)
    base = rows[3]
    for level in (2, 1, 0):
        base = jnp.where(differ < 1 << level, rows[level], base)
    parts = [jnp.where(source <= within, base, 0.0)]
    for bit in range(3, bits_of(TILE)):
        upper = jnp.bitwise_and(jnp.right_shift(target, bit), 1) == 1
        parts = [jnp.where(upper, rows[bit + 1], part) for part in parts] + [
            jnp.where(upper, part, 0.0) for part in parts
        ]
    return jnp.concatenate(parts, axis=0)


def local_kernel(half, queries, keys, values, weights, local, rows):
    tokens, width = queries.shape
    chunks = tokens // CHUNK
    levels = rows.shape[1]
    top = bits_of(CHUNK)
    spans = [slice(low, low + CHUNK) for low in range(0, tokens, CHUNK)]
    parts = [slice(low, low + HEAD) for low in range(0, width, HEAD)]
    first = (half[0] * pl.num_programs(0) + pl.program_id(0)) * len(parts)
    for at in range(len(parts)):
        rows[at] = weights[:, pl.ds(first + at, 1), :].reshape(levels, tokens)
    flipped = turned(values[...])

    def row(at, level, low, size):
        return rows[at, level : level + 1, low : low + size]

    nodes = []
    for part in parts:
        line = [product(flipped[part, span], keys[span, part]) for span in spans[:-1]]
        known = [line]
        while len(known[-1]) > 1:
            below = known[-1]
            known.append([below[at] + below[at + 1] for at in range(0, len(below) - 1, 2)])
        nodes.append([[state.astype(BF16) for state in level] for level in known])
    scores = {}
    for at, part in enumerate(parts):
        for chunk, span in enumerate(spans):
            used = [bit for bit in range(bits_of(chunks)) if chunk >> bit & 1]
            left = [keys[span, part]] + [nodes[at][bit][(chunk >> bit) - 1] for bit in used]
            left = jnp.concatenate(left, axis=0) if used else left[0]
            scores[at, chunk] = product_nt(left, queries[span, part])
    for at, part in enumerate(parts):
        for chunk, span in enumerate(spans):
            low = chunk * CHUNK
            score = scores[at, chunk]
            lower, upper = (
                tile_mixing([row(at, level, start, TILE) for level in range(top)]) for start in (low, low + TILE)
            )
            across = row(at, top, low + TILE, TILE)
            weighted = jnp.concatenate(
                [
                    jnp.concatenate([score[:TILE, :TILE] * lower, score[:TILE, TILE:] * across], axis=1),
                    jnp.concatenate([jnp.zeros_like(lower), score[TILE:CHUNK, TILE:] * upper], axis=1),
                ],
                axis=0,
            ).astype(BF16)
            total = product(flipped[part, span], weighted)
            below = CHUNK
            for bit in range(bits_of(chunks)):
                if chunk >> bit & 1:
                    total = total + row(at, top + 1 + bit, low, CHUNK) * score[below : below + HEAD, :]
                    below += HEAD
            local[part, span] = total.astype(BF16)


def local_part(half, queries, keys, values, level_weights):
    tokens, width = queries.shape
    step = 2 * HEAD
    steps = width // step // 2
    column = pl.BlockSpec((tokens, step), lambda pair, half: (0, half[0] * steps + pair))
    return pl.pallas_call(
        local_kernel,
        grid_spec=pltpu.PrefetchScalarGridSpec(
            num_scalar_prefetch=1,
            grid=(steps,),
            in_specs=[column, column, column, pl.BlockSpec(level_weights.shape, lambda pair, half: (0, 0, 0))],
            out_specs=pl.BlockSpec((step, tokens), lambda pair, half: (pair, 0)),
            scratch_shapes=[pltpu.VMEM((2, level_weights.shape[0], tokens), F32)],
        ),
        out_shape=pltpu.HBM((width // 2, tokens), BF16),
        cost_estimate=cost(tokens * width, MIB // 4),
        compiler_params=params(16),
    )(half.reshape(1), queries, keys, values, level_weights)


def has_bit(place, bit):
    return jnp.bitwise_and(jnp.right_shift(place, bit), 1) == 1


def near_kernel(half, place, queries, weights, local, held, *rest):
    *first, near, states, rows = rest
    step = pl.program_id(0)
    bits = states.shape[1] // HEAD
    size = held.shape[1]

    @pl.when(step == 0)
    def _():
        side = jnp.bitwise_and(jnp.right_shift(place[0], 1), 1)
        for quarter in range(2):
            slot = jnp.bitwise_xor(side, quarter)
            for bit in range(bits):
                if first and bit == 0:
                    state = first[0][quarter * size : (quarter + 1) * size, :]
                else:
                    state = held[2 * bit + slot]
                state = jnp.where(has_bit(place[0], bit), state, 0.0).astype(BF16)
                for at in range(0, size, HEAD):
                    states[(quarter * size + at) // HEAD, bit * HEAD : (bit + 1) * HEAD, :] = state[at : at + HEAD]

    for at in range(rows.shape[0]):
        part = slice(at * HEAD, (at + 1) * HEAD)
        head = step * rows.shape[0] + at
        rows[at] = weights[:, pl.ds(half[0] * states.shape[0] + head, 1), :].reshape(rows.shape[1:])
        products = product_nt(states[head], queries[:, part])
        total = local[part, :].astype(F32)
        for bit in range(bits):
            level = LOCAL_BITS + 1 + bit
            total = total + rows[at, level : level + 1, :] * products[bit * HEAD : (bit + 1) * HEAD]
        near[part, :] = total.astype(BF16)


def near_part(half, place, bits, queries, level_weights, local, held, *first):
    tokens, width = queries.shape
    heads = width // HEAD // 2
    step = 2 * HEAD
    steps = width // step // 2
    return pl.pallas_call(
        near_kernel,
        grid_spec=pltpu.PrefetchScalarGridSpec(
            num_scalar_prefetch=2,
            grid=(steps,),
            in_specs=[
                pl.BlockSpec((tokens, step), lambda pair, half, place: (0, half[0] * steps + pair)),
                pl.BlockSpec(level_weights.shape, lambda pair, half, place: (0, 0, 0)),
                pl.BlockSpec((step, tokens), lambda pair, half, place: (pair, 0)),
                pl.BlockSpec((2 * bits,) + held.shape[1:], lambda pair, half, place: (0, 0, 0)),
                *[pl.BlockSpec(part.shape, lambda pair, half, place: (0, 0)) for part in first],
            ],
            out_specs=pl.BlockSpec((step, tokens), lambda pair, half, place: (pair, 0)),
            scratch_shapes=[
                pltpu.VMEM((heads, bits * HEAD, HEAD), BF16),
                pltpu.VMEM((2, level_weights.shape[0], tokens), F32),
            ],
        ),
        out_shape=jax.ShapeDtypeStruct((width // 2, tokens), BF16),
        cost_estimate=cost(tokens * width, MIB // 4),
        compiler_params=params(16),
    )(half.reshape(1), place, queries, level_weights, *outside(local), held, *first)


def far_kernel(first_level, place, queries, weights, near_mine, near_other, early, early_other, late, late_other,
               out_weight, mixed, states, flipped, attended, projection, ready):
    rows, width = attended.shape
    bits = states.shape[1] // HEAD
    size = late.shape[0]
    skip = early.shape[0] + 1 - 2 * bits
    core = jnp.bitwise_and(place[0], 1)
    fetch = pltpu.make_async_copy(out_weight, projection, ready)

    @pl.when(pl.program_id(0) == 0)
    def _():
        fetch.start()
        side = jnp.bitwise_and(jnp.right_shift(place[0], 1), 1)
        for bit in range(bits):
            mine, other = ([part[skip + 2 * bit], part[skip + 2 * bit + 1] if bit + 1 < bits else final[...]]
                           for part, final in ((early, late), (early_other, late_other)))
            for quarter in range(4):
                here, there = (jnp.where(side == quarter % 2, *part) for part in (mine, other))
                state = jnp.where(core == quarter // 2, here, there)
                state = jnp.where(has_bit(place[1], bit), state, 0.0).astype(BF16)
                for at in range(0, size, HEAD):
                    head = (quarter * size + at) // HEAD
                    states[head, bit * HEAD : (bit + 1) * HEAD, :] = state[at : at + HEAD]

    for half in range(2):
        for low in range(0, width // 2, HEAD):
            part = slice(half * (width // 2) + low, half * (width // 2) + low + HEAD)
            head = part.start // HEAD
            products = product_nt(states[head], queries[:, part])
            span = slice(low, low + HEAD)
            total = jnp.where(core == half, near_mine[span, :], near_other[span, :]).astype(F32)
            for bit in range(bits):
                row = weights[first_level + bit, head : head + 1, :]
                total = total + row * products[bit * HEAD : (bit + 1) * HEAD]
            flipped[part, :] = total.astype(BF16)
    unit = identity(CHUNK)
    for top in range(0, rows, CHUNK):
        for low in range(0, width, CHUNK):
            block = flipped[low : low + CHUNK, top : top + CHUNK]
            attended[top : top + CHUNK, low : low + CHUNK] = product_nt(unit, block).astype(BF16)

    @pl.when(pl.program_id(0) == 0)
    def _():
        fetch.wait()

    mixed[...] = product(attended[...], projection[...]).astype(BF16)


def far_part(first_level, bits, place, queries, level_weights, near_mine, near_other, *rest):
    *fixed, out_weight = rest
    tokens, width = queries.shape
    rows = min(2 * CHUNK, tokens)
    band = pl.BlockSpec((rows, width), lambda step: (step, 0))
    near = pl.BlockSpec((width // 2, rows), lambda step: (0, step))

    def tail(part):
        count = 2 * bits - 1
        if part.ndim == 3 and part.shape[0] % count == 0:
            last = part.shape[0] // count - 1
            return pl.BlockSpec((count,) + part.shape[1:], lambda step: (last, 0, 0))
        return pl.BlockSpec(part.shape, lambda step: (0,) * part.ndim)

    return pl.pallas_call(
        functools.partial(far_kernel, first_level),
        grid=(tokens // rows,),
        in_specs=[
            pl.BlockSpec(memory_space=pltpu.SMEM),
            band,
            pl.BlockSpec(level_weights.shape[:2] + (rows,), lambda step: (0, 0, step)),
            near,
            near,
            *[tail(part) for part in fixed],
            pl.BlockSpec(memory_space=pl.ANY),
        ],
        out_specs=band,
        out_shape=jax.ShapeDtypeStruct((tokens, width), BF16),
        scratch_shapes=[
            pltpu.VMEM((width // HEAD, bits * HEAD, HEAD), BF16),
            pltpu.VMEM((width, rows), BF16),
            pltpu.VMEM((rows, width), BF16),
            pltpu.VMEM(out_weight.shape, BF16),
            pltpu.SemaphoreType.DMA,
        ],
        cost_estimate=cost(2 * tokens * width * (width + bits * HEAD), 12 * MIB),
        compiler_params=params(28),
    )(place, queries, level_weights, near_mine, near_other, *fixed, *outside(out_weight))


def body(queries, keys, values, level_weights, out_weight):
    inner, outer = lax.axis_size("inner"), lax.axis_size("outer")
    inner_bits, outer_bits = bits_of(inner), bits_of(outer)
    inner_place, outer_place = lax.axis_index("inner"), lax.axis_index("outer")
    place = jnp.stack([inner_place, outer_place]).astype(jnp.int32)
    core = jnp.bitwise_and(inner_place, 1).astype(jnp.int32)
    side = jnp.bitwise_and(jnp.right_shift(inner_place, 1), 1)
    half = keys.shape[1] // 2
    quarter = half // 2
    tie = lax.optimization_barrier

    inputs = outside(keys, values)
    give = block_state(1 - core, 2, *inputs)
    give, inputs = tie((give, inputs))
    first = swap(give, "inner", 1)

    def quarter_of(at, state):
        return state + lax.dynamic_slice_in_dim(first, at * quarter, quarter, 0)

    keep_theirs = block_state(2 * core + 1 - side, 4, *inputs)
    passed = quarter_of(1 - side, keep_theirs)
    passed, inputs = tie((passed, inputs))
    buckets = [swap(passed, "inner", 2)]
    keep_ours = block_state(2 * core + side, 4, *inputs)
    inputs = (queries, keys, values, level_weights)
    own = quarter_of(side, keep_ours)
    others = [swap(own, "inner", 2)]
    running = own + buckets[0]
    running, inputs = tie((running, inputs))
    local = [local_part(core, *inputs)]
    for bit in range(2, inner_bits):
        arrived = swap(running, "inner", 1 << bit)
        if bit == 2:
            arrived, others, local[0] = tie((arrived, others, local[0]))
        buckets.append(arrived)
        running = running + arrived
    sent = swap(jnp.stack(buckets[1:]), "inner", 2)

    far = [swap(running, "outer", 1)]
    beside = []
    for bit in range(1, outer_bits):
        running = running + far[-1]
        running, inputs = tie((running, inputs))
        far.append(swap(running, "outer", 1 << bit))
        beside.append(swap(far[-2], "inner", 2))
        if bit == 1:
            local.append(local_part(1 - core, *inputs))
            far[-1], beside, sent, others, local[1] = tie((far[-1], beside, sent, others, local[1]))
    if len(local) < 2:
        local.append(local_part(1 - core, *inputs))
        far[-1], sent, others, local[1] = tie((far[-1], sent, others, local[1]))
    late = swap(far[-1], "inner", 2)
    others += [sent[at] for at in range(inner_bits - 2)]
    pairs = [(keep_ours, keep_theirs), *zip(buckets, others), *zip(far, beside)]
    mine = jnp.stack([part for pair in pairs for part in pair] + far[-1:])
    other = swap(mine, "inner", 1)
    nears = [
        near_part(core, place, inner_bits, inputs[0], inputs[3], local[0], mine, first),
        near_part(1 - core, place, inner_bits, inputs[0], inputs[3], local[1], other),
    ]
    late, nears = tie((late, nears))
    late_other = swap(late, "inner", 1)
    first_level = LOCAL_BITS + 1 + inner_bits
    return far_part(
        first_level, outer_bits, place, queries, level_weights, *nears, mine, other, late, late_other, out_weight
    )


def solution(mesh):
    spec = P(("outer", "inner"), None)
    in_specs = (spec, spec, spec, P(None, None, ("outer", "inner")), P())
    return jax.shard_map(body, mesh=mesh, in_specs=in_specs, out_specs=spec, check_vma=False)
```

```python
import functools

import jax
import jax.numpy as jnp
from jax import lax
from jax.experimental import pallas as pl
from jax.experimental.pallas import tpu as pltpu
from jax.sharding import PartitionSpec as P

HEADS = 8
HEAD = 128
LOCAL_BITS = 10
TILE = 128
CHUNK = 256
F32 = jnp.float32
BF16 = jnp.bfloat16
MIB = 1 << 20


def bits_of(count):
    return count.bit_length() - 1


def swap(block, axis, stride):
    count = lax.axis_size(axis)
    return lax.ppermute(block, axis, [(place, place ^ stride) for place in range(count)])


def raise_to(block, axis, stride):
    count = lax.axis_size(axis)
    route = [(place, place | stride) for place in range(count) if not place & stride]
    return lax.ppermute(block, axis, route)


def cost(flops, moved):
    return pl.CostEstimate(flops=flops, bytes_accessed=moved, transcendentals=0)


def params(limit):
    return pltpu.CompilerParams(vmem_limit_bytes=limit * MIB)


def outside(*parts):
    return tuple(pltpu.with_memory_space_constraint(part, pltpu.HBM) for part in parts)


def product(left, right):
    return jnp.dot(left, right, preferred_element_type=F32)


def product_nt(left, right):
    return lax.dot_general(left, right, (((1,), (1,)), ((), ())), preferred_element_type=F32)


def identity(size):
    row = lax.broadcasted_iota(jnp.int32, (size, size), 0)
    column = lax.broadcasted_iota(jnp.int32, (size, size), 1)
    return (row == column).astype(F32).astype(BF16)


def turned(block):
    return product_nt(identity(block.shape[1]), block).astype(BF16)


def state_kernel(place, keys, values, state):
    both = product(turned(values[...]), keys[...])
    for low in range(0, keys.shape[1], HEAD):
        part = slice(low, low + HEAD)
        state[part, :] = both[part, part]


def block_state(place, share, keys, values):
    tokens, width = keys.shape
    step = 2 * HEAD
    steps = width // share // step
    column = pl.BlockSpec((tokens, step), lambda pair, place: (0, place[0] * steps + pair))
    return pl.pallas_call(
        state_kernel,
        grid_spec=pltpu.PrefetchScalarGridSpec(
            num_scalar_prefetch=1,
            grid=(steps,),
            in_specs=[column, column],
            out_specs=pl.BlockSpec((step, HEAD), lambda pair, place: (pair, 0)),
        ),
        out_shape=pltpu.VMEM((width // share, HEAD), F32),
        cost_estimate=cost(2 * tokens * width * HEAD // share, 5 * MIB // share),
        compiler_params=params(16),
    )(place.reshape(1).astype(jnp.int32), keys, values)


def tile_mixing(rows):
    target = lax.broadcasted_iota(jnp.int32, (8, TILE), 1)
    source = lax.broadcasted_iota(jnp.int32, (8, TILE), 0)
    rows = [jnp.broadcast_to(row, (8, TILE)) for row in rows]
    within = jnp.bitwise_and(target, 7)
    differ = jnp.bitwise_xor(within, source)
    base = rows[3]
    for level in (2, 1, 0):
        base = jnp.where(differ < 1 << level, rows[level], base)
    parts = [jnp.where(source <= within, base, 0.0)]
    for bit in range(3, bits_of(TILE)):
        upper = jnp.bitwise_and(jnp.right_shift(target, bit), 1) == 1
        parts = [jnp.where(upper, rows[bit + 1], part) for part in parts] + [
            jnp.where(upper, part, 0.0) for part in parts
        ]
    return jnp.concatenate(parts, axis=0)


def local_kernel(half, queries, keys, values, weights, local, *rest):
    *state, rows = rest
    tokens, width = queries.shape
    chunks = tokens // CHUNK
    levels = rows.shape[1]
    top = bits_of(CHUNK)
    spans = [slice(low, low + CHUNK) for low in range(0, tokens, CHUNK)]
    parts = [slice(low, low + HEAD) for low in range(0, width, HEAD)]
    first = (half[0] * pl.num_programs(0) + pl.program_id(0)) * len(parts)
    for at in range(len(parts)):
        rows[at] = weights[:, pl.ds(first + at, 1), :].reshape(levels, tokens)
    flipped = turned(values[...])

    def row(at, level, low, size):
        return rows[at, level : level + 1, low : low + size]

    nodes = []
    for part in parts:
        line = [product(flipped[part, span], keys[span, part]) for span in (spans if state else spans[:-1])]
        if state:
            state[0][part, :] = functools.reduce(jnp.add, line)
        known = [line]
        while len(known[-1]) > 1:
            below = known[-1]
            known.append([below[at] + below[at + 1] for at in range(0, len(below) - 1, 2)])
        nodes.append([[state.astype(BF16) for state in level] for level in known])
    scores = {}
    for at, part in enumerate(parts):
        for chunk, span in enumerate(spans):
            used = [bit for bit in range(bits_of(chunks)) if chunk >> bit & 1]
            left = [keys[span, part]] + [nodes[at][bit][(chunk >> bit) - 1] for bit in used]
            left = jnp.concatenate(left, axis=0) if used else left[0]
            scores[at, chunk] = product_nt(left, queries[span, part])
    for at, part in enumerate(parts):
        for chunk, span in enumerate(spans):
            low = chunk * CHUNK
            score = scores[at, chunk]
            lower, upper = (
                tile_mixing([row(at, level, start, TILE) for level in range(top)]) for start in (low, low + TILE)
            )
            across = row(at, top, low + TILE, TILE)
            weighted = jnp.concatenate(
                [
                    jnp.concatenate([score[:TILE, :TILE] * lower, score[:TILE, TILE:] * across], axis=1),
                    jnp.concatenate([jnp.zeros_like(lower), score[TILE:CHUNK, TILE:] * upper], axis=1),
                ],
                axis=0,
            ).astype(BF16)
            total = product(flipped[part, span], weighted)
            below = CHUNK
            for bit in range(bits_of(chunks)):
                if chunk >> bit & 1:
                    total = total + row(at, top + 1 + bit, low, CHUNK) * score[below : below + HEAD, :]
                    below += HEAD
            local[part, span] = total.astype(BF16)


def local_part(half, with_state, queries, keys, values, level_weights):
    tokens, width = queries.shape
    step = 2 * HEAD
    steps = width // step // 2
    column = pl.BlockSpec((tokens, step), lambda pair, half: (0, half[0] * steps + pair))
    return pl.pallas_call(
        local_kernel,
        grid_spec=pltpu.PrefetchScalarGridSpec(
            num_scalar_prefetch=1,
            grid=(steps,),
            in_specs=[column, column, column, pl.BlockSpec(level_weights.shape, lambda pair, half: (0, 0, 0))],
            out_specs=[
                pl.BlockSpec((step, tokens), lambda pair, half: (pair, 0)),
                pl.BlockSpec((step, HEAD), lambda pair, half: (pair, 0)),
            ][: 1 + with_state],
            scratch_shapes=[pltpu.VMEM((2, level_weights.shape[0], tokens), F32)],
        ),
        out_shape=[pltpu.HBM((width // 2, tokens), BF16), pltpu.VMEM((width // 2, HEAD), F32)][: 1 + with_state],
        cost_estimate=cost(tokens * width, MIB // 4),
        compiler_params=params(16),
    )(half.reshape(1), queries, keys, values, level_weights)


def has_bit(place, bit):
    return jnp.bitwise_and(jnp.right_shift(place, bit), 1) == 1


def near_kernel(half, place, queries, weights, local, *rest):
    *held, near, states, rows = rest
    step = pl.program_id(0)
    bits = states.shape[1] // HEAD
    size = states.shape[0] * HEAD // 2

    def quarter_state(bit, quarter, slot):
        if len(held) == 1:
            return held[0][2 * bit + slot]
        if bit == 0:
            return held[0][quarter * size : (quarter + 1) * size, :]
        return jnp.where(slot == 0, held[2 * bit - 1][...], held[2 * bit][...])

    @pl.when(step == 0)
    def _():
        side = jnp.bitwise_and(jnp.right_shift(place[0], 1), 1)
        for quarter in range(2):
            slot = jnp.bitwise_xor(side, quarter)
            for bit in range(bits):
                state = jnp.where(has_bit(place[0], bit), quarter_state(bit, quarter, slot), 0.0).astype(BF16)
                for at in range(0, size, HEAD):
                    states[(quarter * size + at) // HEAD, bit * HEAD : (bit + 1) * HEAD, :] = state[at : at + HEAD]

    for at in range(rows.shape[0]):
        part = slice(at * HEAD, (at + 1) * HEAD)
        head = step * rows.shape[0] + at
        rows[at] = weights[:, pl.ds(half[0] * states.shape[0] + head, 1), :].reshape(rows.shape[1:])
        products = product_nt(states[head], queries[:, part])
        total = local[part, :].astype(F32)
        for bit in range(bits):
            level = LOCAL_BITS + 1 + bit
            total = total + rows[at, level : level + 1, :] * products[bit * HEAD : (bit + 1) * HEAD]
        near[part, :] = total


def near_part(half, place, bits, queries, level_weights, local, *held):
    tokens, width = queries.shape
    heads = width // HEAD // 2
    step = 2 * HEAD
    steps = width // step // 2
    return pl.pallas_call(
        near_kernel,
        grid_spec=pltpu.PrefetchScalarGridSpec(
            num_scalar_prefetch=2,
            grid=(steps,),
            in_specs=[
                pl.BlockSpec((tokens, step), lambda pair, half, place: (0, half[0] * steps + pair)),
                pl.BlockSpec(level_weights.shape, lambda pair, half, place: (0, 0, 0)),
                pl.BlockSpec((step, tokens), lambda pair, half, place: (pair, 0)),
                *[
                    pl.BlockSpec(
                        (2 * bits,) + part.shape[1:] if part.ndim == 3 else part.shape,
                        lambda pair, half, place, rank=part.ndim: (0,) * rank,
                    )
                    for part in held
                ],
            ],
            out_specs=pl.BlockSpec((step, tokens), lambda pair, half, place: (pair, 0)),
            scratch_shapes=[
                pltpu.VMEM((heads, bits * HEAD, HEAD), BF16),
                pltpu.VMEM((2, level_weights.shape[0], tokens), F32),
            ],
        ),
        out_shape=pltpu.VMEM((width // 2, tokens), F32),
        cost_estimate=cost(tokens * width, MIB // 4),
        compiler_params=params(16),
    )(half.reshape(1), place, *outside(queries, level_weights, local), *held)


def far_kernel(first_level, place, queries, weights, near_mine, near_other, early, early_other, late, late_other,
               out_weight, mixed, states, flipped, attended):
    rows, width = attended.shape
    bits = states.shape[1] // HEAD
    size = late.shape[0]
    skip = early.shape[0] + 1 - 2 * bits
    core = jnp.bitwise_and(place[0], 1)

    @pl.when(pl.program_id(0) == 0)
    def _():
        side = jnp.bitwise_and(jnp.right_shift(place[0], 1), 1)
        for bit in range(bits):
            mine, other = ([part[skip + 2 * bit], part[skip + 2 * bit + 1] if bit + 1 < bits else final[...]]
                           for part, final in ((early, late), (early_other, late_other)))
            for quarter in range(4):
                here, there = (jnp.where(side == quarter % 2, *part) for part in (mine, other))
                state = jnp.where(core == quarter // 2, here, there)
                state = jnp.where(has_bit(place[1], bit), state, 0.0).astype(BF16)
                for at in range(0, size, HEAD):
                    head = (quarter * size + at) // HEAD
                    states[head, bit * HEAD : (bit + 1) * HEAD, :] = state[at : at + HEAD]

    for half in range(2):
        for low in range(0, width // 2, HEAD):
            part = slice(half * (width // 2) + low, half * (width // 2) + low + HEAD)
            head = part.start // HEAD
            products = product_nt(states[head], queries[:, part])
            span = slice(low, low + HEAD)
            total = jnp.where(core == half, near_mine[span, :], near_other[span, :])
            for bit in range(bits):
                row = weights[first_level + bit, head : head + 1, :]
                total = total + row * products[bit * HEAD : (bit + 1) * HEAD]
            flipped[part, :] = total.astype(BF16)
    unit = identity(CHUNK)
    for top in range(0, rows, CHUNK):
        for low in range(0, width, CHUNK):
            block = flipped[low : low + CHUNK, top : top + CHUNK]
            attended[top : top + CHUNK, low : low + CHUNK] = product_nt(unit, block).astype(BF16)
    mixed[...] = product(attended[...], out_weight[...]).astype(BF16)


def far_part(first_level, bits, place, queries, level_weights, near_mine, near_other, *fixed):
    tokens, width = queries.shape
    rows = min(2 * CHUNK, tokens)
    band = pl.BlockSpec((rows, width), lambda step: (step, 0))
    near = pl.BlockSpec((width // 2, rows), lambda step: (0, step))

    def tail(part):
        count = 2 * bits - 1
        if part.ndim == 3 and part.shape[0] % count == 0:
            last = part.shape[0] // count - 1
            return pl.BlockSpec((count,) + part.shape[1:], lambda step: (last, 0, 0))
        return pl.BlockSpec(part.shape, lambda step: (0,) * part.ndim)

    return pl.pallas_call(
        functools.partial(far_kernel, first_level),
        grid=(tokens // rows,),
        in_specs=[
            pl.BlockSpec(memory_space=pltpu.SMEM),
            band,
            pl.BlockSpec(level_weights.shape[:2] + (rows,), lambda step: (0, 0, step)),
            near,
            near,
            *[tail(part) for part in fixed],
        ],
        out_specs=band,
        out_shape=jax.ShapeDtypeStruct((tokens, width), BF16),
        scratch_shapes=[
            pltpu.VMEM((width // HEAD, bits * HEAD, HEAD), BF16),
            pltpu.VMEM((width, rows), BF16),
            pltpu.VMEM((rows, width), BF16),
        ],
        cost_estimate=cost(2 * tokens * width * (width + bits * HEAD), 12 * MIB),
        compiler_params=params(28),
    )(place, queries, level_weights, near_mine, near_other, *fixed)


def body(queries, keys, values, level_weights, out_weight):
    inner, outer = lax.axis_size("inner"), lax.axis_size("outer")
    inner_bits, outer_bits = bits_of(inner), bits_of(outer)
    inner_place, outer_place = lax.axis_index("inner"), lax.axis_index("outer")
    place = jnp.stack([inner_place, outer_place]).astype(jnp.int32)
    core = jnp.bitwise_and(inner_place, 1).astype(jnp.int32)
    side = jnp.bitwise_and(jnp.right_shift(inner_place, 1), 1)
    half = keys.shape[1] // 2
    quarter = half // 2
    tie = lax.optimization_barrier

    inputs = outside(keys, values)
    give = block_state(1 - core, 2, *inputs)
    give, inputs = tie((give, inputs))
    first = swap(give, "inner", 1)

    def quarter_of(at, state):
        return state + lax.dynamic_slice_in_dim(first, at * quarter, quarter, 0)

    keep_theirs = block_state(2 * core + 1 - side, 4, *inputs)
    passed = quarter_of(1 - side, keep_theirs)
    passed, inputs = tie((passed, inputs))
    buckets = [swap(passed, "inner", 2)]
    inputs = outside(queries, keys, values, level_weights)
    local = [None, None]
    local[0], keep = local_part(core, True, *inputs)
    keep_ours = lax.dynamic_slice_in_dim(keep, side * quarter, quarter, 0)
    own = quarter_of(side, keep_ours)
    running = own + buckets[0]
    running, inputs = tie((running, inputs))
    (local[1],) = local_part(1 - core, False, *inputs)
    for bit in range(2, inner_bits):
        arrived = swap(running, "inner", 1 << bit)
        if bit == 2:
            arrived, local = tie((arrived, local))
        buckets.append(arrived)
        running = running + arrived

    running, sent = tie((running, jnp.stack([own] + buckets[1:])))
    far = [swap(running, "outer", 1)]
    others = swap(sent, "inner", 2)
    beside = []

    def own_near():
        held = [part for at, bucket in enumerate(buckets) for part in (bucket, others[at])]
        return near_part(core, place, inner_bits, queries, level_weights, local[0], first, *held)

    for bit in range(1, outer_bits):
        running = running + far[-1]
        far.append(swap(running, "outer", 1 << bit))
        beside.append(swap(far[-2], "inner", 2))
        if bit == 1:
            near_mine = own_near()
            far[-1], beside, others, near_mine = tie((far[-1], beside, others, near_mine))
    if outer_bits == 1:
        near_mine = own_near()
        far[-1], others, near_mine = tie((far[-1], others, near_mine))
    late = swap(far[-1], "inner", 2)
    pairs = [(keep_ours, keep_theirs), *((bucket, others[at]) for at, bucket in enumerate(buckets)), *zip(far, beside)]
    mine = jnp.stack([part for pair in pairs for part in pair] + far[-1:])
    other = swap(mine, "inner", 1)
    nears = [
        near_mine,
        near_part(1 - core, place, inner_bits, queries, level_weights, local[1], other),
    ]
    late, nears = tie((late, nears))
    late_other = swap(late, "inner", 1)
    first_level = LOCAL_BITS + 1 + inner_bits
    return far_part(
        first_level, outer_bits, place, queries, level_weights, *nears, mine, other, late, late_other, out_weight
    )


def solution(mesh):
    spec = P(("outer", "inner"), None)
    in_specs = (spec, spec, spec, P(None, None, ("outer", "inner")), P())
    return jax.shard_map(body, mesh=mesh, in_specs=in_specs, out_specs=spec, check_vma=False)
```

```python
import functools

import jax
import jax.numpy as jnp
from jax import lax
from jax.experimental import pallas as pl
from jax.experimental.pallas import tpu as pltpu
from jax.sharding import PartitionSpec as P

HEADS = 8
HEAD = 128
LOCAL_BITS = 10
TILE = 128
CHUNK = 256
F32 = jnp.float32
BF16 = jnp.bfloat16
MIB = 1 << 20


def bits_of(count):
    return count.bit_length() - 1


def swap(block, axis, stride):
    count = lax.axis_size(axis)
    return lax.ppermute(block, axis, [(place, place ^ stride) for place in range(count)])


def raise_to(block, axis, stride):
    count = lax.axis_size(axis)
    route = [(place, place | stride) for place in range(count) if not place & stride]
    return lax.ppermute(block, axis, route)


def cost(flops, moved):
    return pl.CostEstimate(flops=flops, bytes_accessed=moved, transcendentals=0)


def params(limit):
    return pltpu.CompilerParams(vmem_limit_bytes=limit * MIB)


def outside(*parts):
    return tuple(pltpu.with_memory_space_constraint(part, pltpu.HBM) for part in parts)


def product(left, right):
    return jnp.dot(left, right, preferred_element_type=F32)


def product_nt(left, right):
    return lax.dot_general(left, right, (((1,), (1,)), ((), ())), preferred_element_type=F32)


def identity(size):
    row = lax.broadcasted_iota(jnp.int32, (size, size), 0)
    column = lax.broadcasted_iota(jnp.int32, (size, size), 1)
    return (row == column).astype(F32).astype(BF16)


def turned(block):
    return product_nt(identity(block.shape[1]), block).astype(BF16)


def state_kernel(place, keys, values, state):
    both = product(turned(values[...]), keys[...])
    for low in range(0, keys.shape[1], HEAD):
        part = slice(low, low + HEAD)
        state[part, :] = both[part, part]


def block_state(place, share, keys, values):
    tokens, width = keys.shape
    step = 2 * HEAD
    steps = width // share // step
    column = pl.BlockSpec((tokens, step), lambda pair, place: (0, place[0] * steps + pair))
    return pl.pallas_call(
        state_kernel,
        grid_spec=pltpu.PrefetchScalarGridSpec(
            num_scalar_prefetch=1,
            grid=(steps,),
            in_specs=[column, column],
            out_specs=pl.BlockSpec((step, HEAD), lambda pair, place: (pair, 0)),
        ),
        out_shape=pltpu.VMEM((width // share, HEAD), F32),
        cost_estimate=cost(2 * tokens * width * HEAD // share, 5 * MIB // share),
        compiler_params=params(16),
    )(place.reshape(1).astype(jnp.int32), keys, values)


def tile_mixing(rows):
    target = lax.broadcasted_iota(jnp.int32, (8, TILE), 1)
    source = lax.broadcasted_iota(jnp.int32, (8, TILE), 0)
    rows = [jnp.broadcast_to(row, (8, TILE)) for row in rows]
    within = jnp.bitwise_and(target, 7)
    differ = jnp.bitwise_xor(within, source)
    base = rows[3]
    for level in (2, 1, 0):
        base = jnp.where(differ < 1 << level, rows[level], base)
    parts = [jnp.where(source <= within, base, 0.0)]
    for bit in range(3, bits_of(TILE)):
        upper = jnp.bitwise_and(jnp.right_shift(target, bit), 1) == 1
        parts = [jnp.where(upper, rows[bit + 1], part) for part in parts] + [
            jnp.where(upper, part, 0.0) for part in parts
        ]
    return jnp.concatenate(parts, axis=0)


def local_kernel(half, queries, keys, values, weights, local, *rest):
    *state, rows = rest
    tokens, width = queries.shape
    chunks = tokens // CHUNK
    levels = rows.shape[1]
    top = bits_of(CHUNK)
    spans = [slice(low, low + CHUNK) for low in range(0, tokens, CHUNK)]
    parts = [slice(low, low + HEAD) for low in range(0, width, HEAD)]
    first = (half[0] * pl.num_programs(0) + pl.program_id(0)) * len(parts)
    for at in range(len(parts)):
        rows[at] = weights[:, pl.ds(first + at, 1), :].reshape(levels, tokens)
    flipped = turned(values[...])

    def row(at, level, low, size):
        return rows[at, level : level + 1, low : low + size]

    nodes = []
    for part in parts:
        line = [product(flipped[part, span], keys[span, part]) for span in (spans if state else spans[:-1])]
        if state:
            state[0][part, :] = functools.reduce(jnp.add, line)
        known = [line]
        while len(known[-1]) > 1:
            below = known[-1]
            known.append([below[at] + below[at + 1] for at in range(0, len(below) - 1, 2)])
        nodes.append([[state.astype(BF16) for state in level] for level in known])
    scores = {}
    for at, part in enumerate(parts):
        for chunk, span in enumerate(spans):
            used = [bit for bit in range(bits_of(chunks)) if chunk >> bit & 1]
            left = [keys[span, part]] + [nodes[at][bit][(chunk >> bit) - 1] for bit in used]
            left = jnp.concatenate(left, axis=0) if used else left[0]
            scores[at, chunk] = product_nt(left, queries[span, part])
    for at, part in enumerate(parts):
        for chunk, span in enumerate(spans):
            low = chunk * CHUNK
            score = scores[at, chunk]
            lower, upper = (
                tile_mixing([row(at, level, start, TILE) for level in range(top)]) for start in (low, low + TILE)
            )
            across = row(at, top, low + TILE, TILE)
            weighted = jnp.concatenate(
                [
                    jnp.concatenate([score[:TILE, :TILE] * lower, score[:TILE, TILE:] * across], axis=1),
                    jnp.concatenate([jnp.zeros_like(lower), score[TILE:CHUNK, TILE:] * upper], axis=1),
                ],
                axis=0,
            ).astype(BF16)
            total = product(flipped[part, span], weighted)
            below = CHUNK
            for bit in range(bits_of(chunks)):
                if chunk >> bit & 1:
                    total = total + row(at, top + 1 + bit, low, CHUNK) * score[below : below + HEAD, :]
                    below += HEAD
            local[part, span] = total.astype(BF16)


def local_part(half, with_state, queries, keys, values, level_weights):
    tokens, width = queries.shape
    step = 2 * HEAD
    steps = width // step // 2
    column = pl.BlockSpec((tokens, step), lambda pair, half: (0, half[0] * steps + pair))
    return pl.pallas_call(
        local_kernel,
        grid_spec=pltpu.PrefetchScalarGridSpec(
            num_scalar_prefetch=1,
            grid=(steps,),
            in_specs=[column, column, column, pl.BlockSpec(level_weights.shape, lambda pair, half: (0, 0, 0))],
            out_specs=[
                pl.BlockSpec((step, tokens), lambda pair, half: (pair, 0)),
                pl.BlockSpec((step, HEAD), lambda pair, half: (pair, 0)),
            ][: 1 + with_state],
            scratch_shapes=[pltpu.VMEM((2, level_weights.shape[0], tokens), F32)],
        ),
        out_shape=[pltpu.HBM((width // 2, tokens), BF16), pltpu.VMEM((width // 2, HEAD), F32)][: 1 + with_state],
        cost_estimate=cost(tokens * width, MIB // 4),
        compiler_params=params(16),
    )(half.reshape(1), queries, keys, values, level_weights)


def has_bit(place, bit):
    return jnp.bitwise_and(jnp.right_shift(place, bit), 1) == 1


def near_kernel(aliased, half, place, queries, weights, local, *rest):
    *held, near, states, rows = rest[aliased:]
    step = pl.program_id(0)
    bits = states.shape[1] // HEAD
    size = states.shape[0] * HEAD // 2

    def quarter_state(bit, quarter, slot):
        if len(held) == 1:
            return held[0][2 * bit + slot]
        if bit == 0:
            return held[0][quarter * size : (quarter + 1) * size, :]
        return jnp.where(slot == 0, held[2 * bit - 1][...], held[2 * bit][...])

    @pl.when(step == 0)
    def _():
        side = jnp.bitwise_and(jnp.right_shift(place[0], 1), 1)
        for quarter in range(2):
            slot = jnp.bitwise_xor(side, quarter)
            for bit in range(bits):
                state = jnp.where(has_bit(place[0], bit), quarter_state(bit, quarter, slot), 0.0).astype(BF16)
                for at in range(0, size, HEAD):
                    states[(quarter * size + at) // HEAD, bit * HEAD : (bit + 1) * HEAD, :] = state[at : at + HEAD]

    for at in range(rows.shape[0]):
        part = slice(at * HEAD, (at + 1) * HEAD)
        head = step * rows.shape[0] + at
        rows[at] = weights[:, pl.ds(half[0] * states.shape[0] + head, 1), :].reshape(rows.shape[1:])
        products = product_nt(states[head], queries[:, part])
        total = local[part, :].astype(F32)
        for bit in range(bits):
            level = LOCAL_BITS + 1 + bit
            total = total + rows[at, level : level + 1, :] * products[bit * HEAD : (bit + 1) * HEAD]
        near[part, :] = total


def near_part(half, place, bits, queries, level_weights, local, into, *held):
    tokens, width = queries.shape
    heads = width // HEAD // 2
    step = 2 * HEAD
    steps = width // step // 2
    into = () if into is None else (pltpu.with_memory_space_constraint(into, pltpu.VMEM),)
    return pl.pallas_call(
        functools.partial(near_kernel, len(into)),
        grid_spec=pltpu.PrefetchScalarGridSpec(
            num_scalar_prefetch=2,
            grid=(steps,),
            in_specs=[
                pl.BlockSpec((tokens, step), lambda pair, half, place: (0, half[0] * steps + pair)),
                pl.BlockSpec(level_weights.shape, lambda pair, half, place: (0, 0, 0)),
                pl.BlockSpec((step, tokens), lambda pair, half, place: (pair, 0)),
                *[pl.BlockSpec(memory_space=pltpu.VMEM)] * len(into),
                *[
                    pl.BlockSpec(
                        (2 * bits,) + part.shape[1:] if part.ndim == 3 else part.shape,
                        lambda pair, half, place, rank=part.ndim: (0,) * rank,
                    )
                    for part in held
                ],
            ],
            out_specs=pl.BlockSpec((step, tokens), lambda pair, half, place: (half[0] * steps + pair, 0)),
            scratch_shapes=[
                pltpu.VMEM((heads, bits * HEAD, HEAD), BF16),
                pltpu.VMEM((2, level_weights.shape[0], tokens), F32),
            ],
        ),
        out_shape=pltpu.VMEM((width, tokens), F32),
        input_output_aliases={5: 0} if into else {},
        cost_estimate=cost(tokens * width, MIB // 4),
        compiler_params=params(16),
    )(half.reshape(1), place, *outside(queries, level_weights, local), *into, *held)


def far_kernel(first_level, place, queries, weights, near, early, early_other, late, late_other, out_weight,
               mixed, states, flipped, attended):
    rows, width = attended.shape
    bits = states.shape[1] // HEAD
    size = late.shape[0]
    skip = early.shape[0] + 1 - 2 * bits
    core = jnp.bitwise_and(place[0], 1)

    @pl.when(pl.program_id(0) == 0)
    def _():
        side = jnp.bitwise_and(jnp.right_shift(place[0], 1), 1)
        for bit in range(bits):
            mine, other = ([part[skip + 2 * bit], part[skip + 2 * bit + 1] if bit + 1 < bits else final[...]]
                           for part, final in ((early, late), (early_other, late_other)))
            for quarter in range(4):
                here, there = (jnp.where(side == quarter % 2, *part) for part in (mine, other))
                state = jnp.where(core == quarter // 2, here, there)
                state = jnp.where(has_bit(place[1], bit), state, 0.0).astype(BF16)
                for at in range(0, size, HEAD):
                    head = (quarter * size + at) // HEAD
                    states[head, bit * HEAD : (bit + 1) * HEAD, :] = state[at : at + HEAD]

    for half in range(2):
        for low in range(0, width // 2, HEAD):
            part = slice(half * (width // 2) + low, half * (width // 2) + low + HEAD)
            head = part.start // HEAD
            products = product_nt(states[head], queries[:, part])
            total = near[part, :]
            for bit in range(bits):
                row = weights[first_level + bit, head : head + 1, :]
                total = total + row * products[bit * HEAD : (bit + 1) * HEAD]
            flipped[part, :] = total.astype(BF16)
    unit = identity(CHUNK)
    for top in range(0, rows, CHUNK):
        for low in range(0, width, CHUNK):
            block = flipped[low : low + CHUNK, top : top + CHUNK]
            attended[top : top + CHUNK, low : low + CHUNK] = product_nt(unit, block).astype(BF16)
    mixed[...] = product(attended[...], out_weight[...]).astype(BF16)


def far_part(first_level, bits, place, queries, level_weights, near, *fixed):
    tokens, width = queries.shape
    rows = min(2 * CHUNK, tokens)
    band = pl.BlockSpec((rows, width), lambda step: (step, 0))

    def tail(part):
        count = 2 * bits - 1
        if part.ndim == 3 and part.shape[0] % count == 0:
            last = part.shape[0] // count - 1
            return pl.BlockSpec((count,) + part.shape[1:], lambda step: (last, 0, 0))
        return pl.BlockSpec(part.shape, lambda step: (0,) * part.ndim)

    return pl.pallas_call(
        functools.partial(far_kernel, first_level),
        grid=(tokens // rows,),
        in_specs=[
            pl.BlockSpec(memory_space=pltpu.SMEM),
            band,
            pl.BlockSpec(level_weights.shape[:2] + (rows,), lambda step: (0, 0, step)),
            pl.BlockSpec((width, rows), lambda step: (0, step)),
            *[tail(part) for part in fixed],
        ],
        out_specs=band,
        out_shape=jax.ShapeDtypeStruct((tokens, width), BF16),
        scratch_shapes=[
            pltpu.VMEM((width // HEAD, bits * HEAD, HEAD), BF16),
            pltpu.VMEM((width, rows), BF16),
            pltpu.VMEM((rows, width), BF16),
        ],
        cost_estimate=cost(2 * tokens * width * (width + bits * HEAD), 12 * MIB),
        compiler_params=params(28),
    )(place, queries, level_weights, near, *fixed)


def body(queries, keys, values, level_weights, out_weight):
    inner, outer = lax.axis_size("inner"), lax.axis_size("outer")
    inner_bits, outer_bits = bits_of(inner), bits_of(outer)
    inner_place, outer_place = lax.axis_index("inner"), lax.axis_index("outer")
    place = jnp.stack([inner_place, outer_place]).astype(jnp.int32)
    core = jnp.bitwise_and(inner_place, 1).astype(jnp.int32)
    side = jnp.bitwise_and(jnp.right_shift(inner_place, 1), 1)
    half = keys.shape[1] // 2
    quarter = half // 2
    tie = lax.optimization_barrier

    inputs = outside(keys, values)
    give = block_state(1 - core, 2, *inputs)
    give, inputs = tie((give, inputs))
    first = swap(give, "inner", 1)

    def quarter_of(at, state):
        return state + lax.dynamic_slice_in_dim(first, at * quarter, quarter, 0)

    keep_theirs = block_state(2 * core + 1 - side, 4, *inputs)
    passed = quarter_of(1 - side, keep_theirs)
    passed, inputs = tie((passed, inputs))
    buckets = [swap(passed, "inner", 2)]
    inputs = outside(queries, keys, values, level_weights)
    local = [None, None]
    local[0], keep = local_part(core, True, *inputs)
    keep_ours = lax.dynamic_slice_in_dim(keep, side * quarter, quarter, 0)
    own = quarter_of(side, keep_ours)
    running = own + buckets[0]
    running, inputs = tie((running, inputs))
    (local[1],) = local_part(1 - core, False, *inputs)
    for bit in range(2, inner_bits):
        arrived = swap(running, "inner", 1 << bit)
        if bit == 2:
            arrived, local = tie((arrived, local))
        buckets.append(arrived)
        running = running + arrived

    running, own, later = tie((running, own, buckets[1:]))
    far = [swap(running, "outer", 1)]
    others = [swap(part, "inner", 2) for part in (own, *later)]
    beside = []

    def own_near():
        held = [part for at, bucket in enumerate(buckets) for part in (bucket, others[at])]
        return near_part(core, place, inner_bits, queries, level_weights, local[0], None, first, *held)

    for bit in range(1, outer_bits):
        running = running + far[-1]
        far.append(swap(running, "outer", 1 << bit))
        beside.append(swap(far[-2], "inner", 2))
        if bit == 1:
            near_mine = own_near()
            far[-1], beside, others, near_mine = tie((far[-1], beside, others, near_mine))
    if outer_bits == 1:
        near_mine = own_near()
        far[-1], others, near_mine = tie((far[-1], others, near_mine))
    late = swap(far[-1], "inner", 2)
    pairs = [(keep_ours, keep_theirs), *((bucket, others[at]) for at, bucket in enumerate(buckets)), *zip(far, beside)]
    mine = jnp.stack([part for pair in pairs for part in pair] + far[-1:])
    other = swap(mine, "inner", 1)
    near = near_part(1 - core, place, inner_bits, queries, level_weights, local[1], near_mine, other)
    late, near = tie((late, near))
    late_other = swap(late, "inner", 1)
    first_level = LOCAL_BITS + 1 + inner_bits
    return far_part(
        first_level, outer_bits, place, queries, level_weights, near, mine, other, late, late_other, out_weight
    )


def solution(mesh):
    spec = P(("outer", "inner"), None)
    in_specs = (spec, spec, spec, P(None, None, ("outer", "inner")), P())
    return jax.shard_map(body, mesh=mesh, in_specs=in_specs, out_specs=spec, check_vma=False)
```

```python
import functools

import jax
import jax.numpy as jnp
from jax import lax
from jax.experimental import pallas as pl
from jax.experimental.pallas import tpu as pltpu
from jax.sharding import PartitionSpec as P

HEADS = 8
HEAD = 128
LOCAL_BITS = 10
TILE = 128
CHUNK = 256
F32 = jnp.float32
BF16 = jnp.bfloat16
MIB = 1 << 20


def bits_of(count):
    return count.bit_length() - 1


def swap(block, axis, stride):
    count = lax.axis_size(axis)
    return lax.ppermute(block, axis, [(place, place ^ stride) for place in range(count)])


def raise_to(block, axis, stride):
    count = lax.axis_size(axis)
    route = [(place, place | stride) for place in range(count) if not place & stride]
    return lax.ppermute(block, axis, route)


def cost(flops, moved):
    return pl.CostEstimate(flops=flops, bytes_accessed=moved, transcendentals=0)


def params(limit):
    return pltpu.CompilerParams(vmem_limit_bytes=limit * MIB)


def outside(*parts):
    return tuple(pltpu.with_memory_space_constraint(part, pltpu.HBM) for part in parts)


def inside(*parts):
    return tuple(pltpu.with_memory_space_constraint(part, pltpu.VMEM) for part in parts)


def product(left, right):
    return jnp.dot(left, right, preferred_element_type=F32)


def product_nt(left, right):
    return lax.dot_general(left, right, (((1,), (1,)), ((), ())), preferred_element_type=F32)


def identity(size):
    row = lax.broadcasted_iota(jnp.int32, (size, size), 0)
    column = lax.broadcasted_iota(jnp.int32, (size, size), 1)
    return (row == column).astype(F32).astype(BF16)


def turned(block):
    return product_nt(identity(block.shape[1]), block).astype(BF16)


def state_kernel(place, keys, values, state):
    both = product(turned(values[...]), keys[...])
    for low in range(0, keys.shape[1], HEAD):
        part = slice(low, low + HEAD)
        state[part, :] = both[part, part]


def block_state(place, share, keys, values):
    tokens, width = keys.shape
    step = 2 * HEAD
    steps = width // share // step
    column = pl.BlockSpec((tokens, step), lambda pair, place: (0, place[0] * steps + pair))
    return pl.pallas_call(
        state_kernel,
        grid_spec=pltpu.PrefetchScalarGridSpec(
            num_scalar_prefetch=1,
            grid=(steps,),
            in_specs=[column, column],
            out_specs=pl.BlockSpec((step, HEAD), lambda pair, place: (pair, 0)),
        ),
        out_shape=pltpu.VMEM((width // share, HEAD), F32),
        cost_estimate=cost(2 * tokens * width * HEAD // share, 5 * MIB // share),
        compiler_params=params(16),
    )(place.reshape(1).astype(jnp.int32), keys, values)


def tile_mixing(rows):
    target = lax.broadcasted_iota(jnp.int32, (8, TILE), 1)
    source = lax.broadcasted_iota(jnp.int32, (8, TILE), 0)
    rows = [jnp.broadcast_to(row, (8, TILE)) for row in rows]
    within = jnp.bitwise_and(target, 7)
    differ = jnp.bitwise_xor(within, source)
    base = rows[3]
    for level in (2, 1, 0):
        base = jnp.where(differ < 1 << level, rows[level], base)
    parts = [jnp.where(source <= within, base, 0.0)]
    for bit in range(3, bits_of(TILE)):
        upper = jnp.bitwise_and(jnp.right_shift(target, bit), 1) == 1
        parts = [jnp.where(upper, rows[bit + 1], part) for part in parts] + [
            jnp.where(upper, part, 0.0) for part in parts
        ]
    return jnp.concatenate(parts, axis=0)


def local_kernel(half, queries, keys, values, weights, local, *rest):
    *state, rows = rest
    tokens, width = queries.shape
    chunks = tokens // CHUNK
    levels = rows.shape[1]
    top = bits_of(CHUNK)
    spans = [slice(low, low + CHUNK) for low in range(0, tokens, CHUNK)]
    parts = [slice(low, low + HEAD) for low in range(0, width, HEAD)]
    first = (half[0] * pl.num_programs(0) + pl.program_id(0)) * len(parts)
    for at in range(len(parts)):
        rows[at] = weights[:, pl.ds(first + at, 1), :].reshape(levels, tokens)
    flipped = turned(values[...])

    def row(at, level, low, size):
        return rows[at, level : level + 1, low : low + size]

    nodes = []
    for part in parts:
        line = [product(flipped[part, span], keys[span, part]) for span in (spans if state else spans[:-1])]
        if state:
            state[0][part, :] = functools.reduce(jnp.add, line)
        known = [line]
        while len(known[-1]) > 1:
            below = known[-1]
            known.append([below[at] + below[at + 1] for at in range(0, len(below) - 1, 2)])
        nodes.append([[state.astype(BF16) for state in level] for level in known])
    scores = {}
    for at, part in enumerate(parts):
        for chunk, span in enumerate(spans):
            used = [bit for bit in range(bits_of(chunks)) if chunk >> bit & 1]
            left = [keys[span, part]] + [nodes[at][bit][(chunk >> bit) - 1] for bit in used]
            left = jnp.concatenate(left, axis=0) if used else left[0]
            scores[at, chunk] = product_nt(left, queries[span, part])
    for at, part in enumerate(parts):
        for chunk, span in enumerate(spans):
            low = chunk * CHUNK
            score = scores[at, chunk]
            lower, upper = (
                tile_mixing([row(at, level, start, TILE) for level in range(top)]) for start in (low, low + TILE)
            )
            across = row(at, top, low + TILE, TILE)
            weighted = jnp.concatenate(
                [
                    jnp.concatenate([score[:TILE, :TILE] * lower, score[:TILE, TILE:] * across], axis=1),
                    jnp.concatenate([jnp.zeros_like(lower), score[TILE:CHUNK, TILE:] * upper], axis=1),
                ],
                axis=0,
            ).astype(BF16)
            total = product(flipped[part, span], weighted)
            below = CHUNK
            for bit in range(bits_of(chunks)):
                if chunk >> bit & 1:
                    total = total + row(at, top + 1 + bit, low, CHUNK) * score[below : below + HEAD, :]
                    below += HEAD
            local[part, span] = total.astype(BF16)


def local_part(half, with_state, queries, keys, values, level_weights):
    tokens, width = queries.shape
    step = 2 * HEAD
    steps = width // step // 2
    levels = LOCAL_BITS + 1
    column = pl.BlockSpec((tokens, step), lambda pair, half: (0, half[0] * steps + pair))
    return pl.pallas_call(
        local_kernel,
        grid_spec=pltpu.PrefetchScalarGridSpec(
            num_scalar_prefetch=1,
            grid=(steps,),
            in_specs=[column, column, column, pl.BlockSpec((levels,) + level_weights.shape[1:], lambda pair, half: (0, 0, 0))],
            out_specs=[
                pl.BlockSpec((step, tokens), lambda pair, half: (pair, 0)),
                pl.BlockSpec((step, HEAD), lambda pair, half: (pair, 0)),
            ][: 1 + with_state],
            scratch_shapes=[pltpu.VMEM((2, levels, tokens), F32)],
        ),
        out_shape=[pltpu.HBM((width // 2, tokens), BF16), pltpu.VMEM((width // 2, HEAD), F32)][: 1 + with_state],
        cost_estimate=cost(tokens * width, MIB // 4),
        compiler_params=params(16),
    )(half.reshape(1), queries, keys, values, level_weights)


def has_bit(place, bit):
    return jnp.bitwise_and(jnp.right_shift(place, bit), 1) == 1


def near_kernel(aliased, half, place, queries, weights, local, *rest):
    *held, near, states, rows = rest[aliased:]
    step = pl.program_id(0)
    bits = states.shape[1] // HEAD
    size = states.shape[0] * HEAD // 2

    def quarter_state(bit, quarter, slot):
        if len(held) == 1:
            return held[0][2 * bit + slot]
        if bit == 0:
            return held[0][quarter * size : (quarter + 1) * size, :]
        return jnp.where(slot == 0, held[2 * bit - 1][...], held[2 * bit][...])

    @pl.when(step == 0)
    def _():
        side = jnp.bitwise_and(jnp.right_shift(place[0], 1), 1)
        for quarter in range(2):
            slot = jnp.bitwise_xor(side, quarter)
            for bit in range(bits):
                state = jnp.where(has_bit(place[0], bit), quarter_state(bit, quarter, slot), 0.0).astype(BF16)
                for at in range(0, size, HEAD):
                    states[(quarter * size + at) // HEAD, bit * HEAD : (bit + 1) * HEAD, :] = state[at : at + HEAD]

    for at in range(rows.shape[0]):
        part = slice(at * HEAD, (at + 1) * HEAD)
        head = step * rows.shape[0] + at
        rows[at] = weights[:, pl.ds(half[0] * states.shape[0] + head, 1), :].reshape(rows.shape[1:])
        products = product_nt(states[head], queries[:, part])
        total = local[part, :].astype(F32)
        for bit in range(bits):
            level = LOCAL_BITS + 1 + bit
            total = total + rows[at, level : level + 1, :] * products[bit * HEAD : (bit + 1) * HEAD]
        near[part, :] = total


def near_part(half, place, bits, queries, level_weights, local, into, *held):
    tokens, width = queries.shape
    heads = width // HEAD // 2
    step = 2 * HEAD
    steps = width // step // 2
    into = () if into is None else (pltpu.with_memory_space_constraint(into, pltpu.VMEM),)
    return pl.pallas_call(
        functools.partial(near_kernel, len(into)),
        grid_spec=pltpu.PrefetchScalarGridSpec(
            num_scalar_prefetch=2,
            grid=(steps,),
            in_specs=[
                pl.BlockSpec((tokens, step), lambda pair, half, place: (0, half[0] * steps + pair)),
                pl.BlockSpec(level_weights.shape, lambda pair, half, place: (0, 0, 0)),
                pl.BlockSpec((step, tokens), lambda pair, half, place: (pair, 0)),
                *[pl.BlockSpec(memory_space=pltpu.VMEM)] * len(into),
                *[
                    pl.BlockSpec(
                        (2 * bits,) + part.shape[1:] if part.ndim == 3 else part.shape,
                        lambda pair, half, place, rank=part.ndim: (0,) * rank,
                    )
                    for part in held
                ],
            ],
            out_specs=pl.BlockSpec((step, tokens), lambda pair, half, place: (half[0] * steps + pair, 0)),
            scratch_shapes=[
                pltpu.VMEM((heads, bits * HEAD, HEAD), BF16),
                pltpu.VMEM((2, level_weights.shape[0], tokens), F32),
            ],
        ),
        out_shape=pltpu.VMEM((width, tokens), F32),
        input_output_aliases={5: 0} if into else {},
        cost_estimate=cost(tokens * width, MIB // 4),
        compiler_params=params(16),
    )(half.reshape(1), place, *inside(queries, level_weights), *outside(local), *into, *held)


def far_kernel(first_level, place, queries, weights, near, early, early_other, late, late_other, out_weight,
               mixed, states, flipped, attended):
    rows, width = attended.shape
    bits = states.shape[1] // HEAD
    size = late.shape[0]
    skip = early.shape[0] + 1 - 2 * bits
    core = jnp.bitwise_and(place[0], 1)

    @pl.when(pl.program_id(0) == 0)
    def _():
        side = jnp.bitwise_and(jnp.right_shift(place[0], 1), 1)
        for bit in range(bits):
            mine, other = ([part[skip + 2 * bit], part[skip + 2 * bit + 1] if bit + 1 < bits else final[...]]
                           for part, final in ((early, late), (early_other, late_other)))
            for quarter in range(4):
                here, there = (jnp.where(side == quarter % 2, *part) for part in (mine, other))
                state = jnp.where(core == quarter // 2, here, there)
                state = jnp.where(has_bit(place[1], bit), state, 0.0).astype(BF16)
                for at in range(0, size, HEAD):
                    head = (quarter * size + at) // HEAD
                    states[head, bit * HEAD : (bit + 1) * HEAD, :] = state[at : at + HEAD]

    for half in range(2):
        for low in range(0, width // 2, HEAD):
            part = slice(half * (width // 2) + low, half * (width // 2) + low + HEAD)
            head = part.start // HEAD
            products = product_nt(states[head], queries[:, part])
            total = near[part, :]
            for bit in range(bits):
                row = weights[first_level + bit, head : head + 1, :]
                total = total + row * products[bit * HEAD : (bit + 1) * HEAD]
            flipped[part, :] = total.astype(BF16)
    unit = identity(CHUNK)
    for top in range(0, rows, CHUNK):
        for low in range(0, width, CHUNK):
            block = flipped[low : low + CHUNK, top : top + CHUNK]
            attended[top : top + CHUNK, low : low + CHUNK] = product_nt(unit, block).astype(BF16)
    mixed[...] = product(attended[...], out_weight[...]).astype(BF16)


def far_part(first_level, bits, place, queries, level_weights, near, *fixed):
    tokens, width = queries.shape
    rows = min(2 * CHUNK, tokens)
    band = pl.BlockSpec((rows, width), lambda step: (step, 0))

    def tail(part):
        count = 2 * bits - 1
        if part.ndim == 3 and part.shape[0] % count == 0:
            last = part.shape[0] // count - 1
            return pl.BlockSpec((count,) + part.shape[1:], lambda step: (last, 0, 0))
        return pl.BlockSpec(part.shape, lambda step: (0,) * part.ndim)

    return pl.pallas_call(
        functools.partial(far_kernel, first_level),
        grid=(tokens // rows,),
        in_specs=[
            pl.BlockSpec(memory_space=pltpu.SMEM),
            band,
            pl.BlockSpec(level_weights.shape[:2] + (rows,), lambda step: (0, 0, step)),
            pl.BlockSpec((width, rows), lambda step: (0, step)),
            *[tail(part) for part in fixed],
        ],
        out_specs=band,
        out_shape=jax.ShapeDtypeStruct((tokens, width), BF16),
        scratch_shapes=[
            pltpu.VMEM((width // HEAD, bits * HEAD, HEAD), BF16),
            pltpu.VMEM((width, rows), BF16),
            pltpu.VMEM((rows, width), BF16),
        ],
        cost_estimate=cost(2 * tokens * width * (width + bits * HEAD), 12 * MIB),
        compiler_params=params(28),
    )(place, queries, level_weights, near, *fixed)


def body(queries, keys, values, level_weights, out_weight):
    inner, outer = lax.axis_size("inner"), lax.axis_size("outer")
    inner_bits, outer_bits = bits_of(inner), bits_of(outer)
    inner_place, outer_place = lax.axis_index("inner"), lax.axis_index("outer")
    place = jnp.stack([inner_place, outer_place]).astype(jnp.int32)
    core = jnp.bitwise_and(inner_place, 1).astype(jnp.int32)
    side = jnp.bitwise_and(jnp.right_shift(inner_place, 1), 1)
    half = keys.shape[1] // 2
    quarter = half // 2
    tie = lax.optimization_barrier

    inputs = outside(keys, values)
    give = block_state(1 - core, 2, *inputs)
    give, inputs = tie((give, inputs))
    first = swap(give, "inner", 1)

    def quarter_of(at, state):
        return state + lax.dynamic_slice_in_dim(first, at * quarter, quarter, 0)

    keep_theirs = block_state(2 * core + 1 - side, 4, *inputs)
    passed = quarter_of(1 - side, keep_theirs)
    passed, inputs = tie((passed, inputs))
    buckets = [swap(passed, "inner", 2)]
    inputs = outside(queries, keys, values, level_weights)
    local = [None, None]
    local[0], keep = local_part(core, True, *inputs)
    keep_ours = lax.dynamic_slice_in_dim(keep, side * quarter, quarter, 0)
    own = quarter_of(side, keep_ours)
    running = own + buckets[0]
    running, inputs = tie((running, inputs))
    (local[1],) = local_part(1 - core, False, *inputs)
    for bit in range(2, inner_bits):
        arrived = swap(running, "inner", 1 << bit)
        if bit == 2:
            arrived, local = tie((arrived, local))
        buckets.append(arrived)
        running = running + arrived

    running, own, later = tie((running, own, buckets[1:]))
    far = [swap(running, "outer", 1)]
    others = [swap(part, "inner", 2) for part in (own, *later)]
    beside = []

    def own_near():
        held = [part for at, bucket in enumerate(buckets) for part in (bucket, others[at])]
        return near_part(core, place, inner_bits, queries, level_weights, local[0], None, first, *held)

    for bit in range(1, outer_bits):
        running = running + far[-1]
        far.append(swap(running, "outer", 1 << bit))
        beside.append(swap(far[-2], "inner", 2))
        if bit == 1:
            near_mine = own_near()
            far[-1], beside, others, near_mine = tie((far[-1], beside, others, near_mine))
    if outer_bits == 1:
        near_mine = own_near()
        far[-1], others, near_mine = tie((far[-1], others, near_mine))
    late = swap(far[-1], "inner", 2)
    pairs = [(keep_ours, keep_theirs), *((bucket, others[at]) for at, bucket in enumerate(buckets)), *zip(far, beside)]
    mine = jnp.stack([part for pair in pairs for part in pair] + far[-1:])
    other = swap(mine, "inner", 1)
    near = near_part(1 - core, place, inner_bits, queries, level_weights, local[1], near_mine, other)
    late, near = tie((late, near))
    late_other = swap(late, "inner", 1)
    first_level = LOCAL_BITS + 1 + inner_bits
    return far_part(
        first_level, outer_bits, place, queries, level_weights, near, mine, other, late, late_other, out_weight
    )


def solution(mesh):
    spec = P(("outer", "inner"), None)
    in_specs = (spec, spec, spec, P(None, None, ("outer", "inner")), P())
    return jax.shard_map(body, mesh=mesh, in_specs=in_specs, out_specs=spec, check_vma=False)
```

```python
import functools

import jax
import jax.numpy as jnp
from jax import lax
from jax.experimental import pallas as pl
from jax.experimental.pallas import tpu as pltpu
from jax.sharding import PartitionSpec as P

HEADS = 8
HEAD = 128
LOCAL_BITS = 10
TILE = 128
CHUNK = 256
F32 = jnp.float32
BF16 = jnp.bfloat16
MIB = 1 << 20


def bits_of(count):
    return count.bit_length() - 1


def swap(block, axis, stride):
    count = lax.axis_size(axis)
    return lax.ppermute(block, axis, [(place, place ^ stride) for place in range(count)])


def raise_to(block, axis, stride):
    count = lax.axis_size(axis)
    route = [(place, place | stride) for place in range(count) if not place & stride]
    return lax.ppermute(block, axis, route)


def cost(flops, moved):
    return pl.CostEstimate(flops=flops, bytes_accessed=moved, transcendentals=0)


def params(limit):
    return pltpu.CompilerParams(vmem_limit_bytes=limit * MIB)


def outside(*parts):
    return tuple(pltpu.with_memory_space_constraint(part, pltpu.HBM) for part in parts)


def product(left, right):
    return jnp.dot(left, right, preferred_element_type=F32)


def product_nt(left, right):
    return lax.dot_general(left, right, (((1,), (1,)), ((), ())), preferred_element_type=F32)


def identity(size):
    row = lax.broadcasted_iota(jnp.int32, (size, size), 0)
    column = lax.broadcasted_iota(jnp.int32, (size, size), 1)
    return (row == column).astype(F32).astype(BF16)


def turned(block):
    return product_nt(identity(block.shape[1]), block).astype(BF16)


def state_kernel(place, keys, values, state):
    step = pl.program_id(0)
    found = []
    for low in range(0, keys.shape[1], 2 * HEAD):
        pair = slice(low, low + 2 * HEAD)
        both = product(turned(values[:, pair]), keys[:, pair])
        found += [both[:HEAD, :HEAD], both[HEAD:, HEAD:]]

    @pl.when(step == 0)
    def _():
        for at, part in enumerate(found):
            state[at * HEAD : (at + 1) * HEAD, :] = part

    @pl.when(step > 0)
    def _():
        for at, part in enumerate(found):
            state[at * HEAD : (at + 1) * HEAD, :] += part


def block_state(place, share, keys, values):
    tokens, width = keys.shape
    rows = min(tokens, share // 2 * CHUNK)
    band = pl.BlockSpec((rows, width // share), lambda step, place: (step, place[0]))
    return pl.pallas_call(
        state_kernel,
        grid_spec=pltpu.PrefetchScalarGridSpec(
            num_scalar_prefetch=1,
            grid=(tokens // rows,),
            in_specs=[band, band],
            out_specs=pl.BlockSpec((width // share, HEAD), lambda step, place: (0, 0)),
        ),
        out_shape=pltpu.VMEM((width // share, HEAD), F32),
        cost_estimate=cost(2 * tokens * width * HEAD // share, 5 * MIB // share),
        compiler_params=params(16),
    )(place.reshape(1).astype(jnp.int32), keys, values)


def tile_mixing(rows):
    target = lax.broadcasted_iota(jnp.int32, (8, TILE), 1)
    source = lax.broadcasted_iota(jnp.int32, (8, TILE), 0)
    rows = [jnp.broadcast_to(row, (8, TILE)) for row in rows]
    within = jnp.bitwise_and(target, 7)
    differ = jnp.bitwise_xor(within, source)
    base = rows[3]
    for level in (2, 1, 0):
        base = jnp.where(differ < 1 << level, rows[level], base)
    parts = [jnp.where(source <= within, base, 0.0)]
    for bit in range(3, bits_of(TILE)):
        upper = jnp.bitwise_and(jnp.right_shift(target, bit), 1) == 1
        parts = [jnp.where(upper, rows[bit + 1], part) for part in parts] + [
            jnp.where(upper, part, 0.0) for part in parts
        ]
    return jnp.concatenate(parts, axis=0)


def local_kernel(half, queries, keys, values, weights, local, *rest):
    *state, rows = rest
    tokens, width = queries.shape
    chunks = tokens // CHUNK
    levels = rows.shape[1]
    top = bits_of(CHUNK)
    spans = [slice(low, low + CHUNK) for low in range(0, tokens, CHUNK)]
    parts = [slice(low, low + HEAD) for low in range(0, width, HEAD)]
    first = (half[0] * pl.num_programs(0) + pl.program_id(0)) * len(parts)
    for at in range(len(parts)):
        rows[at] = weights[:, pl.ds(first + at, 1), :].reshape(levels, tokens)
    flipped = turned(values[...])

    def row(at, level, low, size):
        return rows[at, level : level + 1, low : low + size]

    nodes = []
    for part in parts:
        line = [product(flipped[part, span], keys[span, part]) for span in (spans if state else spans[:-1])]
        if state:
            state[0][part, :] = functools.reduce(jnp.add, line)
        known = [line]
        while len(known[-1]) > 1:
            below = known[-1]
            known.append([below[at] + below[at + 1] for at in range(0, len(below) - 1, 2)])
        nodes.append([[state.astype(BF16) for state in level] for level in known])
    scores = {}
    for at, part in enumerate(parts):
        for chunk, span in enumerate(spans):
            used = [bit for bit in range(bits_of(chunks)) if chunk >> bit & 1]
            left = [keys[span, part]] + [nodes[at][bit][(chunk >> bit) - 1] for bit in used]
            left = jnp.concatenate(left, axis=0) if used else left[0]
            scores[at, chunk] = product_nt(left, queries[span, part])
    for at, part in enumerate(parts):
        for chunk, span in enumerate(spans):
            low = chunk * CHUNK
            score = scores[at, chunk]
            lower, upper = (
                tile_mixing([row(at, level, start, TILE) for level in range(top)]) for start in (low, low + TILE)
            )
            across = row(at, top, low + TILE, TILE)
            weighted = jnp.concatenate(
                [
                    jnp.concatenate([score[:TILE, :TILE] * lower, score[:TILE, TILE:] * across], axis=1),
                    jnp.concatenate([jnp.zeros_like(lower), score[TILE:CHUNK, TILE:] * upper], axis=1),
                ],
                axis=0,
            ).astype(BF16)
            total = product(flipped[part, span], weighted)
            below = CHUNK
            for bit in range(bits_of(chunks)):
                if chunk >> bit & 1:
                    total = total + row(at, top + 1 + bit, low, CHUNK) * score[below : below + HEAD, :]
                    below += HEAD
            local[part, span] = total.astype(BF16)


def local_part(half, with_state, queries, keys, values, level_weights):
    tokens, width = queries.shape
    step = 2 * HEAD
    steps = width // step // 2
    levels = LOCAL_BITS + 1
    column = pl.BlockSpec((tokens, step), lambda pair, half: (0, half[0] * steps + pair))
    return pl.pallas_call(
        local_kernel,
        grid_spec=pltpu.PrefetchScalarGridSpec(
            num_scalar_prefetch=1,
            grid=(steps,),
            in_specs=[column, column, column, pl.BlockSpec((levels,) + level_weights.shape[1:], lambda pair, half: (0, 0, 0))],
            out_specs=[
                pl.BlockSpec((step, tokens), lambda pair, half: (pair, 0)),
                pl.BlockSpec((step, HEAD), lambda pair, half: (pair, 0)),
            ][: 1 + with_state],
            scratch_shapes=[pltpu.VMEM((2, levels, tokens), F32)],
        ),
        out_shape=[pltpu.HBM((width // 2, tokens), BF16), pltpu.VMEM((width // 2, HEAD), F32)][: 1 + with_state],
        cost_estimate=cost(tokens * width, MIB // 4),
        compiler_params=params(16),
    )(half.reshape(1), queries, keys, values, level_weights)


def has_bit(place, bit):
    return jnp.bitwise_and(jnp.right_shift(place, bit), 1) == 1


def near_kernel(aliased, half, place, queries, weights, local, *rest):
    *held, near, states, rows = rest[aliased:]
    step = pl.program_id(0)
    bits = states.shape[1] // HEAD
    size = states.shape[0] * HEAD // 2

    def quarter_state(bit, quarter, slot):
        if len(held) == 1:
            return held[0][2 * bit + slot]
        if bit == 0:
            return held[0][quarter * size : (quarter + 1) * size, :]
        return jnp.where(slot == 0, held[2 * bit - 1][...], held[2 * bit][...])

    @pl.when(step == 0)
    def _():
        side = jnp.bitwise_and(jnp.right_shift(place[0], 1), 1)
        for quarter in range(2):
            slot = jnp.bitwise_xor(side, quarter)
            for bit in range(bits):
                state = jnp.where(has_bit(place[0], bit), quarter_state(bit, quarter, slot), 0.0).astype(BF16)
                for at in range(0, size, HEAD):
                    states[(quarter * size + at) // HEAD, bit * HEAD : (bit + 1) * HEAD, :] = state[at : at + HEAD]

    for at in range(rows.shape[0]):
        part = slice(at * HEAD, (at + 1) * HEAD)
        head = step * rows.shape[0] + at
        rows[at] = weights[:, pl.ds(half[0] * states.shape[0] + head, 1), :].reshape(rows.shape[1:])
        products = product_nt(states[head], queries[:, part])
        total = local[part, :].astype(F32)
        for bit in range(bits):
            level = LOCAL_BITS + 1 + bit
            total = total + rows[at, level : level + 1, :] * products[bit * HEAD : (bit + 1) * HEAD]
        near[part, :] = total


def near_part(half, place, bits, queries, level_weights, local, into, *held):
    tokens, width = queries.shape
    heads = width // HEAD // 2
    step = 2 * HEAD
    steps = width // step // 2
    into = () if into is None else (pltpu.with_memory_space_constraint(into, pltpu.VMEM),)
    return pl.pallas_call(
        functools.partial(near_kernel, len(into)),
        grid_spec=pltpu.PrefetchScalarGridSpec(
            num_scalar_prefetch=2,
            grid=(steps,),
            in_specs=[
                pl.BlockSpec((tokens, step), lambda pair, half, place: (0, half[0] * steps + pair)),
                pl.BlockSpec(level_weights.shape, lambda pair, half, place: (0, 0, 0)),
                pl.BlockSpec((step, tokens), lambda pair, half, place: (pair, 0)),
                *[pl.BlockSpec(memory_space=pltpu.VMEM)] * len(into),
                *[
                    pl.BlockSpec(
                        (2 * bits,) + part.shape[1:] if part.ndim == 3 else part.shape,
                        lambda pair, half, place, rank=part.ndim: (0,) * rank,
                    )
                    for part in held
                ],
            ],
            out_specs=pl.BlockSpec((step, tokens), lambda pair, half, place: (half[0] * steps + pair, 0)),
            scratch_shapes=[
                pltpu.VMEM((heads, bits * HEAD, HEAD), BF16),
                pltpu.VMEM((2, level_weights.shape[0], tokens), F32),
            ],
        ),
        out_shape=pltpu.VMEM((width, tokens), F32),
        input_output_aliases={5: 0} if into else {},
        cost_estimate=cost(tokens * width, MIB // 4),
        compiler_params=params(16),
    )(half.reshape(1), place, *outside(queries, level_weights, local), *into, *held)


def far_kernel(first_level, place, queries, weights, near, early, early_other, late, late_other, out_weight,
               mixed, states, flipped, attended):
    rows, width = attended.shape
    bits = states.shape[1] // HEAD
    size = late.shape[0]
    skip = early.shape[0] + 1 - 2 * bits
    core = jnp.bitwise_and(place[0], 1)

    @pl.when(pl.program_id(0) == 0)
    def _():
        side = jnp.bitwise_and(jnp.right_shift(place[0], 1), 1)
        for bit in range(bits):
            mine, other = ([part[skip + 2 * bit], part[skip + 2 * bit + 1] if bit + 1 < bits else final[...]]
                           for part, final in ((early, late), (early_other, late_other)))
            for quarter in range(4):
                here, there = (jnp.where(side == quarter % 2, *part) for part in (mine, other))
                state = jnp.where(core == quarter // 2, here, there)
                state = jnp.where(has_bit(place[1], bit), state, 0.0).astype(BF16)
                for at in range(0, size, HEAD):
                    head = (quarter * size + at) // HEAD
                    states[head, bit * HEAD : (bit + 1) * HEAD, :] = state[at : at + HEAD]

    for half in range(2):
        for low in range(0, width // 2, HEAD):
            part = slice(half * (width // 2) + low, half * (width // 2) + low + HEAD)
            head = part.start // HEAD
            products = product_nt(states[head], queries[:, part])
            total = near[part, :]
            for bit in range(bits):
                row = weights[first_level + bit, head : head + 1, :]
                total = total + row * products[bit * HEAD : (bit + 1) * HEAD]
            flipped[part, :] = total.astype(BF16)
    unit = identity(CHUNK)
    for top in range(0, rows, CHUNK):
        for low in range(0, width, CHUNK):
            block = flipped[low : low + CHUNK, top : top + CHUNK]
            attended[top : top + CHUNK, low : low + CHUNK] = product_nt(unit, block).astype(BF16)
    mixed[...] = product(attended[...], out_weight[...]).astype(BF16)


def far_part(first_level, bits, place, queries, level_weights, near, *fixed):
    tokens, width = queries.shape
    rows = min(2 * CHUNK, tokens)
    band = pl.BlockSpec((rows, width), lambda step: (step, 0))

    def tail(part):
        count = 2 * bits - 1
        if part.ndim == 3 and part.shape[0] % count == 0:
            last = part.shape[0] // count - 1
            return pl.BlockSpec((count,) + part.shape[1:], lambda step: (last, 0, 0))
        return pl.BlockSpec(part.shape, lambda step: (0,) * part.ndim)

    return pl.pallas_call(
        functools.partial(far_kernel, first_level),
        grid=(tokens // rows,),
        in_specs=[
            pl.BlockSpec(memory_space=pltpu.SMEM),
            band,
            pl.BlockSpec(level_weights.shape[:2] + (rows,), lambda step: (0, 0, step)),
            pl.BlockSpec((width, rows), lambda step: (0, step)),
            *[tail(part) for part in fixed],
        ],
        out_specs=band,
        out_shape=jax.ShapeDtypeStruct((tokens, width), BF16),
        scratch_shapes=[
            pltpu.VMEM((width // HEAD, bits * HEAD, HEAD), BF16),
            pltpu.VMEM((width, rows), BF16),
            pltpu.VMEM((rows, width), BF16),
        ],
        cost_estimate=cost(2 * tokens * width * (width + bits * HEAD), 12 * MIB),
        compiler_params=params(28),
    )(place, queries, level_weights, near, *fixed)


def body(queries, keys, values, level_weights, out_weight):
    inner, outer = lax.axis_size("inner"), lax.axis_size("outer")
    inner_bits, outer_bits = bits_of(inner), bits_of(outer)
    inner_place, outer_place = lax.axis_index("inner"), lax.axis_index("outer")
    place = jnp.stack([inner_place, outer_place]).astype(jnp.int32)
    core = jnp.bitwise_and(inner_place, 1).astype(jnp.int32)
    side = jnp.bitwise_and(jnp.right_shift(inner_place, 1), 1)
    half = keys.shape[1] // 2
    quarter = half // 2
    tie = lax.optimization_barrier

    inputs = outside(keys, values)
    give = block_state(1 - core, 2, *inputs)
    give, inputs = tie((give, inputs))
    first = swap(give, "inner", 1)

    def quarter_of(at, state):
        return state + lax.dynamic_slice_in_dim(first, at * quarter, quarter, 0)

    keep_theirs = block_state(2 * core + 1 - side, 4, *inputs)
    passed = quarter_of(1 - side, keep_theirs)
    passed, inputs = tie((passed, inputs))
    buckets = [swap(passed, "inner", 2)]
    inputs = outside(queries, keys, values, level_weights)
    local = [None, None]
    local[0], keep = local_part(core, True, *inputs)
    keep_ours = lax.dynamic_slice_in_dim(keep, side * quarter, quarter, 0)
    own = quarter_of(side, keep_ours)
    running = own + buckets[0]
    running, inputs = tie((running, inputs))
    (local[1],) = local_part(1 - core, False, *inputs)
    for bit in range(2, inner_bits):
        arrived = swap(running, "inner", 1 << bit)
        if bit == 2:
            arrived, local = tie((arrived, local))
        buckets.append(arrived)
        running = running + arrived

    running, own, later = tie((running, own, buckets[1:]))
    far = [swap(running, "outer", 1)]
    others = [swap(part, "inner", 2) for part in (own, *later)]
    beside = []

    def own_near():
        held = [part for at, bucket in enumerate(buckets) for part in (bucket, others[at])]
        return near_part(core, place, inner_bits, queries, level_weights, local[0], None, first, *held)

    for bit in range(1, outer_bits):
        running = running + far[-1]
        far.append(swap(running, "outer", 1 << bit))
        beside.append(swap(far[-2], "inner", 2))
        if bit == 1:
            near_mine = own_near()
            far[-1], beside, others, near_mine = tie((far[-1], beside, others, near_mine))
    if outer_bits == 1:
        near_mine = own_near()
        far[-1], others, near_mine = tie((far[-1], others, near_mine))
    late = swap(far[-1], "inner", 2)
    pairs = [(keep_ours, keep_theirs), *((bucket, others[at]) for at, bucket in enumerate(buckets)), *zip(far, beside)]
    mine = jnp.stack([part for pair in pairs for part in pair] + far[-1:])
    other = swap(mine, "inner", 1)
    near = near_part(1 - core, place, inner_bits, queries, level_weights, local[1], near_mine, other)
    late, near = tie((late, near))
    late_other = swap(late, "inner", 1)
    first_level = LOCAL_BITS + 1 + inner_bits
    return far_part(
        first_level, outer_bits, place, queries, level_weights, near, mine, other, late, late_other, out_weight
    )


def solution(mesh):
    spec = P(("outer", "inner"), None)
    in_specs = (spec, spec, spec, P(None, None, ("outer", "inner")), P())
    return jax.shard_map(body, mesh=mesh, in_specs=in_specs, out_specs=spec, check_vma=False)
```

```python
import functools

import jax
import jax.numpy as jnp
from jax import lax
from jax.experimental import pallas as pl
from jax.experimental.pallas import tpu as pltpu
from jax.sharding import PartitionSpec as P

HEADS = 8
HEAD = 128
LOCAL_BITS = 10
TILE = 128
CHUNK = 256
F32 = jnp.float32
BF16 = jnp.bfloat16
MIB = 1 << 20


def bits_of(count):
    return count.bit_length() - 1


def swap(block, axis, stride):
    count = lax.axis_size(axis)
    return lax.ppermute(block, axis, [(place, place ^ stride) for place in range(count)])


def raise_to(block, axis, stride):
    count = lax.axis_size(axis)
    route = [(place, place | stride) for place in range(count) if not place & stride]
    return lax.ppermute(block, axis, route)


def cost(flops, moved):
    return pl.CostEstimate(flops=flops, bytes_accessed=moved, transcendentals=0)


def params(limit):
    return pltpu.CompilerParams(vmem_limit_bytes=limit * MIB)


def outside(*parts):
    return tuple(pltpu.with_memory_space_constraint(part, pltpu.HBM) for part in parts)


def product(left, right):
    return jnp.dot(left, right, preferred_element_type=F32)


def product_nt(left, right):
    return lax.dot_general(left, right, (((1,), (1,)), ((), ())), preferred_element_type=F32)


def identity(size):
    row = lax.broadcasted_iota(jnp.int32, (size, size), 0)
    column = lax.broadcasted_iota(jnp.int32, (size, size), 1)
    return (row == column).astype(F32).astype(BF16)


def turned(block):
    return product_nt(identity(block.shape[1]), block).astype(BF16)


def state_kernel(place, keys, values, state):
    both = product(turned(values[...]), keys[...])
    for low in range(0, keys.shape[1], HEAD):
        part = slice(low, low + HEAD)
        state[part, :] = both[part, part]


def block_state(place, share, keys, values):
    tokens, width = keys.shape
    step = 2 * HEAD
    steps = width // share // step
    column = pl.BlockSpec((tokens, step), lambda pair, place: (0, place[0] * steps + pair))
    return pl.pallas_call(
        state_kernel,
        grid_spec=pltpu.PrefetchScalarGridSpec(
            num_scalar_prefetch=1,
            grid=(steps,),
            in_specs=[column, column],
            out_specs=pl.BlockSpec((step, HEAD), lambda pair, place: (pair, 0)),
        ),
        out_shape=pltpu.VMEM((width // share, HEAD), F32),
        cost_estimate=cost(2 * tokens * width * HEAD // share, 5 * MIB // share),
        compiler_params=params(16),
    )(place.reshape(1).astype(jnp.int32), keys, values)


def tile_mixing(rows):
    target = lax.broadcasted_iota(jnp.int32, (8, TILE), 1)
    source = lax.broadcasted_iota(jnp.int32, (8, TILE), 0)
    rows = [jnp.broadcast_to(row, (8, TILE)) for row in rows]
    within = jnp.bitwise_and(target, 7)
    differ = jnp.bitwise_xor(within, source)
    base = rows[3]
    for level in (2, 1, 0):
        base = jnp.where(differ < 1 << level, rows[level], base)
    parts = [jnp.where(source <= within, base, 0.0)]
    for bit in range(3, bits_of(TILE)):
        upper = jnp.bitwise_and(jnp.right_shift(target, bit), 1) == 1
        parts = [jnp.where(upper, rows[bit + 1], part) for part in parts] + [
            jnp.where(upper, part, 0.0) for part in parts
        ]
    return jnp.concatenate(parts, axis=0)


def local_kernel(half, queries, keys, values, weights, local, *rest):
    *state, rows = rest
    tokens, width = queries.shape
    chunks = tokens // CHUNK
    levels = rows.shape[1]
    top = bits_of(CHUNK)
    spans = [slice(low, low + CHUNK) for low in range(0, tokens, CHUNK)]
    parts = [slice(low, low + HEAD) for low in range(0, width, HEAD)]
    first = (half[0] * pl.num_programs(0) + pl.program_id(0)) * len(parts)
    for at in range(len(parts)):
        rows[at] = weights[:, pl.ds(first + at, 1), :].reshape(levels, tokens)
    flipped = turned(values[...])

    def row(at, level, low, size):
        return rows[at, level : level + 1, low : low + size]

    nodes = []
    for part in parts:
        line = [product(flipped[part, span], keys[span, part]) for span in (spans if state else spans[:-1])]
        if state:
            state[0][part, :] = functools.reduce(jnp.add, line)
        known = [line]
        while len(known[-1]) > 1:
            below = known[-1]
            known.append([below[at] + below[at + 1] for at in range(0, len(below) - 1, 2)])
        nodes.append([[state.astype(BF16) for state in level] for level in known])
    scores = {}
    for at, part in enumerate(parts):
        for chunk, span in enumerate(spans):
            used = [bit for bit in range(bits_of(chunks)) if chunk >> bit & 1]
            left = [keys[span, part]] + [nodes[at][bit][(chunk >> bit) - 1] for bit in used]
            left = jnp.concatenate(left, axis=0) if used else left[0]
            scores[at, chunk] = product_nt(left, queries[span, part])
    for at, part in enumerate(parts):
        for chunk, span in enumerate(spans):
            low = chunk * CHUNK
            score = scores[at, chunk]
            lower, upper = (
                tile_mixing([row(at, level, start, TILE) for level in range(top)]) for start in (low, low + TILE)
            )
            across = row(at, top, low + TILE, TILE)
            weighted = jnp.concatenate(
                [
                    jnp.concatenate([score[:TILE, :TILE] * lower, score[:TILE, TILE:] * across], axis=1),
                    jnp.concatenate([jnp.zeros_like(lower), score[TILE:CHUNK, TILE:] * upper], axis=1),
                ],
                axis=0,
            ).astype(BF16)
            total = product(flipped[part, span], weighted)
            below = CHUNK
            for bit in range(bits_of(chunks)):
                if chunk >> bit & 1:
                    total = total + row(at, top + 1 + bit, low, CHUNK) * score[below : below + HEAD, :]
                    below += HEAD
            local[part, span] = total.astype(BF16)


def local_part(half, with_state, queries, keys, values, level_weights):
    tokens, width = queries.shape
    step = 2 * HEAD
    steps = width // step // 2
    levels = LOCAL_BITS + 1
    column = pl.BlockSpec((tokens, step), lambda pair, half: (0, half[0] * steps + pair))
    return pl.pallas_call(
        local_kernel,
        grid_spec=pltpu.PrefetchScalarGridSpec(
            num_scalar_prefetch=1,
            grid=(steps,),
            in_specs=[column, column, column, pl.BlockSpec((levels,) + level_weights.shape[1:], lambda pair, half: (0, 0, 0))],
            out_specs=[
                pl.BlockSpec((step, tokens), lambda pair, half: (pair, 0)),
                pl.BlockSpec((step, HEAD), lambda pair, half: (pair, 0)),
            ][: 1 + with_state],
            scratch_shapes=[pltpu.VMEM((2, levels, tokens), F32)],
        ),
        out_shape=[pltpu.HBM((width // 2, tokens), BF16), pltpu.VMEM((width // 2, HEAD), F32)][: 1 + with_state],
        cost_estimate=cost(tokens * width, MIB // 4),
        compiler_params=params(16),
    )(half.reshape(1), queries, keys, values, level_weights)


def has_bit(place, bit):
    return jnp.bitwise_and(jnp.right_shift(place, bit), 1) == 1


def near_kernel(aliased, half, place, queries, weights, local, *rest):
    *held, near, states, rows = rest[aliased:]
    step = pl.program_id(0)
    bits = states.shape[1] // HEAD
    size = states.shape[0] * HEAD // 2

    def quarter_state(bit, quarter, slot):
        if len(held) == 1:
            return held[0][2 * bit + slot]
        if bit == 0:
            return held[0][quarter * size : (quarter + 1) * size, :]
        return jnp.where(slot == 0, held[2 * bit - 1][...], held[2 * bit][...])

    @pl.when(step == 0)
    def _():
        side = jnp.bitwise_and(jnp.right_shift(place[0], 1), 1)
        for quarter in range(2):
            slot = jnp.bitwise_xor(side, quarter)
            for bit in range(bits):
                state = jnp.where(has_bit(place[0], bit), quarter_state(bit, quarter, slot), 0.0).astype(BF16)
                for at in range(0, size, HEAD):
                    states[(quarter * size + at) // HEAD, bit * HEAD : (bit + 1) * HEAD, :] = state[at : at + HEAD]

    for at in range(rows.shape[0]):
        part = slice(at * HEAD, (at + 1) * HEAD)
        head = step * rows.shape[0] + at
        rows[at] = weights[:, pl.ds(half[0] * states.shape[0] + head, 1), :].reshape(rows.shape[1:])
        products = product_nt(states[head], queries[:, part])
        total = local[part, :].astype(F32)
        for bit in range(bits):
            level = LOCAL_BITS + 1 + bit
            total = total + rows[at, level : level + 1, :] * products[bit * HEAD : (bit + 1) * HEAD]
        near[part, :] = total


def near_part(half, place, bits, queries, level_weights, local, into, *held):
    tokens, width = queries.shape
    heads = width // HEAD // 2
    step = 2 * HEAD
    steps = width // step // 2
    into = () if into is None else (pltpu.with_memory_space_constraint(into, pltpu.VMEM),)
    return pl.pallas_call(
        functools.partial(near_kernel, len(into)),
        grid_spec=pltpu.PrefetchScalarGridSpec(
            num_scalar_prefetch=2,
            grid=(steps,),
            in_specs=[
                pl.BlockSpec((tokens, step), lambda pair, half, place: (0, half[0] * steps + pair)),
                pl.BlockSpec(level_weights.shape, lambda pair, half, place: (0, 0, 0)),
                pl.BlockSpec((step, tokens), lambda pair, half, place: (pair, 0)),
                *[pl.BlockSpec(memory_space=pltpu.VMEM)] * len(into),
                *[
                    pl.BlockSpec(
                        (2 * bits,) + part.shape[1:] if part.ndim == 3 else part.shape,
                        lambda pair, half, place, rank=part.ndim: (0,) * rank,
                    )
                    for part in held
                ],
            ],
            out_specs=pl.BlockSpec((step, tokens), lambda pair, half, place: (half[0] * steps + pair, 0)),
            scratch_shapes=[
                pltpu.VMEM((heads, bits * HEAD, HEAD), BF16),
                pltpu.VMEM((2, level_weights.shape[0], tokens), F32),
            ],
        ),
        out_shape=pltpu.VMEM((width, tokens), F32),
        input_output_aliases={5: 0} if into else {},
        cost_estimate=cost(tokens * width, MIB // 4),
        compiler_params=params(16),
    )(half.reshape(1), place, *outside(queries, level_weights, local), *into, *held)


def far_kernel(first_level, place, queries, weights, near, early, early_other, late, late_other, out_weight,
               mixed, states, flipped, attended):
    rows, width = attended.shape
    bits = states.shape[1] // HEAD
    size = late.shape[0]
    skip = early.shape[0] + 1 - 2 * bits
    core = jnp.bitwise_and(place[0], 1)

    @pl.when(pl.program_id(0) == 0)
    def _():
        side = jnp.bitwise_and(jnp.right_shift(place[0], 1), 1)
        for bit in range(bits):
            mine, other = ([part[skip + 2 * bit], part[skip + 2 * bit + 1] if bit + 1 < bits else final[...]]
                           for part, final in ((early, late), (early_other, late_other)))
            for quarter in range(4):
                here, there = (jnp.where(side == quarter % 2, *part) for part in (mine, other))
                state = jnp.where(core == quarter // 2, here, there)
                state = jnp.where(has_bit(place[1], bit), state, 0.0).astype(BF16)
                for at in range(0, size, HEAD):
                    head = (quarter * size + at) // HEAD
                    states[head, bit * HEAD : (bit + 1) * HEAD, :] = state[at : at + HEAD]

    for half in range(2):
        for low in range(0, width // 2, HEAD):
            part = slice(half * (width // 2) + low, half * (width // 2) + low + HEAD)
            head = part.start // HEAD
            products = product_nt(states[head], queries[:, part])
            total = near[part, :]
            for bit in range(bits):
                row = weights[first_level + bit, head : head + 1, :]
                total = total + row * products[bit * HEAD : (bit + 1) * HEAD]
            flipped[part, :] = total.astype(BF16)
    unit = identity(CHUNK)
    for top in range(0, rows, CHUNK):
        for low in range(0, width, CHUNK):
            block = flipped[low : low + CHUNK, top : top + CHUNK]
            attended[top : top + CHUNK, low : low + CHUNK] = product_nt(unit, block).astype(BF16)
    mixed[...] = product(attended[...], out_weight[...]).astype(BF16)


def far_part(first_level, bits, place, queries, level_weights, near, *fixed):
    tokens, width = queries.shape
    rows = min(2 * CHUNK, tokens)
    band = pl.BlockSpec((rows, width), lambda step: (step, 0))

    def tail(part):
        count = 2 * bits - 1
        if part.ndim == 3 and part.shape[0] % count == 0:
            last = part.shape[0] // count - 1
            return pl.BlockSpec((count,) + part.shape[1:], lambda step: (last, 0, 0))
        return pl.BlockSpec(part.shape, lambda step: (0,) * part.ndim)

    return pl.pallas_call(
        functools.partial(far_kernel, first_level),
        grid=(tokens // rows,),
        in_specs=[
            pl.BlockSpec(memory_space=pltpu.SMEM),
            band,
            pl.BlockSpec(level_weights.shape[:2] + (rows,), lambda step: (0, 0, step)),
            pl.BlockSpec((width, rows), lambda step: (0, step)),
            *[tail(part) for part in fixed],
        ],
        out_specs=band,
        out_shape=jax.ShapeDtypeStruct((tokens, width), BF16),
        scratch_shapes=[
            pltpu.VMEM((width // HEAD, bits * HEAD, HEAD), BF16),
            pltpu.VMEM((width, rows), BF16),
            pltpu.VMEM((rows, width), BF16),
        ],
        cost_estimate=cost(2 * tokens * width * (width + bits * HEAD), 12 * MIB),
        compiler_params=params(28),
    )(place, queries, level_weights, near, *fixed)


def body(queries, keys, values, level_weights, out_weight):
    inner, outer = lax.axis_size("inner"), lax.axis_size("outer")
    inner_bits, outer_bits = bits_of(inner), bits_of(outer)
    inner_place, outer_place = lax.axis_index("inner"), lax.axis_index("outer")
    place = jnp.stack([inner_place, outer_place]).astype(jnp.int32)
    core = jnp.bitwise_and(inner_place, 1).astype(jnp.int32)
    side = jnp.bitwise_and(jnp.right_shift(inner_place, 1), 1)
    half = keys.shape[1] // 2
    quarter = half // 2
    tie = lax.optimization_barrier

    inputs = outside(keys, values)
    give = block_state(1 - core, 2, *inputs)
    give, inputs = tie((give, inputs))
    first = swap(give, "inner", 1)

    def quarter_of(at, state):
        return state + lax.dynamic_slice_in_dim(first, at * quarter, quarter, 0)

    keep_theirs = block_state(2 * core + 1 - side, 4, *inputs)
    passed = quarter_of(1 - side, keep_theirs)
    passed, inputs = tie((passed, inputs))
    buckets = [swap(passed, "inner", 2)]
    inputs = outside(queries, keys, values, level_weights)
    local = [None, None]
    local[0], keep = local_part(core, True, *inputs)
    keep_ours = lax.dynamic_slice_in_dim(keep, side * quarter, quarter, 0)
    own = quarter_of(side, keep_ours)
    running = own + buckets[0]
    running, inputs = tie((running, inputs))
    (local[1],) = local_part(1 - core, False, *inputs)
    for bit in range(2, inner_bits):
        arrived = swap(running, "inner", 1 << bit)
        if bit == 2:
            arrived, local = tie((arrived, local))
        buckets.append(arrived)
        running = running + arrived

    running, own, later = tie((running, own, buckets[1:]))
    far = [swap(running, "outer", 1)]
    others = [swap(part, "inner", 2) for part in (own, *later)]
    beside = []

    def own_near():
        held = [part for at, bucket in enumerate(buckets) for part in (bucket, others[at])]
        return near_part(core, place, inner_bits, queries, level_weights, local[0], None, first, *held)

    for bit in range(1, outer_bits):
        running = running + far[-1]
        far.append(swap(running, "outer", 1 << bit))
        beside.append(swap(far[-2], "inner", 2))
        if bit == 1:
            near_mine = own_near()
            far[-1], beside, others, near_mine = tie((far[-1], beside, others, near_mine))
    if outer_bits == 1:
        near_mine = own_near()
        far[-1], others, near_mine = tie((far[-1], others, near_mine))
    late = swap(far[-1], "inner", 2)
    pairs = [(keep_ours, keep_theirs), *((bucket, others[at]) for at, bucket in enumerate(buckets))]
    other = swap(jnp.stack([part for pair in pairs for part in pair]), "inner", 1)
    early = jnp.stack([part for pair in zip(far, beside) for part in pair] + far[-1:])
    early_other = swap(early, "inner", 1)
    near = near_part(1 - core, place, inner_bits, queries, level_weights, local[1], near_mine, other)
    late, near, early_other = tie((late, near, early_other))
    late_other = swap(late, "inner", 1)
    first_level = LOCAL_BITS + 1 + inner_bits
    return far_part(
        first_level, outer_bits, place, queries, level_weights, near, early, early_other, late, late_other, out_weight
    )


def solution(mesh):
    spec = P(("outer", "inner"), None)
    in_specs = (spec, spec, spec, P(None, None, ("outer", "inner")), P())
    return jax.shard_map(body, mesh=mesh, in_specs=in_specs, out_specs=spec, check_vma=False)
```

```python
import functools

import jax
import jax.numpy as jnp
from jax import lax
from jax.experimental import pallas as pl
from jax.experimental.pallas import tpu as pltpu
from jax.sharding import PartitionSpec as P

HEADS = 8
HEAD = 128
LOCAL_BITS = 10
TILE = 128
CHUNK = 256
F32 = jnp.float32
BF16 = jnp.bfloat16
MIB = 1 << 20


def bits_of(count):
    return count.bit_length() - 1


def swap(block, axis, stride):
    count = lax.axis_size(axis)
    return lax.ppermute(block, axis, [(place, place ^ stride) for place in range(count)])


def raise_to(block, axis, stride):
    count = lax.axis_size(axis)
    route = [(place, place | stride) for place in range(count) if not place & stride]
    return lax.ppermute(block, axis, route)


def cost(flops, moved):
    return pl.CostEstimate(flops=flops, bytes_accessed=moved, transcendentals=0)


def params(limit):
    return pltpu.CompilerParams(vmem_limit_bytes=limit * MIB)


def outside(*parts):
    return tuple(pltpu.with_memory_space_constraint(part, pltpu.HBM) for part in parts)


def product(left, right):
    return jnp.dot(left, right, preferred_element_type=F32)


def product_nt(left, right):
    return lax.dot_general(left, right, (((1,), (1,)), ((), ())), preferred_element_type=F32)


def identity(size):
    row = lax.broadcasted_iota(jnp.int32, (size, size), 0)
    column = lax.broadcasted_iota(jnp.int32, (size, size), 1)
    return (row == column).astype(F32).astype(BF16)


def turned(block):
    return product_nt(identity(block.shape[1]), block).astype(BF16)


def state_kernel(place, keys, values, state):
    both = product(turned(values[...]), keys[...])
    for low in range(0, keys.shape[1], HEAD):
        part = slice(low, low + HEAD)
        state[part, :] = both[part, part]


def block_state(place, share, keys, values):
    tokens, width = keys.shape
    step = 2 * HEAD
    steps = width // share // step
    column = pl.BlockSpec((tokens, step), lambda pair, place: (0, place[0] * steps + pair))
    return pl.pallas_call(
        state_kernel,
        grid_spec=pltpu.PrefetchScalarGridSpec(
            num_scalar_prefetch=1,
            grid=(steps,),
            in_specs=[column, column],
            out_specs=pl.BlockSpec((step, HEAD), lambda pair, place: (pair, 0)),
        ),
        out_shape=pltpu.VMEM((width // share, HEAD), F32),
        cost_estimate=cost(2 * tokens * width * HEAD // share, 5 * MIB // share),
        compiler_params=params(16),
    )(place.reshape(1).astype(jnp.int32), keys, values)


def tile_mixing(rows):
    target = lax.broadcasted_iota(jnp.int32, (8, TILE), 1)
    source = lax.broadcasted_iota(jnp.int32, (8, TILE), 0)
    rows = [jnp.broadcast_to(row, (8, TILE)) for row in rows]
    within = jnp.bitwise_and(target, 7)
    differ = jnp.bitwise_xor(within, source)
    base = rows[3]
    for level in (2, 1, 0):
        base = jnp.where(differ < 1 << level, rows[level], base)
    parts = [jnp.where(source <= within, base, 0.0)]
    for bit in range(3, bits_of(TILE)):
        upper = jnp.bitwise_and(jnp.right_shift(target, bit), 1) == 1
        parts = [jnp.where(upper, rows[bit + 1], part) for part in parts] + [
            jnp.where(upper, part, 0.0) for part in parts
        ]
    return jnp.concatenate(parts, axis=0)


def local_kernel(half, queries, keys, values, weights, local, *rest):
    *state, rows = rest
    tokens, width = queries.shape
    chunks = tokens // CHUNK
    levels = rows.shape[1]
    top = bits_of(CHUNK)
    spans = [slice(low, low + CHUNK) for low in range(0, tokens, CHUNK)]
    parts = [slice(low, low + HEAD) for low in range(0, width, HEAD)]
    first = (half[0] * pl.num_programs(0) + pl.program_id(0)) * len(parts)
    for at in range(len(parts)):
        rows[at] = weights[:, pl.ds(first + at, 1), :].reshape(levels, tokens)
    flipped = turned(values[...])

    def row(at, level, low, size):
        return rows[at, level : level + 1, low : low + size]

    nodes = []
    for part in parts:
        line = [product(flipped[part, span], keys[span, part]) for span in (spans if state else spans[:-1])]
        if state:
            state[0][part, :] = functools.reduce(jnp.add, line)
        known = [line]
        while len(known[-1]) > 1:
            below = known[-1]
            known.append([below[at] + below[at + 1] for at in range(0, len(below) - 1, 2)])
        nodes.append([[state.astype(BF16) for state in level] for level in known])
    scores = {}
    for at, part in enumerate(parts):
        for chunk, span in enumerate(spans):
            used = [bit for bit in range(bits_of(chunks)) if chunk >> bit & 1]
            left = [keys[span, part]] + [nodes[at][bit][(chunk >> bit) - 1] for bit in used]
            left = jnp.concatenate(left, axis=0) if used else left[0]
            scores[at, chunk] = product_nt(left, queries[span, part])
    for at, part in enumerate(parts):
        for chunk, span in enumerate(spans):
            low = chunk * CHUNK
            score = scores[at, chunk]
            lower, upper = (
                tile_mixing([row(at, level, start, TILE) for level in range(top)]) for start in (low, low + TILE)
            )
            across = row(at, top, low + TILE, TILE)
            weighted = jnp.concatenate(
                [
                    jnp.concatenate([score[:TILE, :TILE] * lower, score[:TILE, TILE:] * across], axis=1),
                    jnp.concatenate([jnp.zeros_like(lower), score[TILE:CHUNK, TILE:] * upper], axis=1),
                ],
                axis=0,
            ).astype(BF16)
            total = product(flipped[part, span], weighted)
            below = CHUNK
            for bit in range(bits_of(chunks)):
                if chunk >> bit & 1:
                    total = total + row(at, top + 1 + bit, low, CHUNK) * score[below : below + HEAD, :]
                    below += HEAD
            local[part, span] = total.astype(BF16)


def local_part(half, with_state, queries, keys, values, level_weights):
    tokens, width = queries.shape
    step = 2 * HEAD
    steps = width // step // 2
    levels = LOCAL_BITS + 1
    column = pl.BlockSpec((tokens, step), lambda pair, half: (0, half[0] * steps + pair))
    return pl.pallas_call(
        local_kernel,
        grid_spec=pltpu.PrefetchScalarGridSpec(
            num_scalar_prefetch=1,
            grid=(steps,),
            in_specs=[column, column, column, pl.BlockSpec((levels,) + level_weights.shape[1:], lambda pair, half: (0, 0, 0))],
            out_specs=[
                pl.BlockSpec((step, tokens), lambda pair, half: (pair, 0)),
                pl.BlockSpec((step, HEAD), lambda pair, half: (pair, 0)),
            ][: 1 + with_state],
            scratch_shapes=[pltpu.VMEM((2, levels, tokens), F32)],
        ),
        out_shape=[pltpu.HBM((width // 2, tokens), BF16), pltpu.VMEM((width // 2, HEAD), F32)][: 1 + with_state],
        cost_estimate=cost(tokens * width, MIB // 4),
        compiler_params=params(16),
    )(half.reshape(1), queries, keys, values, level_weights)


def has_bit(place, bit):
    return jnp.bitwise_and(jnp.right_shift(place, bit), 1) == 1


def near_kernel(aliased, lowest, half, place, queries, weights, local, *rest):
    *held, near, states, rows = rest[aliased:]
    step = pl.program_id(0)
    bits = states.shape[1] // HEAD
    size = states.shape[0] * HEAD // 2

    def quarter_state(bit, quarter, slot):
        if len(held) == 1:
            return held[0][2 * bit + slot]
        if bit == 0:
            return held[0][quarter * size : (quarter + 1) * size, :]
        return jnp.where(slot == 0, held[2 * bit - 1][...], held[2 * bit][...])

    @pl.when(step == 0)
    def _():
        side = jnp.bitwise_and(jnp.right_shift(place[0], 1), 1)
        for quarter in range(2):
            slot = jnp.bitwise_xor(side, quarter)
            for bit in range(bits):
                state = jnp.where(has_bit(place[0], bit), quarter_state(bit, quarter, slot), 0.0).astype(BF16)
                for at in range(0, size, HEAD):
                    states[(quarter * size + at) // HEAD, bit * HEAD : (bit + 1) * HEAD, :] = state[at : at + HEAD]

    for at in range(rows.shape[0]):
        part = slice(at * HEAD, (at + 1) * HEAD)
        head = step * rows.shape[0] + at
        rows[at] = weights[:, pl.ds(half[0] * states.shape[0] + head, 1), :].reshape(rows.shape[1:])
        products = product_nt(states[head], queries[:, part])
        total = local[part, :].astype(F32)
        for bit in range(bits):
            level = LOCAL_BITS + 1 + bit - lowest
            total = total + rows[at, level : level + 1, :] * products[bit * HEAD : (bit + 1) * HEAD]
        near[part, :] = total


def level_block(level_weights, first, count):
    size = 8
    lowest = first // size * size
    if first + count <= lowest + size <= level_weights.shape[0]:
        return lowest, size
    return 0, level_weights.shape[0]


def near_part(half, place, bits, queries, level_weights, local, into, *held):
    tokens, width = queries.shape
    heads = width // HEAD // 2
    step = 2 * HEAD
    steps = width // step // 2
    lowest, levels = level_block(level_weights, LOCAL_BITS + 1, bits)
    into = () if into is None else (pltpu.with_memory_space_constraint(into, pltpu.VMEM),)
    return pl.pallas_call(
        functools.partial(near_kernel, len(into), lowest),
        grid_spec=pltpu.PrefetchScalarGridSpec(
            num_scalar_prefetch=2,
            grid=(steps,),
            in_specs=[
                pl.BlockSpec((tokens, step), lambda pair, half, place: (0, half[0] * steps + pair)),
                pl.BlockSpec((levels,) + level_weights.shape[1:], lambda pair, half, place: (lowest // levels, 0, 0)),
                pl.BlockSpec((step, tokens), lambda pair, half, place: (pair, 0)),
                *[pl.BlockSpec(memory_space=pltpu.VMEM)] * len(into),
                *[
                    pl.BlockSpec(
                        (2 * bits,) + part.shape[1:] if part.ndim == 3 else part.shape,
                        lambda pair, half, place, rank=part.ndim: (0,) * rank,
                    )
                    for part in held
                ],
            ],
            out_specs=pl.BlockSpec((step, tokens), lambda pair, half, place: (half[0] * steps + pair, 0)),
            scratch_shapes=[
                pltpu.VMEM((heads, bits * HEAD, HEAD), BF16),
                pltpu.VMEM((2, levels, tokens), F32),
            ],
        ),
        out_shape=pltpu.VMEM((width, tokens), F32),
        input_output_aliases={5: 0} if into else {},
        cost_estimate=cost(tokens * width, MIB // 4),
        compiler_params=params(16),
    )(half.reshape(1), place, *outside(queries, level_weights, local), *into, *held)


def far_kernel(first_level, place, queries, weights, near, early, early_other, late, late_other, out_weight,
               mixed, states, flipped, attended):
    rows, width = attended.shape
    bits = states.shape[1] // HEAD
    size = late.shape[0]
    skip = early.shape[0] + 1 - 2 * bits
    core = jnp.bitwise_and(place[0], 1)

    @pl.when(pl.program_id(0) == 0)
    def _():
        side = jnp.bitwise_and(jnp.right_shift(place[0], 1), 1)
        for bit in range(bits):
            mine, other = ([part[skip + 2 * bit], part[skip + 2 * bit + 1] if bit + 1 < bits else final[...]]
                           for part, final in ((early, late), (early_other, late_other)))
            for quarter in range(4):
                here, there = (jnp.where(side == quarter % 2, *part) for part in (mine, other))
                state = jnp.where(core == quarter // 2, here, there)
                state = jnp.where(has_bit(place[1], bit), state, 0.0).astype(BF16)
                for at in range(0, size, HEAD):
                    head = (quarter * size + at) // HEAD
                    states[head, bit * HEAD : (bit + 1) * HEAD, :] = state[at : at + HEAD]

    for half in range(2):
        for low in range(0, width // 2, HEAD):
            part = slice(half * (width // 2) + low, half * (width // 2) + low + HEAD)
            head = part.start // HEAD
            products = product_nt(states[head], queries[:, part])
            total = near[part, :]
            for bit in range(bits):
                row = weights[first_level + bit, head : head + 1, :]
                total = total + row * products[bit * HEAD : (bit + 1) * HEAD]
            flipped[part, :] = total.astype(BF16)
    unit = identity(CHUNK)
    for top in range(0, rows, CHUNK):
        for low in range(0, width, CHUNK):
            block = flipped[low : low + CHUNK, top : top + CHUNK]
            attended[top : top + CHUNK, low : low + CHUNK] = product_nt(unit, block).astype(BF16)
    mixed[...] = product(attended[...], out_weight[...]).astype(BF16)


def far_part(first_level, bits, place, queries, level_weights, near, *fixed):
    tokens, width = queries.shape
    rows = min(2 * CHUNK, tokens)
    band = pl.BlockSpec((rows, width), lambda step: (step, 0))

    def tail(part):
        count = 2 * bits - 1
        if part.ndim == 3 and part.shape[0] % count == 0:
            last = part.shape[0] // count - 1
            return pl.BlockSpec((count,) + part.shape[1:], lambda step: (last, 0, 0))
        return pl.BlockSpec(part.shape, lambda step: (0,) * part.ndim)

    return pl.pallas_call(
        functools.partial(far_kernel, first_level),
        grid=(tokens // rows,),
        in_specs=[
            pl.BlockSpec(memory_space=pltpu.SMEM),
            band,
            pl.BlockSpec(level_weights.shape[:2] + (rows,), lambda step: (0, 0, step)),
            pl.BlockSpec((width, rows), lambda step: (0, step)),
            *[tail(part) for part in fixed],
        ],
        out_specs=band,
        out_shape=jax.ShapeDtypeStruct((tokens, width), BF16),
        scratch_shapes=[
            pltpu.VMEM((width // HEAD, bits * HEAD, HEAD), BF16),
            pltpu.VMEM((width, rows), BF16),
            pltpu.VMEM((rows, width), BF16),
        ],
        cost_estimate=cost(2 * tokens * width * (width + bits * HEAD), 12 * MIB),
        compiler_params=params(28),
    )(place, queries, level_weights, near, *fixed)


def body(queries, keys, values, level_weights, out_weight):
    inner, outer = lax.axis_size("inner"), lax.axis_size("outer")
    inner_bits, outer_bits = bits_of(inner), bits_of(outer)
    inner_place, outer_place = lax.axis_index("inner"), lax.axis_index("outer")
    place = jnp.stack([inner_place, outer_place]).astype(jnp.int32)
    core = jnp.bitwise_and(inner_place, 1).astype(jnp.int32)
    side = jnp.bitwise_and(jnp.right_shift(inner_place, 1), 1)
    half = keys.shape[1] // 2
    quarter = half // 2
    tie = lax.optimization_barrier

    inputs = outside(keys, values)
    give = block_state(1 - core, 2, *inputs)
    give, inputs = tie((give, inputs))
    first = swap(give, "inner", 1)

    def quarter_of(at, state):
        return state + lax.dynamic_slice_in_dim(first, at * quarter, quarter, 0)

    keep_theirs = block_state(2 * core + 1 - side, 4, *inputs)
    passed = quarter_of(1 - side, keep_theirs)
    passed, inputs = tie((passed, inputs))
    buckets = [swap(passed, "inner", 2)]
    inputs = outside(queries, keys, values, level_weights)
    local = [None, None]
    local[0], keep = local_part(core, True, *inputs)
    keep_ours = lax.dynamic_slice_in_dim(keep, side * quarter, quarter, 0)
    own = quarter_of(side, keep_ours)
    running = own + buckets[0]
    running, inputs = tie((running, inputs))
    (local[1],) = local_part(1 - core, False, *inputs)
    for bit in range(2, inner_bits):
        arrived = swap(running, "inner", 1 << bit)
        if bit == 2:
            arrived, local = tie((arrived, local))
        buckets.append(arrived)
        running = running + arrived

    running, own, later = tie((running, own, buckets[1:]))
    far = [swap(running, "outer", 1)]
    others = [swap(part, "inner", 2) for part in (own, *later)]
    beside = []

    def own_near():
        held = [part for at, bucket in enumerate(buckets) for part in (bucket, others[at])]
        return near_part(core, place, inner_bits, queries, level_weights, local[0], None, first, *held)

    for bit in range(1, outer_bits):
        running = running + far[-1]
        far.append(swap(running, "outer", 1 << bit))
        beside.append(swap(far[-2], "inner", 2))
        if bit == 1:
            near_mine = own_near()
            far[-1], beside, others, near_mine = tie((far[-1], beside, others, near_mine))
    if outer_bits == 1:
        near_mine = own_near()
        far[-1], others, near_mine = tie((far[-1], others, near_mine))
    late = swap(far[-1], "inner", 2)
    pairs = [(keep_ours, keep_theirs), *((bucket, others[at]) for at, bucket in enumerate(buckets))]
    other = swap(jnp.stack([part for pair in pairs for part in pair]), "inner", 1)
    early = jnp.stack([part for pair in zip(far, beside) for part in pair] + far[-1:])
    early_other = swap(early, "inner", 1)
    near = near_part(1 - core, place, inner_bits, queries, level_weights, local[1], near_mine, other)
    late, near, early_other = tie((late, near, early_other))
    late_other = swap(late, "inner", 1)
    first_level = LOCAL_BITS + 1 + inner_bits
    return far_part(
        first_level, outer_bits, place, queries, level_weights, near, early, early_other, late, late_other, out_weight
    )


def solution(mesh):
    spec = P(("outer", "inner"), None)
    in_specs = (spec, spec, spec, P(None, None, ("outer", "inner")), P())
    return jax.shard_map(body, mesh=mesh, in_specs=in_specs, out_specs=spec, check_vma=False)
```

```python
import functools

import jax
import jax.numpy as jnp
from jax import lax
from jax.experimental import pallas as pl
from jax.experimental.pallas import tpu as pltpu
from jax.sharding import PartitionSpec as P

HEADS = 8
HEAD = 128
LOCAL_BITS = 10
TILE = 128
CHUNK = 256
F32 = jnp.float32
BF16 = jnp.bfloat16
MIB = 1 << 20


def bits_of(count):
    return count.bit_length() - 1


def swap(block, axis, stride):
    count = lax.axis_size(axis)
    return lax.ppermute(block, axis, [(place, place ^ stride) for place in range(count)])


def raise_to(block, axis, stride):
    count = lax.axis_size(axis)
    route = [(place, place | stride) for place in range(count) if not place & stride]
    return lax.ppermute(block, axis, route)


def cost(flops, moved):
    return pl.CostEstimate(flops=flops, bytes_accessed=moved, transcendentals=0)


def params(limit):
    return pltpu.CompilerParams(vmem_limit_bytes=limit * MIB)


def outside(*parts):
    return tuple(pltpu.with_memory_space_constraint(part, pltpu.HBM) for part in parts)


def product(left, right):
    return jnp.dot(left, right, preferred_element_type=F32)


def product_nt(left, right):
    return lax.dot_general(left, right, (((1,), (1,)), ((), ())), preferred_element_type=F32)


def identity(size):
    row = lax.broadcasted_iota(jnp.int32, (size, size), 0)
    column = lax.broadcasted_iota(jnp.int32, (size, size), 1)
    return (row == column).astype(F32).astype(BF16)


def turned(block):
    return product_nt(identity(block.shape[1]), block).astype(BF16)


def state_kernel(place, keys, values, state):
    both = product(turned(values[...]), keys[...])
    for low in range(0, keys.shape[1], HEAD):
        part = slice(low, low + HEAD)
        state[part, :] = both[part, part]


def block_state(place, share, keys, values):
    tokens, width = keys.shape
    step = 2 * HEAD
    steps = width // share // step
    column = pl.BlockSpec((tokens, step), lambda pair, place: (0, place[0] * steps + pair))
    return pl.pallas_call(
        state_kernel,
        grid_spec=pltpu.PrefetchScalarGridSpec(
            num_scalar_prefetch=1,
            grid=(steps,),
            in_specs=[column, column],
            out_specs=pl.BlockSpec((step, HEAD), lambda pair, place: (pair, 0)),
        ),
        out_shape=pltpu.VMEM((width // share, HEAD), F32),
        cost_estimate=cost(2 * tokens * width * HEAD // share, 5 * MIB // share),
        compiler_params=params(16),
    )(place.reshape(1).astype(jnp.int32), keys, values)


def tile_mixing(rows):
    target = lax.broadcasted_iota(jnp.int32, (8, TILE), 1)
    source = lax.broadcasted_iota(jnp.int32, (8, TILE), 0)
    rows = [jnp.broadcast_to(row, (8, TILE)) for row in rows]
    within = jnp.bitwise_and(target, 7)
    differ = jnp.bitwise_xor(within, source)
    base = rows[3]
    for level in (2, 1, 0):
        base = jnp.where(differ < 1 << level, rows[level], base)
    parts = [jnp.where(source <= within, base, 0.0)]
    for bit in range(3, bits_of(TILE)):
        upper = jnp.bitwise_and(jnp.right_shift(target, bit), 1) == 1
        parts = [jnp.where(upper, rows[bit + 1], part) for part in parts] + [
            jnp.where(upper, part, 0.0) for part in parts
        ]
    return jnp.concatenate(parts, axis=0)


def local_kernel(half, queries, keys, values, weights, local, *rest):
    *state, rows = rest
    tokens, width = queries.shape
    chunks = tokens // CHUNK
    levels = rows.shape[1]
    top = bits_of(CHUNK)
    spans = [slice(low, low + CHUNK) for low in range(0, tokens, CHUNK)]
    parts = [slice(low, low + HEAD) for low in range(0, width, HEAD)]
    first = (half[0] * pl.num_programs(0) + pl.program_id(0)) * len(parts)
    for at in range(len(parts)):
        rows[at] = weights[:, pl.ds(first + at, 1), :].reshape(levels, tokens)
    flipped = turned(values[...])

    def row(at, level, low, size):
        return rows[at, level : level + 1, low : low + size]

    nodes = []
    for part in parts:
        line = [product(flipped[part, span], keys[span, part]) for span in (spans if state else spans[:-1])]
        if state:
            state[0][part, :] = functools.reduce(jnp.add, line)
        known = [line]
        while len(known[-1]) > 1:
            below = known[-1]
            known.append([below[at] + below[at + 1] for at in range(0, len(below) - 1, 2)])
        nodes.append([[state.astype(BF16) for state in level] for level in known])
    scores = {}
    for at, part in enumerate(parts):
        for chunk, span in enumerate(spans):
            used = [bit for bit in range(bits_of(chunks)) if chunk >> bit & 1]
            left = [keys[span, part]] + [nodes[at][bit][(chunk >> bit) - 1] for bit in used]
            left = jnp.concatenate(left, axis=0) if used else left[0]
            scores[at, chunk] = product_nt(left, queries[span, part])
    for at, part in enumerate(parts):
        for chunk, span in enumerate(spans):
            low = chunk * CHUNK
            score = scores[at, chunk]
            lower, upper = (
                tile_mixing([row(at, level, start, TILE) for level in range(top)]) for start in (low, low + TILE)
            )
            across = row(at, top, low + TILE, TILE)
            weighted = jnp.concatenate(
                [
                    jnp.concatenate([score[:TILE, :TILE] * lower, score[:TILE, TILE:] * across], axis=1),
                    jnp.concatenate([jnp.zeros_like(lower), score[TILE:CHUNK, TILE:] * upper], axis=1),
                ],
                axis=0,
            ).astype(BF16)
            total = product(flipped[part, span], weighted)
            below = CHUNK
            for bit in range(bits_of(chunks)):
                if chunk >> bit & 1:
                    total = total + row(at, top + 1 + bit, low, CHUNK) * score[below : below + HEAD, :]
                    below += HEAD
            local[part, span] = total.astype(BF16)


def local_part(half, with_state, queries, keys, values, level_weights):
    tokens, width = queries.shape
    step = 2 * HEAD
    steps = width // step // 2
    levels = LOCAL_BITS + 1
    column = pl.BlockSpec((tokens, step), lambda pair, half: (0, half[0] * steps + pair))
    return pl.pallas_call(
        local_kernel,
        grid_spec=pltpu.PrefetchScalarGridSpec(
            num_scalar_prefetch=1,
            grid=(steps,),
            in_specs=[column, column, column, pl.BlockSpec((levels,) + level_weights.shape[1:], lambda pair, half: (0, 0, 0))],
            out_specs=[
                pl.BlockSpec((step, tokens), lambda pair, half: (pair, 0)),
                pl.BlockSpec((step, HEAD), lambda pair, half: (pair, 0)),
            ][: 1 + with_state],
            scratch_shapes=[pltpu.VMEM((2, levels, tokens), F32)],
        ),
        out_shape=[pltpu.HBM((width // 2, tokens), BF16), pltpu.VMEM((width // 2, HEAD), F32)][: 1 + with_state],
        cost_estimate=cost(tokens * width, MIB // 4),
        compiler_params=params(16),
    )(half.reshape(1), queries, keys, values, level_weights)


def has_bit(place, bit):
    return jnp.bitwise_and(jnp.right_shift(place, bit), 1) == 1


def near_kernel(aliased, lowest, half, place, queries, weights, local, *rest):
    *held, near, states, rows = rest[aliased:]
    step = pl.program_id(0)
    bits = states.shape[1] // HEAD
    size = states.shape[0] * HEAD // 2

    def quarter_state(bit, quarter, slot):
        if len(held) == 1:
            return held[0][2 * bit + slot]
        if bit == 0:
            return held[0][quarter * size : (quarter + 1) * size, :]
        return jnp.where(slot == 0, held[2 * bit - 1][...], held[2 * bit][...])

    @pl.when(step == 0)
    def _():
        side = jnp.bitwise_and(jnp.right_shift(place[0], 1), 1)
        for quarter in range(2):
            slot = jnp.bitwise_xor(side, quarter)
            for bit in range(bits):
                state = jnp.where(has_bit(place[0], bit), quarter_state(bit, quarter, slot), 0.0).astype(BF16)
                for at in range(0, size, HEAD):
                    states[(quarter * size + at) // HEAD, bit * HEAD : (bit + 1) * HEAD, :] = state[at : at + HEAD]

    for at in range(rows.shape[0]):
        part = slice(at * HEAD, (at + 1) * HEAD)
        head = step * rows.shape[0] + at
        rows[at] = weights[:, pl.ds(half[0] * states.shape[0] + head, 1), :].reshape(rows.shape[1:])
        products = product_nt(states[head], queries[:, part])
        total = local[part, :].astype(F32)
        for bit in range(bits):
            level = LOCAL_BITS + 1 + bit - lowest
            total = total + rows[at, level : level + 1, :] * products[bit * HEAD : (bit + 1) * HEAD]
        near[part, :] = total


def level_block(level_weights, first, count):
    size = 8
    lowest = first // size * size
    if first + count <= lowest + size <= level_weights.shape[0]:
        return lowest, size
    return 0, level_weights.shape[0]


def near_part(half, place, bits, queries, level_weights, local, into, *held):
    tokens, width = queries.shape
    heads = width // HEAD // 2
    step = 2 * HEAD
    steps = width // step // 2
    lowest, levels = level_block(level_weights, LOCAL_BITS + 1, bits)
    into = () if into is None else (pltpu.with_memory_space_constraint(into, pltpu.VMEM),)
    return pl.pallas_call(
        functools.partial(near_kernel, len(into), lowest),
        grid_spec=pltpu.PrefetchScalarGridSpec(
            num_scalar_prefetch=2,
            grid=(steps,),
            in_specs=[
                pl.BlockSpec((tokens, step), lambda pair, half, place: (0, half[0] * steps + pair)),
                pl.BlockSpec((levels,) + level_weights.shape[1:], lambda pair, half, place: (lowest // levels, 0, 0)),
                pl.BlockSpec((step, tokens), lambda pair, half, place: (pair, 0)),
                *[pl.BlockSpec(memory_space=pltpu.VMEM)] * len(into),
                *[
                    pl.BlockSpec(
                        (2 * bits,) + part.shape[1:] if part.ndim == 3 else part.shape,
                        lambda pair, half, place, rank=part.ndim: (0,) * rank,
                    )
                    for part in held
                ],
            ],
            out_specs=pl.BlockSpec((step, tokens), lambda pair, half, place: (half[0] * steps + pair, 0)),
            scratch_shapes=[
                pltpu.VMEM((heads, bits * HEAD, HEAD), BF16),
                pltpu.VMEM((2, levels, tokens), F32),
            ],
        ),
        out_shape=pltpu.VMEM((width, tokens), F32),
        input_output_aliases={5: 0} if into else {},
        cost_estimate=cost(tokens * width, MIB // 4),
        compiler_params=params(16),
    )(half.reshape(1), place, *outside(queries, level_weights, local), *into, *held)


def far_kernel(first_level, place, queries, weights, near, early, early_other, late, late_other, out_weight,
               mixed, states, flipped, attended):
    rows, width = attended.shape
    bits = states.shape[1] // HEAD
    size = late.shape[0]
    skip = early.shape[0] + 1 - 2 * bits
    core = jnp.bitwise_and(place[0], 1)

    @pl.when(pl.program_id(0) == 0)
    def _():
        side = jnp.bitwise_and(jnp.right_shift(place[0], 1), 1)
        for bit in range(bits):
            mine, other = ([part[skip + 2 * bit], part[skip + 2 * bit + 1] if bit + 1 < bits else final[...]]
                           for part, final in ((early, late), (early_other, late_other)))
            for quarter in range(4):
                here, there = (jnp.where(side == quarter % 2, *part) for part in (mine, other))
                state = jnp.where(core == quarter // 2, here, there)
                state = jnp.where(has_bit(place[1], bit), state, 0.0).astype(BF16)
                for at in range(0, size, HEAD):
                    head = (quarter * size + at) // HEAD
                    states[head, bit * HEAD : (bit + 1) * HEAD, :] = state[at : at + HEAD]

    for half in range(2):
        for low in range(0, width // 2, HEAD):
            part = slice(half * (width // 2) + low, half * (width // 2) + low + HEAD)
            head = part.start // HEAD
            products = product_nt(states[head], queries[:, part])
            total = near[part, :]
            for bit in range(bits):
                row = weights[first_level + bit, head : head + 1, :]
                total = total + row * products[bit * HEAD : (bit + 1) * HEAD]
            flipped[part, :] = total.astype(BF16)
    unit = identity(CHUNK)
    for top in range(0, rows, CHUNK):
        for low in range(0, width, CHUNK):
            block = flipped[low : low + CHUNK, top : top + CHUNK]
            attended[top : top + CHUNK, low : low + CHUNK] = product_nt(unit, block).astype(BF16)
    mixed[...] = product(attended[...], out_weight[...]).astype(BF16)


def far_part(first_level, bits, place, queries, level_weights, near, *fixed):
    tokens, width = queries.shape
    lowest, levels = level_block(level_weights, first_level, bits)
    rows = min(2 * CHUNK, tokens)
    band = pl.BlockSpec((rows, width), lambda step: (step, 0))

    def tail(part):
        count = 2 * bits - 1
        if part.ndim == 3 and part.shape[0] % count == 0:
            last = part.shape[0] // count - 1
            return pl.BlockSpec((count,) + part.shape[1:], lambda step: (last, 0, 0))
        return pl.BlockSpec(part.shape, lambda step: (0,) * part.ndim)

    return pl.pallas_call(
        functools.partial(far_kernel, first_level - lowest),
        grid=(tokens // rows,),
        in_specs=[
            pl.BlockSpec(memory_space=pltpu.SMEM),
            band,
            pl.BlockSpec((levels, level_weights.shape[1], rows), lambda step: (lowest // levels, 0, step)),
            pl.BlockSpec((width, rows), lambda step: (0, step)),
            *[tail(part) for part in fixed],
        ],
        out_specs=band,
        out_shape=jax.ShapeDtypeStruct((tokens, width), BF16),
        scratch_shapes=[
            pltpu.VMEM((width // HEAD, bits * HEAD, HEAD), BF16),
            pltpu.VMEM((width, rows), BF16),
            pltpu.VMEM((rows, width), BF16),
        ],
        cost_estimate=cost(2 * tokens * width * (width + bits * HEAD), 12 * MIB),
        compiler_params=params(28),
    )(place, queries, level_weights, near, *fixed)


def body(queries, keys, values, level_weights, out_weight):
    inner, outer = lax.axis_size("inner"), lax.axis_size("outer")
    inner_bits, outer_bits = bits_of(inner), bits_of(outer)
    inner_place, outer_place = lax.axis_index("inner"), lax.axis_index("outer")
    place = jnp.stack([inner_place, outer_place]).astype(jnp.int32)
    core = jnp.bitwise_and(inner_place, 1).astype(jnp.int32)
    side = jnp.bitwise_and(jnp.right_shift(inner_place, 1), 1)
    half = keys.shape[1] // 2
    quarter = half // 2
    tie = lax.optimization_barrier

    inputs = outside(keys, values)
    give = block_state(1 - core, 2, *inputs)
    give, inputs = tie((give, inputs))
    first = swap(give, "inner", 1)

    def quarter_of(at, state):
        return state + lax.dynamic_slice_in_dim(first, at * quarter, quarter, 0)

    keep_theirs = block_state(2 * core + 1 - side, 4, *inputs)
    passed = quarter_of(1 - side, keep_theirs)
    passed, inputs = tie((passed, inputs))
    buckets = [swap(passed, "inner", 2)]
    inputs = outside(queries, keys, values, level_weights)
    local = [None, None]
    local[0], keep = local_part(core, True, *inputs)
    keep_ours = lax.dynamic_slice_in_dim(keep, side * quarter, quarter, 0)
    own = quarter_of(side, keep_ours)
    running = own + buckets[0]
    running, inputs = tie((running, inputs))
    (local[1],) = local_part(1 - core, False, *inputs)
    for bit in range(2, inner_bits):
        arrived = swap(running, "inner", 1 << bit)
        if bit == 2:
            arrived, local = tie((arrived, local))
        buckets.append(arrived)
        running = running + arrived

    running, own, later = tie((running, own, buckets[1:]))
    far = [swap(running, "outer", 1)]
    others = [swap(part, "inner", 2) for part in (own, *later)]
    beside = []

    def own_near():
        held = [part for at, bucket in enumerate(buckets) for part in (bucket, others[at])]
        return near_part(core, place, inner_bits, queries, level_weights, local[0], None, first, *held)

    for bit in range(1, outer_bits):
        running = running + far[-1]
        far.append(swap(running, "outer", 1 << bit))
        beside.append(swap(far[-2], "inner", 2))
        if bit == 1:
            near_mine = own_near()
            far[-1], beside, others, near_mine = tie((far[-1], beside, others, near_mine))
    if outer_bits == 1:
        near_mine = own_near()
        far[-1], others, near_mine = tie((far[-1], others, near_mine))
    late = swap(far[-1], "inner", 2)
    pairs = [(keep_ours, keep_theirs), *((bucket, others[at]) for at, bucket in enumerate(buckets))]
    other = swap(jnp.stack([part for pair in pairs for part in pair]), "inner", 1)
    early = jnp.stack([part for pair in zip(far, beside) for part in pair] + far[-1:])
    early_other = swap(early, "inner", 1)
    near = near_part(1 - core, place, inner_bits, queries, level_weights, local[1], near_mine, other)
    late, near, early_other = tie((late, near, early_other))
    late_other = swap(late, "inner", 1)
    first_level = LOCAL_BITS + 1 + inner_bits
    return far_part(
        first_level, outer_bits, place, queries, level_weights, near, early, early_other, late, late_other, out_weight
    )


def solution(mesh):
    spec = P(("outer", "inner"), None)
    in_specs = (spec, spec, spec, P(None, None, ("outer", "inner")), P())
    return jax.shard_map(body, mesh=mesh, in_specs=in_specs, out_specs=spec, check_vma=False)
```
